128 devices in a mesh: lon: 32 (over y, z, x_lo), lat: 4 (over x_hi, core).
Axes of the slice: x: 4 (x_hi: 2, x_lo: 2; x = x_hi * 2 + x_lo), y: 4, z: 4, core: 2. Of those that a mesh axis runs over, the one named last changes fastest.
Arguments:
- inputs: bfloat16 [1, 8, 48, 384, 192], P(None, None, 'lat', 'lon'), may hold values from -6 to 6
- upstream: bfloat16 [1, 8, 48, 384, 192], P(None, None, 'lat', 'lon'), may hold values from -6 to 6
- land_ids: int32 [48, 384], P('lat', 'lon'), may hold values from 0 to 3
- window_kinds: int32 [32], P('lat'), may hold values from 0 to 31, each once
- class_table: float32 [4, 192], replicated, may hold values from -3 to 3
- norm_gain: float32 [192], replicated, may hold values from 0.5 to 1.5
- norm_bias: float32 [192], replicated, may hold values from -3 to 3
- qkv_weight: bfloat16 [192, 576], replicated, may hold values from -0.4375 to 0.4375
- qkv_bias: float32 [576], replicated, may hold values from -3 to 3
- out_weight: bfloat16 [192, 192], replicated, may hold values from -0.4375 to 0.4375
- bias_table: float32 [32, 6, 3312], replicated, may hold values from -8 to 330
Outputs:
- grad_inputs: bfloat16 [1, 8, 48, 384, 192], P(None, None, 'lat', 'lon')
- grad_class: float32 [4, 192], replicated
- grad_gain: float32 [192], replicated
- grad_norm_bias: float32 [192], replicated
- grad_qkv_weight: float32 [192, 576], replicated
- grad_qkv_bias: float32 [576], replicated
- grad_out_weight: float32 [192, 192], replicated
- grad_out_bias: float32 [192], replicated
- grad_table: float32 [32, 6, 3312], replicated
The draws below stay inside these ranges and needn't reach their ends.
Inputs may be any that keep to these rules, and one draw needn't show every extreme that they name: `window_kinds`: each row of bias_table serves exactly one window position.
All inputs are finite; a program needn't handle non-finite values.
Results may differ from the reference program's by a relative error of at most 0.0095.
Values may be sent and summed in bfloat16 or wider, within the bound.
No kernel may reach another device: no remote copies, remote signals or barrier semaphores. Data moves between devices by JAX's collectives and lax.ppermute only.
A program may use at most 256 MiB of HBM per device.

```python
import math
import jax
import jax.numpy as jnp
from jax import lax

WIDTH = 192
HEADS = 6
HEAD_DIM = 32
LEVELS = 8
WIN_LEVELS = 2
WIN_LAT = 6
WIN_LON = 12
BATCH = 1
CLASSES = 4
LAT = 48
LON = 384
WIN_TOKENS = 144
TYPES = 32
POSITIONS = 3312


def draw_bias_table(key, part):
    key = jax.random.fold_in(key, 11)
    noise_key = jax.random.fold_in(key, 0)
    table = jnp.clip(jax.random.normal(noise_key, (TYPES, HEADS, POSITIONS), jnp.float32), -6.0, 6.0)
    return table


def with_ends(entries, own_key, least, top_value):
    longest = entries.shape.index(max(entries.shape))
    spots = []
    for shift in (0, 1):
        where = [jax.random.randint(jax.random.fold_in(own_key, axis), (), 0, length) for axis, length in enumerate(entries.shape)]
        where[longest] = (where[longest] + shift) % entries.shape[longest]
        spots.append(tuple(where))
    return entries.at[spots[0]].set(least).at[spots[1]].set(top_value)


def shard_levels(own_key, shape, cuts, least, largest):
    gain = 1.0
    for axis_at, blocks in cuts:
        steps = jax.random.uniform(jax.random.fold_in(jax.random.fold_in(own_key, 6), axis_at), (blocks,), jnp.float32, least / len(cuts), largest / len(cuts))
        gain = gain * jnp.repeat(jnp.exp(steps), shape[axis_at] // blocks).reshape((-1,) + (1,) * (len(shape) - 1 - axis_at))
    return gain


def scatter_about(own_key, dims, deviation, reach, cuts=(), held_as=jnp.bfloat16):
    entries = jax.random.normal(own_key, dims, jnp.float32) * deviation
    if len(cuts) > 0:
        entries = shard_levels(own_key, dims, cuts, -0.22, 0.18) * entries
    return jnp.clip(entries, min=-reach, max=reach).astype(held_as)


def setup_inputs(seed: int = 0) -> dict:
    streams_of = jax.random.split(jax.random.key(seed), 12)
    inputs = scatter_about(streams_of[0], (BATCH, LEVELS, LAT, LON, WIDTH), 1.0, 6.0, ((2, 4), (3, 32)))
    upstream = scatter_about(streams_of[1], (BATCH, LEVELS, LAT, LON, WIDTH), 1.0, 6.0, ((2, 4), (3, 32)))
    land_ids = with_ends(jax.random.randint(streams_of[2], (LAT, LON), 0, CLASSES), jax.random.fold_in(streams_of[2], 1), 0, CLASSES - 1).astype(jnp.int32)
    window_kinds = jax.random.permutation(streams_of[3], TYPES).astype(jnp.int32)
    class_table = scatter_about(streams_of[4], (CLASSES, WIDTH), 0.5, 3.0, (), jnp.float32)
    norm_gain = jnp.clip(1.0 + 0.1 * jax.random.normal(streams_of[5], (WIDTH,), jnp.float32), 0.5, 1.5)
    norm_bias = scatter_about(streams_of[6], (WIDTH,), 0.5, 3.0, (), jnp.float32)
    qkv_weight = scatter_about(streams_of[7], (WIDTH, 3 * WIDTH), WIDTH ** -0.5, 0.4375)
    qkv_bias = scatter_about(streams_of[8], (3 * WIDTH,), 0.5, 3.0, (), jnp.float32)
    out_weight = scatter_about(streams_of[9], (WIDTH, WIDTH), WIDTH ** -0.5, 0.4375)
    bias_table = draw_bias_table(jax.random.fold_in(streams_of[11], 71), 0)
    return {"inputs": inputs, "upstream": upstream, "land_ids": land_ids, "window_kinds": window_kinds, "class_table": class_table, "norm_gain": norm_gain, "norm_bias": norm_bias, "qkv_weight": qkv_weight, "qkv_bias": qkv_bias, "out_weight": out_weight, "bias_table": bias_table}


HIGHEST_PRECISION = lax.Precision.HIGHEST
MASKED_SCORE = -1000000000.0
NORM_EPS = 1e-05

def position_table():
    first_col = jnp.arange(WIN_LON)[:, None, None]
    second_col = jnp.arange(WIN_LON)[None, :, None]
    spread = jnp.arange(2 * WIN_LON - 1)[None, None, :]
    return (first_col - second_col + WIN_LON - 1 == spread).astype(jnp.float32)

def expand_bias(table_rows, offsets):
    win_count = table_rows.shape[0]
    shaped = table_rows.reshape(win_count, HEADS, WIN_LEVELS, WIN_LEVELS, WIN_LAT, WIN_LAT, 2 * WIN_LON - 1)
    expanded = jnp.einsum('nhpqabd,ijd->nhpaiqbj', shaped, offsets, precision=HIGHEST_PRECISION)
    return expanded.reshape(win_count, HEADS, WIN_TOKENS, WIN_TOKENS)

def fold_bias(grad_rows, offsets):
    win_count = grad_rows.shape[0]
    shaped = grad_rows.reshape(win_count, HEADS, WIN_LEVELS, WIN_LAT, WIN_LON, WIN_LEVELS, WIN_LAT, WIN_LON)
    folded = jnp.einsum('nhpaiqbj,ijd->nhpqabd', shaped, offsets, precision=HIGHEST_PRECISION)
    return folded.reshape(win_count, HEADS, POSITIONS)

def region_of(places, extent, window_len):
    half_len = window_len // 2
    return jnp.where(places < extent - window_len, 0, jnp.where(places < extent - half_len, 1, 2)).astype(jnp.int32)

def layer_norm(hidden, norm_gain, norm_bias):
    average = lax.optimization_barrier(jnp.mean(hidden, axis=-1, keepdims=True))
    centred = hidden - average
    inv_std = lax.rsqrt(lax.optimization_barrier(jnp.mean(centred * centred, axis=-1, keepdims=True)) + NORM_EPS)
    normal_hat = centred * inv_std
    return (normal_hat, inv_std, (normal_hat * norm_gain + norm_bias).astype(jnp.bfloat16))

def norm_backward(grad_normal, normal_hat, inv_std, norm_gain):
    scaled = grad_normal * norm_gain
    centred = scaled - lax.optimization_barrier(jnp.mean(scaled, axis=-1, keepdims=True))
    return inv_std * (centred - normal_hat * lax.optimization_barrier(jnp.mean(scaled * normal_hat, axis=-1, keepdims=True)))

def split_windows(grid_field):
    leading, batch_size, levels, lat_rows, lon_cols, channels = grid_field.shape
    shaped = grid_field.reshape(leading, batch_size, levels // WIN_LEVELS, WIN_LEVELS, lat_rows // WIN_LAT, WIN_LAT, lon_cols // WIN_LON, WIN_LON, channels)
    shaped = shaped.transpose(0, 1, 2, 4, 6, 3, 5, 7, 8)
    return shaped.reshape(leading, -1, WIN_TOKENS, channels)

def merge_windows(windows, batch_size, levels, lat_rows, lon_cols):
    channels = windows.shape[-1]
    shaped = windows.reshape(batch_size, levels // WIN_LEVELS, lat_rows // WIN_LAT, lon_cols // WIN_LON, WIN_LEVELS, WIN_LAT, WIN_LON, channels)
    shaped = shaped.transpose(0, 1, 4, 2, 5, 3, 6, 7)
    return shaped.reshape(batch_size, levels, lat_rows, lon_cols, channels)

def window_backward(normed, upstream, bias_full, qkv_weight, qkv_bias, out_weight):
    win_count = normed.shape[0]
    score_scale = HEAD_DIM ** (-0.5)
    flat_rows = normed.reshape(win_count * WIN_TOKENS, WIDTH)
    packed = (jnp.dot(flat_rows, qkv_weight, preferred_element_type=jnp.float32) + qkv_bias).astype(jnp.bfloat16)
    packed = packed.reshape(win_count, WIN_TOKENS, 3, HEADS, HEAD_DIM)
    query_heads = packed[:, :, 0].astype(jnp.float32)
    key_heads = packed[:, :, 1].astype(jnp.float32)
    value_heads = packed[:, :, 2].astype(jnp.float32)
    scores = jnp.einsum('ntha,nsha->nhts', query_heads, key_heads) * score_scale + bias_full
    highest = lax.optimization_barrier(jnp.max(scores, axis=-1, keepdims=True))
    powers = jnp.exp(scores - highest)
    attention = powers / lax.optimization_barrier(jnp.sum(powers, axis=-1, keepdims=True))
    attention_low = attention.astype(jnp.bfloat16)
    mixed_heads = jnp.einsum('nhts,nsha->ntha', attention_low.astype(jnp.float32), value_heads).astype(jnp.bfloat16)
    mixed_rows = mixed_heads.reshape(win_count * WIN_TOKENS, WIDTH)
    grad_rows = upstream.reshape(win_count * WIN_TOKENS, WIDTH)
    grad_wout = jnp.dot(mixed_rows.T, grad_rows, preferred_element_type=jnp.float32)
    grad_bout = lax.optimization_barrier(jnp.sum(grad_rows.astype(jnp.float32), axis=0))
    grad_mixed = jnp.dot(grad_rows, out_weight.T, preferred_element_type=jnp.float32).astype(jnp.bfloat16)
    grad_mixed = grad_mixed.reshape(win_count, WIN_TOKENS, HEADS, HEAD_DIM).astype(jnp.float32)
    grad_attention = jnp.einsum('ntha,nsha->nhts', grad_mixed, value_heads)
    grad_values = jnp.einsum('nhts,ntha->nsha', attention_low.astype(jnp.float32), grad_mixed)
    grad_scores = attention * (grad_attention - lax.optimization_barrier(jnp.sum(grad_attention * attention, axis=-1, keepdims=True)))
    grad_scores_low = grad_scores.astype(jnp.bfloat16).astype(jnp.float32)
    grad_query = jnp.einsum('nhts,nsha->ntha', grad_scores_low, key_heads) * score_scale
    grad_keys = jnp.einsum('nhts,ntha->nsha', grad_scores_low, query_heads) * score_scale
    grad_packed = jnp.stack([grad_query, grad_keys, grad_values], axis=2).reshape(win_count * WIN_TOKENS, 3 * WIDTH)
    grad_bqkv = lax.optimization_barrier(jnp.sum(grad_packed, axis=0))
    grad_packed_low = grad_packed.astype(jnp.bfloat16)
    grad_wqkv = jnp.dot(flat_rows.T, grad_packed_low, preferred_element_type=jnp.float32)
    grad_normed = jnp.dot(grad_packed_low, qkv_weight.T, preferred_element_type=jnp.float32)
    return (grad_normed.reshape(win_count, WIN_TOKENS, WIDTH), grad_scores, grad_wqkv, grad_bqkv, grad_wout, grad_bout)

def sample_backward(inputs_one, upstream_one, land_ids, window_kinds, class_table, norm_gain, norm_bias, qkv_weight, qkv_bias, out_weight, bias_table):
    offsets = position_table()
    classes_hot = (land_ids[:, :, None] == jnp.arange(CLASSES)[None, None, :]).astype(jnp.float32)
    embedded = jnp.einsum('yxk,kc->yxc', classes_hot, class_table, precision=HIGHEST_PRECISION)
    hidden = inputs_one.astype(jnp.float32) + embedded[None]
    normal_hat, inv_std, normed = layer_norm(hidden, norm_gain, norm_bias)
    level_shift = WIN_LEVELS // 2
    lat_shift = WIN_LAT // 2
    lon_shift = WIN_LON // 2
    shifted = jnp.roll(jnp.stack([normed, upstream_one]), (-level_shift, -lat_shift, -lon_shift), axis=(1, 2, 3))
    level_windows = LEVELS // WIN_LEVELS
    lat_windows = LAT // WIN_LAT
    lon_windows = LON // WIN_LON
    windows = split_windows(shifted[:, None]).reshape(2, level_windows, lat_windows * lon_windows, WIN_TOKENS, WIDTH)
    level_region = region_of(jnp.arange(LEVELS), LEVELS, WIN_LEVELS).reshape(level_windows, WIN_LEVELS)
    lat_region = region_of(jnp.arange(LAT), LAT, WIN_LAT).reshape(lat_windows, WIN_LAT)
    kinds_grid = window_kinds.reshape(lat_windows, level_windows)
    kinds_range = jnp.arange(TYPES).astype(jnp.int32)
    table_grad = jnp.zeros((TYPES, HEADS, POSITIONS), jnp.float32)
    grad_wqkv = jnp.zeros((WIDTH, 3 * WIDTH), jnp.float32)
    grad_bqkv = jnp.zeros((3 * WIDTH,), jnp.float32)
    grad_wout = jnp.zeros((WIDTH, WIDTH), jnp.float32)
    grad_bout = jnp.zeros((WIDTH,), jnp.float32)
    grad_parts = []
    for level_window in range(level_windows):
        token_region = level_region[level_window][None, :, None, None] * 3 + lat_region[:, None, :, None] + jnp.zeros((1, 1, 1, WIN_LON), jnp.int32)
        token_region = token_region.reshape(lat_windows, WIN_TOKENS)
        same_region = token_region[:, :, None] == token_region[:, None, :]
        kinds_here = kinds_grid[:, level_window].astype(jnp.int32)
        bias_here = jnp.where(same_region[:, None], expand_bias(jnp.take(bias_table, kinds_here, axis=0), offsets), MASKED_SCORE)
        bias_here = jnp.broadcast_to(bias_here[:, None], (lat_windows, lon_windows, HEADS, WIN_TOKENS, WIN_TOKENS)).reshape(-1, HEADS, WIN_TOKENS, WIN_TOKENS)
        outcome = window_backward(windows[0, level_window], windows[1, level_window], bias_here, qkv_weight, qkv_bias, out_weight)
        grad_parts.append(outcome[0])
        score_sum = outcome[1].reshape(lat_windows, lon_windows, HEADS, WIN_TOKENS, WIN_TOKENS).sum(axis=1)
        kinds_hot = (kinds_here[:, None] == kinds_range[None, :]).astype(jnp.float32)
        table_grad = table_grad + jnp.einsum('wt,whp->thp', kinds_hot, fold_bias(score_sum, offsets), precision=HIGHEST_PRECISION)
        grad_wqkv = grad_wqkv + outcome[2]
        grad_bqkv = grad_bqkv + outcome[3]
        grad_wout = grad_wout + outcome[4]
        grad_bout = grad_bout + outcome[5]
    grad_windows = jnp.stack(grad_parts).reshape(-1, WIN_TOKENS, WIDTH)
    grad_shifted = merge_windows(grad_windows, 1, LEVELS, LAT, LON)[0]
    grad_normal = jnp.roll(grad_shifted, (level_shift, lat_shift, lon_shift), axis=(0, 1, 2))
    grad_hidden = upstream_one.astype(jnp.float32) + norm_backward(grad_normal, normal_hat, inv_std, norm_gain)
    grad_gain = lax.optimization_barrier(jnp.sum(grad_normal * normal_hat, axis=(0, 1, 2)))
    grad_shift_sum = lax.optimization_barrier(jnp.sum(grad_normal, axis=(0, 1, 2)))
    grad_class = jnp.einsum('yxk,yxc->kc', classes_hot, lax.optimization_barrier(jnp.sum(grad_hidden, axis=0)), precision=HIGHEST_PRECISION)
    return (grad_hidden.astype(jnp.bfloat16), (grad_class, grad_gain, grad_shift_sum, grad_wqkv, grad_bqkv, grad_wout, grad_bout, table_grad))

def reference(inputs, upstream, land_ids, window_kinds, class_table, norm_gain, norm_bias, qkv_weight, qkv_bias, out_weight, bias_table):

    def one_sample(sample_pair):
        return sample_backward(sample_pair[0], sample_pair[1], land_ids, window_kinds, class_table, norm_gain, norm_bias, qkv_weight, qkv_bias, out_weight, bias_table)
    grad_inputs, stacked_grads = lax.map(one_sample, (inputs, upstream))
    token_root = math.sqrt(BATCH * LEVELS * LAT * LON)
    summed = [lax.optimization_barrier(jnp.sum(stacked_grad, axis=0)) / token_root for stacked_grad in stacked_grads]
    return (grad_inputs, summed[0], summed[1], summed[2], summed[3], summed[4], summed[5], summed[6], summed[7])
```

```python
import math

import jax
import jax.numpy as jnp
import numpy as np
from jax import lax
from jax.experimental import pallas as pl
from jax.experimental.pallas import tpu as pltpu
from jax.sharding import PartitionSpec as P

WIDTH = 192
HEADS = 6
HEAD_DIM = 32
CLASSES = 4
WIN_TOKENS = 144
POSITIONS = 3312
SPREAD = 23
GROUP = 138
PAIRS = 864
MASKED_SCORE = -1000000000.0
NORM_EPS = 1e-05
LOG2E = 1.4426950408889634
SCALE = HEAD_DIM ** (-0.5)
VMEM = 56 * 1024 * 1024
SEND_ROWS = 24
GATHER_ROWS = 56
BOTH = ("lon", "lat")

f32 = jnp.float32
bf16 = jnp.bfloat16


def dot(a, b):
    return lax.dot_general(a, b, (((1,), (0,)), ((), ())), preferred_element_type=f32)


def dot_nt(a, b):
    return lax.dot_general(a, b, (((1,), (1,)), ((), ())), preferred_element_type=f32)


def dot_tn(a, b):
    return lax.dot_general(a, b, (((0,), (0,)), ((), ())), preferred_element_type=f32)


def iota(shape, axis):
    return lax.broadcasted_iota(jnp.int32, shape, axis)


def quotient(a, b):
    return jnp.floor((a.astype(f32) + 0.5) * (1.0 / b)).astype(jnp.int32)


def bias_kernel(scal_ref, tab_ref, out_ref, sel_ref, t_ref, e_ref):
    for w in range(8):
        kind = scal_ref[w]
        for h in range(HEADS):
            sel_ref[h, w : w + 1, :] = tab_ref[h, pl.ds(kind, 1), :]
    last_lat = scal_ref[8]
    for lu in range(2):
        for lt in range(2):
            for a in range(6):
                g = (lt * 2 + lu) * 6 + a
                for h in range(HEADS):
                    row = ((lt * 6 + a) * 6 + h) * 8
                    t_ref[lu, row : row + 8, 0:GROUP] = sel_ref[h, :, g * GROUP : (g + 1) * GROUP]
    row = iota((576, GROUP), 0)
    lane = iota((576, GROUP), 1)
    win = row & 7
    la = quotient(row, 48)
    late = (la >= 6).astype(jnp.int32)
    low_lat = ((la - 6 * late) < 3).astype(jnp.int32)
    low_key = (lane < 3 * SPREAD).astype(jnp.int32)
    cut_lat = jnp.where(win >= 4, last_lat, 0) * (low_lat ^ low_key)
    cut_lev = ((win & 3) == 3).astype(jnp.int32)
    srow = iota((GROUP, 256), 0)
    scol = iota((GROUP, 256), 1)
    col_hi = (scol >= 128).astype(jnp.int32)
    col = scol - 128 * col_hi
    a_u = quotient(col, 12)
    base = a_u * SPREAD - (col - 12 * a_u) + 11
    base = jnp.where(col < 72, base + col_hi, -1000)
    for lu in range(2):
        cut = cut_lat + cut_lev * (late if lu == 0 else 1 - late)
        t = jnp.where(cut > 0, MASKED_SCORE, t_ref[lu, :, 0:GROUP] * LOG2E)
        hi = t.astype(bf16)
        rest = t - hi.astype(f32)
        mid = rest.astype(bf16)
        low = (rest - mid.astype(f32)).astype(bf16)
        for ip in range(6):
            spread = jnp.where(srow == base + 2 * ip, 1.0, 0.0).astype(bf16)
            acc = dot(hi, spread) + dot(mid, spread) + dot(low, spread)
            e_ref[2 * ip] = acc[:, 0:128]
            e_ref[2 * ip + 1] = acc[:, 128:256]
        for w in range(8):
            rows = jnp.concatenate([e_ref[i, pl.ds(w, 72, stride=8), :] for i in range(12)], axis=0)
            out_ref[w, lu * 72 : (lu + 1) * 72, :] = rows.T[0:72, :]


def expand_bias(table, scal):
    return pl.pallas_call(
        bias_kernel,
        out_shape=jax.ShapeDtypeStruct((8, WIN_TOKENS, PAIRS), f32),
        in_specs=[
            pl.BlockSpec(memory_space=pltpu.SMEM),
            pl.BlockSpec(memory_space=pltpu.VMEM),
        ],
        out_specs=pl.BlockSpec(memory_space=pltpu.VMEM),
        scratch_shapes=[
            pltpu.VMEM((HEADS, 8, POSITIONS), f32),
            pltpu.VMEM((2, 576, 256), f32),
            pltpu.VMEM((12, 576, 128), f32),
        ],
        compiler_params=pltpu.CompilerParams(vmem_limit_bytes=VMEM),
        cost_estimate=pl.CostEstimate(flops=2 * 10**9, bytes_accessed=7 * 10**6, transcendentals=0),
        name="bias",
    )(scal, table)


def window_kernel(
    x_ref,
    u_ref,
    e_ref,
    s_ref,
    d_ref,
    ids_ref,
    ct_ref,
    gain_ref,
    nb_ref,
    w_ref,
    bq_ref,
    wo_ref,
    b_ref,
    own_ref,
    eo_ref,
    so_ref,
    do_ref,
    send_ref,
    xs,
    us,
    os,
    idc,
    rep,
    rept,
    mask,
    maskt,
    fold,
    gw,
    gwo,
    sm,
    snd,
):
    w = pl.program_id(0)

    @pl.when(w == 0)
    def _():
        for half in range(2):
            lanes = slice(0, 128) if half == 0 else slice(128, 192)
            far = slice(192, 320) if half == 0 else slice(320, 384)
            width = 128 if half == 0 else 64
            for lat in range(12):
                at = lat * 96
                if lat < 9:
                    src = (lat + 3) * 96 + 48
                    xs[half, at : at + 48, 0:width] = x_ref[src : src + 48, lanes].astype(f32)
                    us[half, at : at + 48, 0:width] = u_ref[src : src + 48, lanes].astype(f32)
                    east, esrc = e_ref, lat * 48
                else:
                    src = (lat - 9) * 48
                    xs[half, at : at + 48, 0:width] = s_ref[src : src + 48, lanes].astype(f32)
                    us[half, at : at + 48, 0:width] = s_ref[src : src + 48, far].astype(f32)
                    east, esrc = d_ref, (lat - 9) * 48
                xs[half, at + 48 : at + 96, 0:width] = east[esrc : esrc + 48, lanes].astype(f32)
                us[half, at + 48 : at + 96, 0:width] = east[esrc : esrc + 48, far].astype(f32)
        id_row = (
            ids_ref[0:1, 0:WIN_TOKENS]
            + e_ref[432:440, 0:WIN_TOKENS].astype(f32)[0:1]
            + s_ref[144:152, 0:WIN_TOKENS].astype(f32)[0:1]
            + d_ref[144:152, 0:WIN_TOKENS].astype(f32)[0:1]
        )
        same = iota((WIN_TOKENS, WIN_TOKENS), 0) == iota((WIN_TOKENS, WIN_TOKENS), 1)
        column = jnp.sum(jnp.where(same, id_row, 0.0), axis=1, keepdims=True)
        idc[...] = jnp.broadcast_to(column, (WIN_TOKENS, WIDTH))
        r = iota((PAIRS, WIN_TOKENS), 0)
        i = quotient(r, 72)
        la = quotient(r - 72 * i, 6)
        rep[...] = jnp.where(la * 12 + i == iota((PAIRS, WIN_TOKENS), 1), 1.0, 0.0).astype(bf16)
        r = iota((WIN_TOKENS, PAIRS), 1)
        i = quotient(r, 72)
        la = quotient(r - 72 * i, 6)
        rept[...] = jnp.where(la * 12 + i == iota((WIN_TOKENS, PAIRS), 0), 1.0, 0.0).astype(bf16)
        r = iota((PAIRS, WIDTH), 0)
        head = r - 6 * quotient(r, 6)
        mask[...] = jnp.where(head == (iota((PAIRS, WIDTH), 1) >> 5), 1.0, 0.0).astype(bf16)
        r = iota((WIDTH, PAIRS), 1)
        head = r - 6 * quotient(r, 6)
        maskt[...] = jnp.where(head == (iota((WIDTH, PAIRS), 0) >> 5), 1.0, 0.0).astype(bf16)
        gw[...] = jnp.zeros_like(gw)
        gwo[...] = jnp.zeros_like(gwo)
        sm[...] = jnp.zeros_like(sm)

    wa = w // 4
    wl = w % 4
    first = wa * 576 + 2 * wl + 1
    second = wa * 576 + lax.rem(2 * wl + 2, 8)

    def window_of(ref):
        parts = []
        for half in range(2):
            rows = jnp.concatenate(
                [ref[half, pl.ds(first, 72, stride=8), :], ref[half, pl.ds(second, 72, stride=8), :]],
                axis=0,
            )
            parts.append(rows)
        return jnp.concatenate(parts, axis=1)[:, 0:WIDTH]

    x = window_of(xs)
    up = window_of(us)
    up_low = up.astype(bf16)
    cell = idc[pl.ds(pl.multiple_of(wa * 72, 8), 72), :]
    cell = jnp.concatenate([cell, cell], axis=0)
    embedded = jnp.where(
        cell < 1.5,
        jnp.where(cell < 0.5, ct_ref[0:1, :], ct_ref[1:2, :]),
        jnp.where(cell < 2.5, ct_ref[2:3, :], ct_ref[3:4, :]),
    )
    hidden = x + embedded
    centred = hidden - jnp.mean(hidden, axis=1, keepdims=True)
    inv_std = lax.rsqrt(jnp.mean(centred * centred, axis=1, keepdims=True) + NORM_EPS)
    normal_hat = centred * inv_std
    normed = (normal_hat * gain_ref[...] + nb_ref[...]).astype(bf16)

    query = (dot(normed, w_ref[0]) + bq_ref[0]).astype(bf16)
    key = (dot(normed, w_ref[1]) + bq_ref[1]).astype(bf16)
    value = (dot(normed, w_ref[2]) + bq_ref[2]).astype(bf16)
    grad_mixed = dot_nt(up_low, wo_ref[...]).astype(bf16)
    query_pairs = dot(rep[...], query).astype(bf16) * mask[...]
    grad_pairs = dot(rep[...], grad_mixed).astype(bf16) * mask[...]

    scores = dot_nt(key, query_pairs) * (SCALE * LOG2E) + b_ref[0]
    powers = jnp.exp2(scores - jnp.max(scores, axis=0, keepdims=True))
    attention = powers * (1.0 / jnp.sum(powers, axis=0, keepdims=True))
    attention_low = attention.astype(bf16)
    mixed_pairs = dot_tn(value, attention_low).astype(bf16) * maskt[...]
    mixed = dot(mixed_pairs, rep[...]).astype(bf16)
    gwo[...] += dot(mixed, up_low)
    grad_attention = dot_nt(value, grad_pairs)
    grad_value = dot(attention_low, grad_pairs)
    row_sum = jnp.sum(grad_attention * attention, axis=0, keepdims=True)
    grad_scores = attention * (grad_attention - row_sum)
    grad_scores_low = grad_scores.astype(bf16)
    grad_key = dot(grad_scores_low, query_pairs) * SCALE
    grad_query_pairs = (dot_tn(key, grad_scores_low) * SCALE).astype(bf16) * maskt[...]
    grad_query = dot_nt(rept[...], grad_query_pairs)
    for lu in range(2):
        turned = grad_scores[lu * 72 : (lu + 1) * 72, :].T
        turned = jnp.concatenate([turned, jnp.zeros((PAIRS, 56), f32)], axis=1)
        for i in range(12):
            fold[lu, i, pl.ds(w, 72, stride=8), :] = turned[i * 72 : (i + 1) * 72, :]

    grad_normed = jnp.zeros((WIN_TOKENS, WIDTH), f32)
    for part, grad in enumerate((grad_query, grad_key, grad_value)):
        sm[6 + part : 7 + part, :] += jnp.sum(grad, axis=0, keepdims=True)
        grad_low = grad.astype(bf16)
        gw[part] += dot_tn(normed, grad_low)
        grad_normed = grad_normed + dot_nt(grad_low, w_ref[part])

    scaled = grad_normed * gain_ref[...]
    scaled_mean = jnp.mean(scaled, axis=1, keepdims=True)
    hat_mean = jnp.mean(scaled * normal_hat, axis=1, keepdims=True)
    grad_hidden = up + inv_std * (scaled - scaled_mean - normal_hat * hat_mean)
    for k in range(CLASSES):
        picked = jnp.where(cell == float(k), grad_hidden, 0.0)
        sm[k : k + 1, :] += jnp.sum(picked, axis=0, keepdims=True)
    sm[4:5, :] += jnp.sum(grad_normed * normal_hat, axis=0, keepdims=True)
    sm[5:6, :] += jnp.sum(grad_normed, axis=0, keepdims=True)
    sm[9:10, :] += jnp.sum(up, axis=0, keepdims=True)
    for half in range(2):
        if half == 0:
            part = grad_hidden[:, 0:128]
        else:
            part = jnp.concatenate([grad_hidden[:, 128:192], jnp.zeros((WIN_TOKENS, 64), f32)], axis=1)
        os[half, pl.ds(first, 72, stride=8), :] = part[0:72]
        os[half, pl.ds(second, 72, stride=8), :] = part[72:144]

    @pl.when(w == 7)
    def _():
        for half in range(2):
            lanes = slice(0, 128) if half == 0 else slice(128, 192)
            width = 128 if half == 0 else 64
            for lat in range(12):
                at = lat * 96
                west, east = (own_ref, eo_ref) if lat < 9 else (so_ref, do_ref)
                to = (lat if lat < 9 else lat - 9) * 48
                west[to : to + 48, lanes] = os[half, at : at + 48, 0:width].astype(bf16)
                east[to : to + 48, lanes] = os[half, at + 48 : at + 96, 0:width].astype(bf16)
        srow = iota((256, 256), 0)
        scol = iota((256, 256), 1)
        row_hi = (srow >= 128).astype(jnp.int32)
        pos = srow - 128 * row_hi
        a_u = quotient(pos, 12)
        target = a_u * SPREAD - (pos - 12 * a_u) + 11 + row_hi
        target = jnp.where(pos < 72, target, -1000)
        tail = scol - 128
        tail = tail - 10 * quotient(tail, 10) + 128
        wanted = jnp.where(scol < 128, scol, jnp.where(scol < 218, tail, -1))
        mains = []
        tails = []
        for lu in range(2):
            acc = jnp.zeros((576, 256), f32)
            for ip in range(6):
                sums = jnp.where(target + 2 * ip == wanted, 1.0, 0.0).astype(bf16)
                both = jnp.concatenate([fold[lu, 2 * ip], fold[lu, 2 * ip + 1]], axis=1).astype(bf16)
                acc = acc + dot(both, sums)
            mains.append(acc[:, 0:128])
            tails.append(acc[:, 128:256])
        main = jnp.concatenate(mains, axis=0)
        tail = jnp.concatenate(tails, axis=0)
        for k in range(9):
            snd[pl.ds(k, 128, stride=SEND_ROWS), :] = main[k * 128 : (k + 1) * 128]
        lane = iota((128, 128), 1)
        slot = quotient(lane, 10)
        plane = jnp.zeros((128, 128), f32)
        for k in range(9):
            plane = jnp.where(slot == k, tail[k * 128 : (k + 1) * 128], plane)
        small = sm[...]
        small = jnp.concatenate(
            [
                jnp.zeros((96, 128), f32),
                small[:, 0:128],
                jnp.concatenate([small[:, 128:192], jnp.zeros((16, 64), f32)], axis=1),
            ],
            axis=0,
        )
        snd[pl.ds(9, 128, stride=SEND_ROWS), :] = jnp.where(lane < 96, plane, small.T)
        weights = jnp.concatenate([gw[0], gw[1], gw[2], gwo[...]], axis=1)
        weights = jnp.concatenate([weights[:, b * 128 : (b + 1) * 128] for b in range(6)], axis=0)
        for k in range(9):
            snd[pl.ds(10 + k, 128, stride=SEND_ROWS), :] = weights[k * 128 : (k + 1) * 128]
        for k in range(19, SEND_ROWS):
            snd[pl.ds(k, 128, stride=SEND_ROWS), :] = jnp.zeros((128, 128), f32)
        send_ref[...] = snd[...].astype(bf16)


def attend(x, u, east, south, diag, ids, ct, gain, nb, w3, bq, wo, bias):
    def whole(shape):
        return pl.BlockSpec(shape, lambda w: (0,) * len(shape))

    ins = [x, u, east, south, diag, ids, ct, gain, nb, w3, bq, wo]
    outs = [(432, WIDTH), (432, WIDTH), (144, WIDTH), (144, WIDTH), (128 * SEND_ROWS, 128)]
    return pl.pallas_call(
        window_kernel,
        grid=(8,),
        out_shape=[jax.ShapeDtypeStruct(o, bf16) for o in outs],
        in_specs=[whole(a.shape) for a in ins]
        + [pl.BlockSpec((1, WIN_TOKENS, PAIRS), lambda w: (w, 0, 0))],
        out_specs=[whole(o) for o in outs],
        scratch_shapes=[
            pltpu.VMEM((2, 1152, 128), f32),
            pltpu.VMEM((2, 1152, 128), f32),
            pltpu.VMEM((2, 1152, 128), f32),
            pltpu.VMEM((WIN_TOKENS, WIDTH), f32),
            pltpu.VMEM((PAIRS, WIN_TOKENS), bf16),
            pltpu.VMEM((WIN_TOKENS, PAIRS), bf16),
            pltpu.VMEM((PAIRS, WIDTH), bf16),
            pltpu.VMEM((WIDTH, PAIRS), bf16),
            pltpu.VMEM((2, 12, 576, 128), f32),
            pltpu.VMEM((3, WIDTH, WIDTH), f32),
            pltpu.VMEM((WIDTH, WIDTH), f32),
            pltpu.VMEM((16, WIDTH), f32),
            pltpu.VMEM((128 * SEND_ROWS, 128), f32),
        ],
        compiler_params=pltpu.CompilerParams(
            vmem_limit_bytes=VMEM, dimension_semantics=("arbitrary",)
        ),
        cost_estimate=pl.CostEstimate(flops=4 * 10**9, bytes_accessed=8 * 10**6, transcendentals=10**6),
        name="windows",
    )(*ins, bias)


def sum_kernel(root, in_ref, kinds_ref, out_ref):
    total = jnp.sum(in_ref[...].astype(f32).reshape(32, 4 * SEND_ROWS, 128), axis=0) * (1.0 / root)
    parts = [total[lat * SEND_ROWS : (lat + 1) * SEND_ROWS] for lat in range(4)]
    weights = (parts[0] + parts[1]) + (parts[2] + parts[3])
    lane = iota((1, 128), 1)
    tails = [jnp.where(lane < 96, p[9:10], weights[9:10]) for p in parts]
    rows = [p[0:9] for p in parts] + [weights[10:19]] + tails
    rows = rows + [kinds_ref[...], jnp.zeros((GATHER_ROWS - 50, 128), f32)]
    out_ref[...] = jnp.concatenate(rows, axis=0).astype(bf16)


def summed(received, kinds, root):
    def body(in_ref, kinds_ref, out_ref):
        sum_kernel(root, in_ref, kinds_ref, out_ref)

    return pl.pallas_call(
        body,
        out_shape=jax.ShapeDtypeStruct((GATHER_ROWS, 128), bf16),
        in_specs=[pl.BlockSpec(memory_space=pltpu.VMEM)] * 2,
        out_specs=pl.BlockSpec(memory_space=pltpu.VMEM),
        compiler_params=pltpu.CompilerParams(vmem_limit_bytes=VMEM),
        name="sums",
    )(received, kinds)


def spread_kernel(kinds_ref, in_ref, tab_ref, wqkv_ref, wo_ref, sm_ref, g, p):
    g[...] = in_ref[...].astype(f32)
    for lat in range(4):
        for w in range(8):
            kind = kinds_ref[lat * 8 + w]
            for q in range(16):
                src = (q * 8 + w) * GATHER_ROWS
                to = pl.multiple_of((q * 32 + kind) * 16, 16)
                p[pl.ds(to, 9), :] = g[src + lat * 9 : src + lat * 9 + 9, :]
                p[pl.ds(to + 9, 1), :] = g[src + 45 + lat : src + 46 + lat, :]
    for m in range(144):
        k, q = m // 16, m % 16
        lu, c = m // 72, m % 72
        la, h = c // 6, c % 6
        at = (((la // 6) * 2 + lu) * 6 + la % 6) * GROUP
        tab_ref[h, :, at : at + 128] = p[pl.ds(q * 512 + k, 32, stride=16), :]
        tail = p[pl.ds(q * 512 + 9, 32, stride=16), :]
        tab_ref[h, :, at + 128 : at + GROUP] = tail[:, k * 10 : k * 10 + 10]
    weights = jnp.concatenate(
        [g[pl.ds(36 + k, 128, stride=GATHER_ROWS), :] for k in range(9)], axis=0
    )
    weights = jnp.concatenate([weights[b * 192 : (b + 1) * 192] for b in range(6)], axis=1)
    wqkv_ref[...] = weights[:, 0:576]
    wo_ref[...] = weights[:, 576:768]
    small = g[pl.ds(45, 128, stride=GATHER_ROWS), :].T
    sm_ref[...] = jnp.concatenate([small[96:112], small[112:128]], axis=1)[:, 0:WIDTH]


def spread(gathered, kinds):
    return pl.pallas_call(
        spread_kernel,
        out_shape=[
            jax.ShapeDtypeStruct((HEADS, 32, POSITIONS), f32),
            jax.ShapeDtypeStruct((WIDTH, 3 * WIDTH), f32),
            jax.ShapeDtypeStruct((WIDTH, WIDTH), f32),
            jax.ShapeDtypeStruct((16, WIDTH), f32),
        ],
        in_specs=[
            pl.BlockSpec(memory_space=pltpu.SMEM),
            pl.BlockSpec(memory_space=pltpu.VMEM),
        ],
        out_specs=[pl.BlockSpec(memory_space=pltpu.VMEM)] * 4,
        scratch_shapes=[
            pltpu.VMEM((128 * GATHER_ROWS, 128), f32),
            pltpu.VMEM((16 * 32 * 16, 128), f32),
        ],
        compiler_params=pltpu.CompilerParams(vmem_limit_bytes=VMEM),
        name="spread",
    )(kinds, gathered)


def moved(array, lon_by, lat_by):
    lon, lat = lax.axis_size("lon"), lax.axis_size("lat")
    pairs = [
        (i * lat + j, ((i + lon_by) % lon) * lat + (j + lat_by) % lat)
        for i in range(lon)
        for j in range(lat)
    ]
    return lax.ppermute(array, BOTH, pairs)


def shards(
    inputs,
    upstream,
    land_ids,
    window_kinds,
    class_table,
    norm_gain,
    norm_bias,
    qkv_weight,
    qkv_bias,
    out_weight,
    bias_table,
):
    x = inputs[0].transpose(1, 2, 0, 3)
    u = upstream[0].transpose(1, 2, 0, 3)
    both = jnp.concatenate([x, u], axis=-1)
    ids = land_ids.astype(bf16)

    def frame_row(piece, before, after):
        row = jnp.pad(piece, (before, after)).reshape(1, WIN_TOKENS)
        return jnp.pad(row, ((0, 7), (0, 2 * WIDTH - WIN_TOKENS)))

    def packet(rows, row):
        return jnp.concatenate([rows.reshape(-1, 2 * WIDTH), row], axis=0)

    east = packet(both[3:12, 0:6], frame_row(ids[3:12, 0:6], (0, 3), (6, 0)))
    south = packet(both[0:3, 6:12], frame_row(ids[0:3, 6:12], (9, 0), (0, 6)))
    diag = packet(both[0:3, 0:6], frame_row(ids[0:3, 0:6], (9, 0), (6, 0)))
    east = moved(east, -1, 0)
    south = moved(south, 0, -1)
    diag = moved(diag, -1, -1)
    own_ids = frame_row(ids[3:12, 6:12], (0, 3), (0, 6)).astype(f32)

    last_lat = (lax.axis_index("lat") == lax.axis_size("lat") - 1).astype(jnp.int32)
    scal = jnp.concatenate([window_kinds, last_lat.reshape(1)])
    bias = expand_bias(bias_table.transpose(1, 0, 2), scal)

    own, east_out, south_out, diag_out, send = attend(
        x.reshape(1152, WIDTH),
        u.reshape(1152, WIDTH),
        east,
        south,
        diag,
        own_ids,
        class_table,
        norm_gain.reshape(1, WIDTH),
        norm_bias.reshape(1, WIDTH),
        qkv_weight.reshape(WIDTH, 3, WIDTH).transpose(1, 0, 2),
        qkv_bias.reshape(3, 1, WIDTH),
        out_weight,
        bias,
    )
    east_back = moved(east_out, 1, 0).reshape(9, 6, 8, WIDTH)
    south_back = moved(south_out, 0, 1).reshape(3, 6, 8, WIDTH)
    diag_back = moved(diag_out, 1, 1).reshape(3, 6, 8, WIDTH)
    own = own.reshape(9, 6, 8, WIDTH)

    root = math.sqrt(inputs.size // WIDTH * lax.axis_size("lon") * lax.axis_size("lat"))
    received = lax.all_to_all(send.reshape(128, SEND_ROWS, 128), BOTH, 0, 0)
    kinds_row = jnp.pad(window_kinds.astype(f32).reshape(1, 8), ((0, 0), (0, 120)))
    part = summed(received.reshape(128 * SEND_ROWS, 128), kinds_row, root)
    gathered = lax.all_to_all(
        jnp.broadcast_to(part, (128, GATHER_ROWS, 128)), BOTH, 0, 0
    )
    kinds = gathered[0:4, 49, 0:8].astype(jnp.int32).reshape(32)
    table, grad_wqkv, grad_wout, small = spread(gathered.reshape(128 * GATHER_ROWS, 128), kinds)

    grad_x = jnp.concatenate(
        [
            jnp.concatenate([diag_back, south_back], axis=1),
            jnp.concatenate([east_back, own], axis=1),
        ],
        axis=0,
    )
    return (
        grad_x.transpose(2, 0, 1, 3)[None],
        small[0:4],
        small[4],
        small[5],
        grad_wqkv,
        small[6:9].reshape(3 * WIDTH),
        grad_wout,
        small[9],
        table.transpose(1, 0, 2),
    )


def solution(mesh):
    placed = (
        P(None, None, "lat", "lon", None),
        P(None, None, "lat", "lon", None),
        P("lat", "lon"),
        P("lat"),
        P(),
        P(),
        P(),
        P(),
        P(),
        P(),
        P(),
    )
    return jax.shard_map(
        shards,
        mesh=mesh,
        in_specs=placed,
        out_specs=(P(None, None, "lat", "lon", None), P(), P(), P(), P(), P(), P(), P(), P()),
        check_vma=False,
    )
```

```python
import math

import jax
import jax.numpy as jnp
import numpy as np
from jax import lax
from jax.experimental import pallas as pl
from jax.experimental.pallas import tpu as pltpu
from jax.sharding import PartitionSpec as P

WIDTH = 192
HEADS = 6
HEAD_DIM = 32
CLASSES = 4
WIN_TOKENS = 144
POSITIONS = 3312
SPREAD = 23
GROUP = 138
PAIRS = 864
MASKED_SCORE = -1000000000.0
NORM_EPS = 1e-05
LOG2E = 1.4426950408889634
SCALE = HEAD_DIM ** (-0.5)
VMEM = 56 * 1024 * 1024
SEND_ROWS = 24
GATHER_ROWS = 48
BOTH = ("lon", "lat")
PER_STEP = 2

f32 = jnp.float32
bf16 = jnp.bfloat16


def dot(a, b):
    return lax.dot_general(a, b, (((1,), (0,)), ((), ())), preferred_element_type=f32)


def dot_nt(a, b):
    return lax.dot_general(a, b, (((1,), (1,)), ((), ())), preferred_element_type=f32)


def dot_tn(a, b):
    return lax.dot_general(a, b, (((0,), (0,)), ((), ())), preferred_element_type=f32)


def iota(shape, axis):
    return lax.broadcasted_iota(jnp.int32, shape, axis)


def quotient(a, b):
    return jnp.floor((a.astype(f32) + 0.5) * (1.0 / b)).astype(jnp.int32)


def bias_kernel(scal_ref, tab_ref, out_ref, sel_ref, t_ref, e_ref):
    for w in range(8):
        kind = scal_ref[w]
        for h in range(HEADS):
            sel_ref[h, w : w + 1, 0:POSITIONS] = tab_ref[h, pl.ds(kind, 1), :]
    last_lat = scal_ref[8]
    for lu in range(2):
        for lt in range(2):
            for a in range(6):
                g = (lt * 2 + lu) * 6 + a
                for h in range(HEADS):
                    at = h * 12 + lt * 6 + a
                    piece = sel_ref[h, :, g * GROUP : g * GROUP + 256]
                    t_ref[lu, 0, pl.ds(at, 8, stride=72), :] = piece[:, 0:128]
                    t_ref[lu, 1, pl.ds(at, 8, stride=72), :] = piece[:, 128:256]
    row = iota((576, GROUP), 0)
    lane = iota((576, GROUP), 1)
    win = quotient(row, 72)
    la = row - 12 * quotient(row, 12)
    late = (la >= 6).astype(jnp.int32)
    low_lat = ((la - 6 * late) < 3).astype(jnp.int32)
    low_key = (lane < 3 * SPREAD).astype(jnp.int32)
    cut_lat = jnp.where(win >= 4, last_lat, 0) * (low_lat ^ low_key)
    cut_lev = ((win & 3) == 3).astype(jnp.int32)
    srow = iota((GROUP, 256), 0)
    scol = iota((GROUP, 256), 1)
    col_hi = (scol >= 128).astype(jnp.int32)
    col = scol - 128 * col_hi
    a_u = quotient(col, 12)
    base = a_u * SPREAD - (col - 12 * a_u) + 11
    base = jnp.where(col < 72, base + col_hi, -1000)
    for lu in range(2):
        cut = cut_lat + cut_lev * (late if lu == 0 else 1 - late)
        t = jnp.concatenate([t_ref[lu, 0], t_ref[lu, 1]], axis=1)[:, 0:GROUP]
        t = jnp.where(cut > 0, MASKED_SCORE, t * LOG2E)
        hi = t.astype(bf16)
        rest = t - hi.astype(f32)
        mid = rest.astype(bf16)
        low = (rest - mid.astype(f32)).astype(bf16)
        for ip in range(6):
            spread = jnp.where(srow == base + 2 * ip, 1.0, 0.0).astype(bf16)
            acc = dot(hi, spread) + dot(mid, spread) + dot(low, spread)
            e_ref[pl.ds(2 * ip, 576, stride=12), :] = acc[:, 0:128]
            e_ref[pl.ds(2 * ip + 1, 576, stride=12), :] = acc[:, 128:256]
        for w in range(8):
            for h in range(HEADS):
                at = (w * HEADS + h) * WIN_TOKENS
                turned = e_ref[at : at + WIN_TOKENS, :].T
                to = h * WIN_TOKENS + lu * 72
                out_ref[w, to : to + 72, :] = turned[0:72, :]


def expand_bias(table, scal):
    return pl.pallas_call(
        bias_kernel,
        out_shape=jax.ShapeDtypeStruct((8, PAIRS, WIN_TOKENS), f32),
        in_specs=[
            pl.BlockSpec(memory_space=pltpu.SMEM),
            pl.BlockSpec(memory_space=pltpu.VMEM),
        ],
        out_specs=pl.BlockSpec(memory_space=pltpu.VMEM),
        scratch_shapes=[
            pltpu.VMEM((HEADS, 8, 3456), f32),
            pltpu.VMEM((2, 2, 576, 128), f32),
            pltpu.VMEM((8 * PAIRS, 128), f32),
        ],
        compiler_params=pltpu.CompilerParams(vmem_limit_bytes=VMEM),
        cost_estimate=pl.CostEstimate(flops=2 * 10**9, bytes_accessed=7 * 10**6, transcendentals=0),
        name="bias",
    )(scal, table)


def window_kernel(
    x_ref,
    u_ref,
    e_ref,
    s_ref,
    d_ref,
    ids_ref,
    ct_ref,
    gain_ref,
    nb_ref,
    w_ref,
    bq_ref,
    wo_ref,
    b_ref,
    own_ref,
    eo_ref,
    so_ref,
    do_ref,
    send_ref,
    xs,
    us,
    os,
    idc,
    w3,
    mask,
    fold,
    gw,
    gwo,
    sm,
    folded,
    snd,
):
    step = pl.program_id(0)

    @pl.when(step == 0)
    def _():
        for half in range(2):
            lanes = slice(0, 128) if half == 0 else slice(128, 192)
            far = slice(192, 320) if half == 0 else slice(320, 384)
            width = 128 if half == 0 else 64
            for lat in range(12):
                at = lat * 96
                if lat < 9:
                    src = (lat + 3) * 96 + 48
                    xs[half, at : at + 48, 0:width] = x_ref[src : src + 48, lanes].astype(f32)
                    us[half, at : at + 48, 0:width] = u_ref[src : src + 48, lanes].astype(f32)
                    east, esrc = e_ref, lat * 48
                else:
                    src = (lat - 9) * 48
                    xs[half, at : at + 48, 0:width] = s_ref[src : src + 48, lanes].astype(f32)
                    us[half, at : at + 48, 0:width] = s_ref[src : src + 48, far].astype(f32)
                    east, esrc = d_ref, (lat - 9) * 48
                xs[half, at + 48 : at + 96, 0:width] = east[esrc : esrc + 48, lanes].astype(f32)
                us[half, at + 48 : at + 96, 0:width] = east[esrc : esrc + 48, far].astype(f32)
        id_row = (
            ids_ref[0:1, 0:WIN_TOKENS]
            + e_ref[432:440, 0:WIN_TOKENS].astype(f32)[0:1]
            + s_ref[144:152, 0:WIN_TOKENS].astype(f32)[0:1]
            + d_ref[144:152, 0:WIN_TOKENS].astype(f32)[0:1]
        )
        same = iota((WIN_TOKENS, WIN_TOKENS), 0) == iota((WIN_TOKENS, WIN_TOKENS), 1)
        column = jnp.sum(jnp.where(same, id_row, 0.0), axis=1, keepdims=True)
        idc[...] = jnp.broadcast_to(column, (WIN_TOKENS, WIDTH))
        head = quotient(iota((PAIRS, WIDTH), 0), WIN_TOKENS)
        mask[...] = jnp.where(head == (iota((PAIRS, WIDTH), 1) >> 5), 1.0, 0.0).astype(bf16)
        for part in range(3):
            w3[part] = w_ref[:, part * WIDTH : (part + 1) * WIDTH]
        gw[...] = jnp.zeros_like(gw)
        gwo[...] = jnp.zeros_like(gwo)
        sm[...] = jnp.zeros_like(sm)

    for sub in range(PER_STEP):
        w = step * PER_STEP + sub
        wa = w // 4
        wl = w % 4
        first = wa * 576 + 2 * wl + 1
        second = wa * 576 + lax.rem(2 * wl + 2, 8)

        def window_of(ref):
            parts = []
            for half in range(2):
                rows = jnp.concatenate(
                    [ref[half, pl.ds(first, 72, stride=8), :], ref[half, pl.ds(second, 72, stride=8), :]],
                    axis=0,
                )
                parts.append(rows)
            return jnp.concatenate(parts, axis=1)[:, 0:WIDTH]

        x = window_of(xs)
        up = window_of(us)
        up_low = up.astype(bf16)
        cell = idc[pl.ds(pl.multiple_of(wa * 72, 8), 72), :]
        cell = jnp.concatenate([cell, cell], axis=0)
        embedded = jnp.where(
            cell < 1.5,
            jnp.where(cell < 0.5, ct_ref[0:1, :], ct_ref[1:2, :]),
            jnp.where(cell < 2.5, ct_ref[2:3, :], ct_ref[3:4, :]),
        )
        hidden = x + embedded
        centred = hidden - jnp.mean(hidden, axis=1, keepdims=True)
        inv_std = lax.rsqrt(jnp.mean(centred * centred, axis=1, keepdims=True) + NORM_EPS)
        normal_hat = centred * inv_std
        normed = (normal_hat * gain_ref[...] + nb_ref[...]).astype(bf16)

        query = (dot(normed, w3[0]) + bq_ref[:, 0:192]).astype(bf16)
        key = dot(normed, w3[1]) + bq_ref[:, 192:384]
        value = dot(normed, w3[2]) + bq_ref[:, 384:576]
        key_turned, value_turned = key.T.astype(bf16), value.T.astype(bf16)
        key_heads = jnp.concatenate([key.astype(bf16)] * HEADS, axis=0) * mask[...]
        value_heads = jnp.concatenate([value.astype(bf16)] * HEADS, axis=0) * mask[...]
        grad_mixed = dot_nt(up_low, wo_ref[...]).astype(bf16)

        def heads_of(a):
            return a.reshape(HEADS, WIN_TOKENS, WIN_TOKENS)

        def by_head(turned, pairs):
            parts = [
                dot(turned[h * 32 : h * 32 + 32], pairs[h * WIN_TOKENS : (h + 1) * WIN_TOKENS])
                for h in range(HEADS)
            ]
            return jnp.concatenate(parts, axis=0)

        def own_head(wide):
            lane = iota((WIN_TOKENS, WIDTH), 1)
            picked = wide[0:WIN_TOKENS]
            for h in range(1, HEADS):
                picked = jnp.where(lane >= 32 * h, wide[h * WIN_TOKENS : (h + 1) * WIN_TOKENS], picked)
            return picked

        scores = heads_of(dot_nt(key_heads, query) * (SCALE * LOG2E) + b_ref[sub])
        powers = jnp.exp2(scores - jnp.max(scores, axis=1, keepdims=True))
        attention = powers * (1.0 / jnp.sum(powers, axis=1, keepdims=True))
        attention_low = attention.astype(bf16).reshape(PAIRS, WIN_TOKENS)
        mixed = by_head(value_turned, attention_low).astype(bf16)
        gwo[...] += dot(mixed, up_low)
        grad_attention = heads_of(dot_nt(value_heads, grad_mixed))
        grad_value = own_head(dot(attention_low, grad_mixed))
        row_sum = jnp.sum(grad_attention * attention, axis=1, keepdims=True)
        grad_scores = attention * (grad_attention - row_sum)
        grad_scores_low = grad_scores.astype(bf16).reshape(PAIRS, WIN_TOKENS)
        grad_key = own_head(dot(grad_scores_low, query)) * SCALE
        grad_query = (by_head(key_turned, grad_scores_low) * SCALE).T
        for h in range(HEADS):
            at = pl.multiple_of((w * HEADS + h) * WIN_TOKENS, WIN_TOKENS)
            for lu in range(2):
                fold[lu, pl.ds(at, WIN_TOKENS), :] = grad_scores[h, lu * 16 : lu * 16 + 128, :].T

        normed_turned = normed.T
        grad_normed = jnp.zeros((WIN_TOKENS, WIDTH), f32)
        for part, grad in enumerate((grad_query, grad_key, grad_value)):
            sm[6 + part : 7 + part, :] += jnp.sum(grad, axis=0, keepdims=True)
            grad_low = grad.astype(bf16)
            gw[part] += dot(normed_turned, grad_low)
            grad_normed = grad_normed + dot_nt(grad_low, w3[part])

        scaled = grad_normed * gain_ref[...]
        scaled_mean = jnp.mean(scaled, axis=1, keepdims=True)
        hat_mean = jnp.mean(scaled * normal_hat, axis=1, keepdims=True)
        grad_hidden = up + inv_std * (scaled - scaled_mean - normal_hat * hat_mean)
        for k in range(CLASSES):
            picked = jnp.where(cell == float(k), grad_hidden, 0.0)
            sm[k : k + 1, :] += jnp.sum(picked, axis=0, keepdims=True)
        sm[4:5, :] += jnp.sum(grad_normed * normal_hat, axis=0, keepdims=True)
        sm[5:6, :] += jnp.sum(grad_normed, axis=0, keepdims=True)
        sm[9:10, :] += jnp.sum(up, axis=0, keepdims=True)
        for half in range(2):
            if half == 0:
                part = grad_hidden[:, 0:128]
            else:
                part = jnp.concatenate([grad_hidden[:, 128:192], jnp.zeros((WIN_TOKENS, 64), f32)], axis=1)
            os[half, pl.ds(first, 72, stride=8), :] = part[0:72]
            os[half, pl.ds(second, 72, stride=8), :] = part[72:144]

    @pl.when(step == 8 // PER_STEP - 1)
    def _():
        for half in range(2):
            lanes = slice(0, 128) if half == 0 else slice(128, 192)
            width = 128 if half == 0 else 64
            for lat in range(12):
                at = lat * 96
                west, east = (own_ref, eo_ref) if lat < 9 else (so_ref, do_ref)
                to = (lat if lat < 9 else lat - 9) * 48
                west[to : to + 48, lanes] = os[half, at : at + 48, 0:width].astype(bf16)
                east[to : to + 48, lanes] = os[half, at + 48 : at + 96, 0:width].astype(bf16)
        srow = iota((256, 256), 0)
        scol = iota((256, 256), 1)
        row_hi = (srow >= 128).astype(jnp.int32)
        pos = srow - 128 * row_hi
        tail = scol - 128
        tail = tail - 10 * quotient(tail, 10) + 128
        wanted = jnp.where(scol < 128, scol, jnp.where(scol < 218, tail, -1))
        for lu in range(2):
            key_at = pos - 56 * lu
            a_u = quotient(key_at, 12)
            target = a_u * SPREAD - (key_at - 12 * a_u) + 11 + row_hi
            target = jnp.where((key_at >= 0) & (key_at < 72), target, -1000)
            acc = jnp.zeros((576, 256), f32)
            for ip in range(6):
                sums = jnp.where(target + 2 * ip == wanted, 1.0, 0.0).astype(bf16)
                both = jnp.concatenate(
                    [fold[lu, pl.ds(2 * ip + i, 576, stride=12), :] for i in range(2)], axis=1
                ).astype(bf16)
                acc = acc + dot(both, sums)
            for at in range(8):
                rows = acc[at * 72 : (at + 1) * 72]
                folded[0, pl.ds(lu * 576 + at, 72, stride=8), :] = rows[:, 0:128]
                folded[1, pl.ds(lu * 576 + at, 72, stride=8), :] = rows[:, 128:256]

        def put(k, plane):
            for core in range(2):
                rows = pl.ds(core * SEND_ROWS + k, 64, stride=2 * SEND_ROWS)
                snd[rows, :] = plane[core * 64 : (core + 1) * 64]

        for k in range(9):
            put(k, folded[0, k * 128 : (k + 1) * 128])
        lane = iota((128, 128), 1)
        slot = quotient(lane, 10)
        plane = jnp.zeros((128, 128), f32)
        for k in range(9):
            plane = jnp.where(slot == k, folded[1, k * 128 : (k + 1) * 128], plane)
        small = sm[...]
        small = jnp.concatenate(
            [
                jnp.zeros((96, 128), f32),
                small[0:10, 0:128],
                jnp.concatenate([small[0:10, 128:192], jnp.zeros((10, 64), f32)], axis=1),
                jnp.zeros((12, 128), f32),
            ],
            axis=0,
        )
        put(9, jnp.where(lane < 96, plane, small.T))
        weights = jnp.concatenate([gw[0], gw[1], gw[2], gwo[...]], axis=1)
        weights = jnp.concatenate([weights[:, b * 128 : (b + 1) * 128] for b in range(6)], axis=0)
        for k in range(9):
            put(10 + k, weights[k * 128 : (k + 1) * 128])
        for k in range(19, SEND_ROWS):
            put(k, jnp.zeros((128, 128), f32))
        send_ref[...] = snd[...].astype(bf16)


def attend(x, u, east, south, diag, ids, ct, gain, nb, w3, bq, wo, bias):
    def whole(shape):
        return pl.BlockSpec(shape, lambda w: (0,) * len(shape))

    ins = [x, u, east, south, diag, ids, ct, gain, nb, w3, bq, wo]
    outs = [(432, WIDTH), (432, WIDTH), (144, WIDTH), (144, WIDTH), (128 * SEND_ROWS, 128)]
    return pl.pallas_call(
        window_kernel,
        grid=(8 // PER_STEP,),
        out_shape=[jax.ShapeDtypeStruct(o, bf16) for o in outs],
        in_specs=[whole(a.shape) for a in ins]
        + [pl.BlockSpec((PER_STEP, PAIRS, WIN_TOKENS), lambda w: (w, 0, 0))],
        out_specs=[whole(o) for o in outs],
        scratch_shapes=[
            pltpu.VMEM((2, 1152, 128), f32),
            pltpu.VMEM((2, 1152, 128), f32),
            pltpu.VMEM((2, 1152, 128), f32),
            pltpu.VMEM((WIN_TOKENS, WIDTH), f32),
            pltpu.VMEM((3, WIDTH, WIDTH), bf16),
            pltpu.VMEM((PAIRS, WIDTH), bf16),
            pltpu.VMEM((2, 8 * PAIRS, 128), f32),
            pltpu.VMEM((3, WIDTH, WIDTH), f32),
            pltpu.VMEM((WIDTH, WIDTH), f32),
            pltpu.VMEM((16, WIDTH), f32),
            pltpu.VMEM((2, 1152, 128), f32),
            pltpu.VMEM((128 * SEND_ROWS, 128), f32),
        ],
        compiler_params=pltpu.CompilerParams(
            vmem_limit_bytes=VMEM, dimension_semantics=("arbitrary",)
        ),
        cost_estimate=pl.CostEstimate(flops=4 * 10**9, bytes_accessed=8 * 10**6, transcendentals=10**6),
        name="windows",
    )(*ins, bias)


def sum_kernel(root, in_ref, out_ref):
    total = jnp.sum(in_ref[...].astype(f32).reshape(32, 4 * SEND_ROWS, 128), axis=0) * (1.0 / root)
    parts = [total[lat * SEND_ROWS : (lat + 1) * SEND_ROWS] for lat in range(4)]
    shared = (parts[0] + parts[1]) + (parts[2] + parts[3])
    tails = [
        jnp.concatenate(
            [
                parts[j][9:10, 0:90],
                parts[3][9:10, 30 * j : 30 * j + 30],
                shared[9:10, 96 + 7 * j : 103 + 7 * j],
                jnp.zeros((1, 1), f32),
            ],
            axis=1,
        )
        for j in range(3)
    ]
    rows = [p[0:9] for p in parts] + [shared[10:19]] + tails
    rows = jnp.concatenate(rows, axis=0).astype(bf16)
    for peer in range(64):
        out_ref[peer * GATHER_ROWS : (peer + 1) * GATHER_ROWS, :] = rows


def summed(received, root):
    def body(in_ref, out_ref):
        sum_kernel(root, in_ref, out_ref)

    return pl.pallas_call(
        body,
        out_shape=jax.ShapeDtypeStruct((64 * GATHER_ROWS, 128), bf16),
        in_specs=[pl.BlockSpec(memory_space=pltpu.VMEM)],
        out_specs=pl.BlockSpec(memory_space=pltpu.VMEM),
        compiler_params=pltpu.CompilerParams(vmem_limit_bytes=VMEM),
        name="sums",
    )(received)


def spread_kernel(
    scal_ref,
    own_ref,
    other_ref,
    tab_ref,
    class_ref,
    gain_ref,
    nb_ref,
    wqkv_ref,
    bqkv_ref,
    wo_ref,
    bo_ref,
    g,
    tails,
    p,
):
    core = scal_ref[32]
    half = 64 * GATHER_ROWS
    g[pl.ds(pl.multiple_of(core * half, half), half), :] = own_ref[...].astype(f32)
    g[pl.ds(pl.multiple_of((1 - core) * half, half), half), :] = other_ref[...].astype(f32)
    extra = [g[pl.ds(45 + j, 128, stride=GATHER_ROWS), :] for j in range(3)]
    for lat in range(3):
        tails[lat] = extra[lat]
    tails[3] = jnp.concatenate([e[:, 90:120] for e in extra] + [jnp.zeros((128, 38), f32)], axis=1)
    for lat in range(4):
        for w in range(8):
            kind = scal_ref[lat * 8 + w]
            for q in range(16):
                e = q * 8 + w
                src = e * GATHER_ROWS + lat * 9
                to = pl.multiple_of((q * 32 + kind) * 16, 16)
                p[pl.ds(to, 9), :] = g[src : src + 9, :]
                p[pl.ds(to + 9, 1), :] = tails[lat, e : e + 1, :]
    for m in range(144):
        k, q = m // 16, m % 16
        lu, c = m // 72, m % 72
        h, la = c // 12, c % 12
        at = (((la // 6) * 2 + lu) * 6 + la % 6) * GROUP
        tab_ref[h, :, at : at + 128] = p[pl.ds(q * 512 + k, 32, stride=16), :]
        tail = p[pl.ds(q * 512 + 9, 32, stride=16), :]
        tab_ref[h, :, at + 128 : at + GROUP] = tail[:, k * 10 : k * 10 + 10]
    weights = jnp.concatenate(
        [g[pl.ds(36 + k, 128, stride=GATHER_ROWS), :] for k in range(9)], axis=0
    )
    weights = jnp.concatenate([weights[b * 192 : (b + 1) * 192] for b in range(6)], axis=1)
    wqkv_ref[...] = weights[:, 0:576]
    wo_ref[...] = weights[:, 576:768]
    small = jnp.concatenate([e[:, 120:127] for e in extra] + [jnp.zeros((128, 107), f32)], axis=1).T
    small = jnp.concatenate([small[0:10], small[10:20]], axis=1)[:, 0:WIDTH]
    class_ref[...] = small[0:4]
    gain_ref[...] = small[4:5]
    nb_ref[...] = small[5:6]
    bqkv_ref[...] = jnp.concatenate([small[6:7], small[7:8], small[8:9]], axis=1)
    bo_ref[...] = small[9:10]


def spread(own, other, scal):
    outs = [
        (HEADS, 32, POSITIONS),
        (CLASSES, WIDTH),
        (1, WIDTH),
        (1, WIDTH),
        (WIDTH, 3 * WIDTH),
        (1, 3 * WIDTH),
        (WIDTH, WIDTH),
        (1, WIDTH),
    ]
    return pl.pallas_call(
        spread_kernel,
        out_shape=[jax.ShapeDtypeStruct(o, f32) for o in outs],
        in_specs=[
            pl.BlockSpec(memory_space=pltpu.SMEM),
            pl.BlockSpec(memory_space=pltpu.VMEM),
            pl.BlockSpec(memory_space=pltpu.VMEM),
        ],
        out_specs=[pl.BlockSpec(memory_space=pltpu.VMEM)] * len(outs),
        scratch_shapes=[
            pltpu.VMEM((128 * GATHER_ROWS, 128), f32),
            pltpu.VMEM((4, 128, 128), f32),
            pltpu.VMEM((16 * 32 * 16, 128), f32),
        ],
        compiler_params=pltpu.CompilerParams(vmem_limit_bytes=VMEM),
        name="spread",
    )(scal, own, other)


def moved(array, lon_by, lat_by):
    lon, lat = lax.axis_size("lon"), lax.axis_size("lat")
    pairs = [
        (i * lat + j, ((i + lon_by) % lon) * lat + (j + lat_by) % lat)
        for i in range(lon)
        for j in range(lat)
    ]
    return lax.ppermute(array, BOTH, pairs)


def shards(
    inputs,
    upstream,
    land_ids,
    window_kinds,
    class_table,
    norm_gain,
    norm_bias,
    qkv_weight,
    qkv_bias,
    out_weight,
    bias_table,
):
    x = inputs[0].transpose(1, 2, 0, 3)
    u = upstream[0].transpose(1, 2, 0, 3)
    both = jnp.concatenate([x, u], axis=-1)
    ids = land_ids.astype(bf16)

    def frame_row(piece, before, after):
        row = jnp.pad(piece, (before, after)).reshape(1, WIN_TOKENS)
        return jnp.pad(row, ((0, 7), (0, 2 * WIDTH - WIN_TOKENS)))

    def packet(rows, row):
        return jnp.concatenate([rows.reshape(-1, 2 * WIDTH), row], axis=0)

    east = packet(both[3:12, 0:6], frame_row(ids[3:12, 0:6], (0, 3), (6, 0)))
    south = packet(both[0:3, 6:12], frame_row(ids[0:3, 6:12], (9, 0), (0, 6)))
    diag = packet(both[0:3, 0:6], frame_row(ids[0:3, 0:6], (9, 0), (6, 0)))
    east = moved(east, -1, 0)
    south = moved(south, 0, -1)
    diag = moved(diag, -1, -1)
    own_ids = frame_row(ids[3:12, 6:12], (0, 3), (0, 6)).astype(f32)

    lats = lax.axis_size("lat")
    mine_at = lax.axis_index("lat")
    kinds = jnp.zeros((lats, 8), jnp.int32)
    for by in range(lats):
        theirs = window_kinds if by == 0 else moved(window_kinds, 0, -by)
        owner = lax.rem(mine_at + by, lats)
        kinds = jnp.where((jnp.arange(lats) == owner)[:, None], theirs[None], kinds)
    kinds = kinds.reshape(32)

    last_lat = (lax.axis_index("lat") == lax.axis_size("lat") - 1).astype(jnp.int32)
    scal = jnp.concatenate([window_kinds, last_lat.reshape(1)])
    bias = expand_bias(bias_table.transpose(1, 0, 2), scal)

    own, east_out, south_out, diag_out, send = attend(
        x.reshape(1152, WIDTH),
        u.reshape(1152, WIDTH),
        east,
        south,
        diag,
        own_ids,
        class_table,
        norm_gain.reshape(1, WIDTH),
        norm_bias.reshape(1, WIDTH),
        qkv_weight,
        qkv_bias.reshape(1, 3 * WIDTH),
        out_weight,
        bias,
    )
    east_back = moved(east_out, 1, 0).reshape(9, 6, 8, WIDTH)
    south_back = moved(south_out, 0, 1).reshape(3, 6, 8, WIDTH)
    diag_back = moved(diag_out, 1, 1).reshape(3, 6, 8, WIDTH)
    own = own.reshape(9, 6, 8, WIDTH)

    root = math.sqrt(inputs.size // WIDTH * lax.axis_size("lon") * lax.axis_size("lat"))
    received = lax.all_to_all(send.reshape(128, SEND_ROWS, 128), BOTH, 0, 0)
    received, east_back, south_back, diag_back = lax.optimization_barrier(
        (received, east_back, south_back, diag_back)
    )
    part = summed(received.reshape(128 * SEND_ROWS, 128), root)
    same_core = [[d for d in range(128) if d % 2 == core] for core in range(2)]
    mine = lax.all_to_all(
        part.reshape(64, GATHER_ROWS, 128), BOTH, 0, 0, axis_index_groups=same_core
    )
    other = lax.ppermute(mine, BOTH, [(d, d ^ 1) for d in range(128)])
    flat = (64 * GATHER_ROWS, 128)
    scal = jnp.concatenate([kinds, (lax.axis_index("lat") % 2).reshape(1)])
    table, grad_class, grad_gain, grad_nb, grad_wqkv, grad_bqkv, grad_wout, grad_bout = spread(
        mine.reshape(flat), other.reshape(flat), scal
    )

    grad_x = jnp.concatenate(
        [
            jnp.concatenate([diag_back, south_back], axis=1),
            jnp.concatenate([east_back, own], axis=1),
        ],
        axis=0,
    )
    return (
        grad_x.transpose(2, 0, 1, 3)[None],
        grad_class,
        grad_gain.reshape(WIDTH),
        grad_nb.reshape(WIDTH),
        grad_wqkv,
        grad_bqkv.reshape(3 * WIDTH),
        grad_wout,
        grad_bout.reshape(WIDTH),
        table.transpose(1, 0, 2),
    )


def solution(mesh):
    placed = (
        P(None, None, "lat", "lon", None),
        P(None, None, "lat", "lon", None),
        P("lat", "lon"),
        P("lat"),
        P(),
        P(),
        P(),
        P(),
        P(),
        P(),
        P(),
    )
    return jax.shard_map(
        shards,
        mesh=mesh,
        in_specs=placed,
        out_specs=(P(None, None, "lat", "lon", None), P(), P(), P(), P(), P(), P(), P(), P()),
        check_vma=False,
    )
```

```python
import math

import jax
import jax.numpy as jnp
import numpy as np
from jax import lax
from jax.experimental import pallas as pl
from jax.experimental.pallas import tpu as pltpu
from jax.sharding import PartitionSpec as P

WIDTH = 192
HEADS = 6
HEAD_DIM = 32
CLASSES = 4
WIN_TOKENS = 144
POSITIONS = 3312
SPREAD = 23
GROUP = 138
PAIRS = 864
MASKED_SCORE = -1000000000.0
NORM_EPS = 1e-05
LOG2E = 1.4426950408889634
SCALE = HEAD_DIM ** (-0.5)
VMEM = 56 * 1024 * 1024
SEND_ROWS = 24
GATHER_ROWS = 48
BOTH = ("lon", "lat")
PER_STEP = 2

f32 = jnp.float32
bf16 = jnp.bfloat16


def dot(a, b):
    return lax.dot_general(a, b, (((1,), (0,)), ((), ())), preferred_element_type=f32)


def dot_nt(a, b):
    return lax.dot_general(a, b, (((1,), (1,)), ((), ())), preferred_element_type=f32)


def dot_tn(a, b):
    return lax.dot_general(a, b, (((0,), (0,)), ((), ())), preferred_element_type=f32)


def iota(shape, axis):
    return lax.broadcasted_iota(jnp.int32, shape, axis)


def quotient(a, b):
    return jnp.floor((a.astype(f32) + 0.5) * (1.0 / b)).astype(jnp.int32)


def bias_kernel(scal_ref, tab_ref, out_ref, sel_ref, t_ref, e_ref, stage, sems):
    for w in range(8):
        kind = scal_ref[w]
        for h in range(HEADS):
            sel_ref[h, w : w + 1, 0:POSITIONS] = tab_ref[h, pl.ds(kind, 1), :]
    last_lat = scal_ref[8]
    for lu in range(2):
        for lt in range(2):
            for a in range(6):
                g = (lt * 2 + lu) * 6 + a
                for h in range(HEADS):
                    at = h * 12 + lt * 6 + a
                    piece = sel_ref[h, :, g * GROUP : g * GROUP + 256]
                    t_ref[lu, 0, pl.ds(at, 8, stride=72), :] = piece[:, 0:128]
                    t_ref[lu, 1, pl.ds(at, 8, stride=72), :] = piece[:, 128:256]
    row = iota((576, GROUP), 0)
    lane = iota((576, GROUP), 1)
    win = quotient(row, 72)
    la = row - 12 * quotient(row, 12)
    late = (la >= 6).astype(jnp.int32)
    low_lat = ((la - 6 * late) < 3).astype(jnp.int32)
    low_key = (lane < 3 * SPREAD).astype(jnp.int32)
    cut_lat = jnp.where(win >= 4, last_lat, 0) * (low_lat ^ low_key)
    cut_lev = ((win & 3) == 3).astype(jnp.int32)
    srow = iota((GROUP, 256), 0)
    scol = iota((GROUP, 256), 1)
    col_hi = (scol >= 128).astype(jnp.int32)
    col = scol - 128 * col_hi
    a_u = quotient(col, 12)
    base = a_u * SPREAD - (col - 12 * a_u) + 11
    base = jnp.where(col < 72, base + col_hi, -1000)
    for lu in range(2):
        cut = cut_lat + cut_lev * (late if lu == 0 else 1 - late)
        t = jnp.concatenate([t_ref[lu, 0], t_ref[lu, 1]], axis=1)[:, 0:GROUP]
        t = jnp.where(cut > 0, MASKED_SCORE, t * LOG2E)
        hi = t.astype(bf16)
        rest = t - hi.astype(f32)
        mid = rest.astype(bf16)
        low = (rest - mid.astype(f32)).astype(bf16)
        for ip in range(6):
            spread = jnp.where(srow == base + 2 * ip, 1.0, 0.0).astype(bf16)
            acc = dot(hi, spread) + dot(mid, spread) + dot(low, spread)
            e_ref[lu, pl.ds(2 * ip, 576, stride=12), :] = acc[:, 0:128]
            e_ref[lu, pl.ds(2 * ip + 1, 576, stride=12), :] = acc[:, 128:256]
    copies = []
    for w in range(8):
        for lu in range(2):
            for h in range(HEADS):
                at = (w * HEADS + h) * WIN_TOKENS
                turned = e_ref[lu, at : at + WIN_TOKENS, :].T
                to = h * WIN_TOKENS + lu * 72
                stage[w, to : to + 72, :] = turned[0:72, :]
        copies.append(pltpu.make_async_copy(stage.at[w], out_ref.at[w], sems.at[w]))
        copies[-1].start()
    for copy in copies:
        copy.wait()


def expand_bias(table, scal):
    return pl.pallas_call(
        bias_kernel,
        out_shape=jax.ShapeDtypeStruct((8, PAIRS, WIN_TOKENS), f32),
        in_specs=[
            pl.BlockSpec(memory_space=pltpu.SMEM),
            pl.BlockSpec(memory_space=pltpu.VMEM),
        ],
        out_specs=pl.BlockSpec(memory_space=pl.ANY),
        scratch_shapes=[
            pltpu.VMEM((HEADS, 8, 3456), f32),
            pltpu.VMEM((2, 2, 576, 128), f32),
            pltpu.VMEM((2, 8 * PAIRS, 128), f32),
            pltpu.VMEM((8, PAIRS, WIN_TOKENS), f32),
            pltpu.SemaphoreType.DMA((8,)),
        ],
        compiler_params=pltpu.CompilerParams(vmem_limit_bytes=VMEM),
        cost_estimate=pl.CostEstimate(flops=2 * 10**9, bytes_accessed=7 * 10**6, transcendentals=0),
        name="bias",
    )(scal, table)


def window_kernel(
    x_ref,
    u_ref,
    e_ref,
    s_ref,
    d_ref,
    ids_ref,
    ct_ref,
    gain_ref,
    nb_ref,
    w_ref,
    bq_ref,
    wo_ref,
    b_ref,
    own_ref,
    eo_ref,
    so_ref,
    do_ref,
    send_ref,
    xs,
    us,
    os,
    idc,
    w3,
    mask,
    fold,
    gw,
    gwo,
    sm,
    folded,
    snd,
):
    step = pl.program_id(0)

    @pl.when(step == 0)
    def _():
        for half in range(2):
            lanes = slice(0, 128) if half == 0 else slice(128, 192)
            far = slice(192, 320) if half == 0 else slice(320, 384)
            width = 128 if half == 0 else 64
            for lat in range(12):
                at = lat * 96
                if lat < 9:
                    src = (lat + 3) * 96 + 48
                    xs[half, at : at + 48, 0:width] = x_ref[src : src + 48, lanes].astype(f32)
                    us[half, at : at + 48, 0:width] = u_ref[src : src + 48, lanes].astype(f32)
                    east, esrc = e_ref, lat * 48
                else:
                    src = (lat - 9) * 48
                    xs[half, at : at + 48, 0:width] = s_ref[src : src + 48, lanes].astype(f32)
                    us[half, at : at + 48, 0:width] = s_ref[src : src + 48, far].astype(f32)
                    east, esrc = d_ref, (lat - 9) * 48
                xs[half, at + 48 : at + 96, 0:width] = east[esrc : esrc + 48, lanes].astype(f32)
                us[half, at + 48 : at + 96, 0:width] = east[esrc : esrc + 48, far].astype(f32)
        id_row = (
            ids_ref[0:1, 0:WIN_TOKENS]
            + e_ref[432:440, 0:WIN_TOKENS].astype(f32)[0:1]
            + s_ref[144:152, 0:WIN_TOKENS].astype(f32)[0:1]
            + d_ref[144:152, 0:WIN_TOKENS].astype(f32)[0:1]
        )
        same = iota((WIN_TOKENS, WIN_TOKENS), 0) == iota((WIN_TOKENS, WIN_TOKENS), 1)
        column = jnp.sum(jnp.where(same, id_row, 0.0), axis=1, keepdims=True)
        idc[...] = jnp.broadcast_to(column, (WIN_TOKENS, WIDTH))
        head = quotient(iota((PAIRS, WIDTH), 0), WIN_TOKENS)
        mask[...] = jnp.where(head == (iota((PAIRS, WIDTH), 1) >> 5), 1.0, 0.0).astype(bf16)
        for part in range(3):
            w3[part] = w_ref[:, part * WIDTH : (part + 1) * WIDTH]
        gw[...] = jnp.zeros_like(gw)
        gwo[...] = jnp.zeros_like(gwo)
        sm[...] = jnp.zeros_like(sm)

    for sub in range(PER_STEP):
        w = step * PER_STEP + sub
        wa = w // 4
        wl = w % 4
        first = wa * 576 + 2 * wl + 1
        second = wa * 576 + lax.rem(2 * wl + 2, 8)

        def window_of(ref):
            parts = []
            for half in range(2):
                rows = jnp.concatenate(
                    [ref[half, pl.ds(first, 72, stride=8), :], ref[half, pl.ds(second, 72, stride=8), :]],
                    axis=0,
                )
                parts.append(rows)
            return jnp.concatenate(parts, axis=1)[:, 0:WIDTH]

        x = window_of(xs)
        up = window_of(us)
        up_low = up.astype(bf16)
        cell = idc[pl.ds(pl.multiple_of(wa * 72, 8), 72), :]
        cell = jnp.concatenate([cell, cell], axis=0)
        embedded = jnp.where(
            cell < 1.5,
            jnp.where(cell < 0.5, ct_ref[0:1, :], ct_ref[1:2, :]),
            jnp.where(cell < 2.5, ct_ref[2:3, :], ct_ref[3:4, :]),
        )
        hidden = x + embedded
        centred = hidden - jnp.mean(hidden, axis=1, keepdims=True)
        inv_std = lax.rsqrt(jnp.mean(centred * centred, axis=1, keepdims=True) + NORM_EPS)
        normal_hat = centred * inv_std
        normed = (normal_hat * gain_ref[...] + nb_ref[...]).astype(bf16)

        bq = bq_ref[...].reshape(1, 3 * WIDTH)
        query = (dot(normed, w3[0]) + bq[:, 0:192]).astype(bf16)
        key = dot(normed, w3[1]) + bq[:, 192:384]
        value = dot(normed, w3[2]) + bq[:, 384:576]
        key_turned, value_turned = key.T.astype(bf16), value.T.astype(bf16)
        key_heads = jnp.concatenate([key.astype(bf16)] * HEADS, axis=0) * mask[...]
        value_heads = jnp.concatenate([value.astype(bf16)] * HEADS, axis=0) * mask[...]
        grad_mixed = dot_nt(up_low, wo_ref[...]).astype(bf16)

        def heads_of(a):
            return a.reshape(HEADS, WIN_TOKENS, WIN_TOKENS)

        def by_head(turned, pairs):
            parts = [
                dot(turned[h * 32 : h * 32 + 32], pairs[h * WIN_TOKENS : (h + 1) * WIN_TOKENS])
                for h in range(HEADS)
            ]
            return jnp.concatenate(parts, axis=0)

        def own_head(wide):
            lane = iota((WIN_TOKENS, WIDTH), 1)
            picked = wide[0:WIN_TOKENS]
            for h in range(1, HEADS):
                picked = jnp.where(lane >= 32 * h, wide[h * WIN_TOKENS : (h + 1) * WIN_TOKENS], picked)
            return picked

        scores = heads_of(dot_nt(key_heads, query) * (SCALE * LOG2E) + b_ref[sub])
        powers = jnp.exp2(scores - jnp.max(scores, axis=1, keepdims=True))
        attention = powers * (1.0 / jnp.sum(powers, axis=1, keepdims=True))
        attention_low = attention.astype(bf16).reshape(PAIRS, WIN_TOKENS)
        mixed = by_head(value_turned, attention_low).astype(bf16)
        gwo[...] += dot(mixed, up_low)
        grad_attention = heads_of(dot_nt(value_heads, grad_mixed))
        grad_value = own_head(dot(attention_low, grad_mixed))
        row_sum = jnp.sum(grad_attention * attention, axis=1, keepdims=True)
        grad_scores = attention * (grad_attention - row_sum)
        grad_scores_low = grad_scores.astype(bf16).reshape(PAIRS, WIN_TOKENS)
        grad_key = own_head(dot(grad_scores_low, query)) * SCALE
        grad_query = (by_head(key_turned, grad_scores_low) * SCALE).T
        for h in range(HEADS):
            at = pl.multiple_of((w * HEADS + h) * WIN_TOKENS, WIN_TOKENS)
            for lu in range(2):
                fold[lu, pl.ds(at, WIN_TOKENS), :] = grad_scores[h, lu * 16 : lu * 16 + 128, :].T

        normed_turned = normed.T
        grad_normed = jnp.zeros((WIN_TOKENS, WIDTH), f32)
        for part, grad in enumerate((grad_query, grad_key, grad_value)):
            sm[6 + part : 7 + part, :] += jnp.sum(grad, axis=0, keepdims=True)
            grad_low = grad.astype(bf16)
            gw[part] += dot(normed_turned, grad_low)
            grad_normed = grad_normed + dot_nt(grad_low, w3[part])

        scaled = grad_normed * gain_ref[...]
        scaled_mean = jnp.mean(scaled, axis=1, keepdims=True)
        hat_mean = jnp.mean(scaled * normal_hat, axis=1, keepdims=True)
        grad_hidden = up + inv_std * (scaled - scaled_mean - normal_hat * hat_mean)
        for k in range(CLASSES):
            picked = jnp.where(cell == float(k), grad_hidden, 0.0)
            sm[k : k + 1, :] += jnp.sum(picked, axis=0, keepdims=True)
        sm[4:5, :] += jnp.sum(grad_normed * normal_hat, axis=0, keepdims=True)
        sm[5:6, :] += jnp.sum(grad_normed, axis=0, keepdims=True)
        sm[9:10, :] += jnp.sum(up, axis=0, keepdims=True)
        for half in range(2):
            if half == 0:
                part = grad_hidden[:, 0:128]
            else:
                part = jnp.concatenate([grad_hidden[:, 128:192], jnp.zeros((WIN_TOKENS, 64), f32)], axis=1)
            os[half, pl.ds(first, 72, stride=8), :] = part[0:72]
            os[half, pl.ds(second, 72, stride=8), :] = part[72:144]

    @pl.when(step == 8 // PER_STEP - 1)
    def _():
        for half in range(2):
            lanes = slice(0, 128) if half == 0 else slice(128, 192)
            width = 128 if half == 0 else 64
            for lat in range(12):
                at = lat * 96
                west, east = (own_ref, eo_ref) if lat < 9 else (so_ref, do_ref)
                to = (lat if lat < 9 else lat - 9) * 48
                west[to : to + 48, lanes] = os[half, at : at + 48, 0:width].astype(bf16)
                east[to : to + 48, lanes] = os[half, at + 48 : at + 96, 0:width].astype(bf16)
        srow = iota((256, 256), 0)
        scol = iota((256, 256), 1)
        row_hi = (srow >= 128).astype(jnp.int32)
        pos = srow - 128 * row_hi
        tail = scol - 128
        tail = tail - 10 * quotient(tail, 10) + 128
        wanted = jnp.where(scol < 128, scol, jnp.where(scol < 218, tail, -1))
        for lu in range(2):
            key_at = pos - 56 * lu
            a_u = quotient(key_at, 12)
            target = a_u * SPREAD - (key_at - 12 * a_u) + 11 + row_hi
            target = jnp.where((key_at >= 0) & (key_at < 72), target, -1000)
            acc = jnp.zeros((576, 256), f32)
            for ip in range(6):
                sums = jnp.where(target + 2 * ip == wanted, 1.0, 0.0).astype(bf16)
                both = jnp.concatenate(
                    [fold[lu, pl.ds(2 * ip + i, 576, stride=12), :] for i in range(2)], axis=1
                ).astype(bf16)
                acc = acc + dot(both, sums)
            for at in range(8):
                rows = acc[at * 72 : (at + 1) * 72]
                folded[0, pl.ds(lu * 576 + at, 72, stride=8), :] = rows[:, 0:128]
                folded[1, pl.ds(lu * 576 + at, 72, stride=8), :] = rows[:, 128:256]

        def put(k, plane):
            for core in range(2):
                rows = pl.ds(core * SEND_ROWS + k, 64, stride=2 * SEND_ROWS)
                snd[rows, :] = plane[core * 64 : (core + 1) * 64]

        for k in range(9):
            put(k, folded[0, k * 128 : (k + 1) * 128])
        lane = iota((128, 128), 1)
        slot = quotient(lane, 10)
        plane = jnp.zeros((128, 128), f32)
        for k in range(9):
            plane = jnp.where(slot == k, folded[1, k * 128 : (k + 1) * 128], plane)
        small = sm[...]
        small = jnp.concatenate(
            [
                jnp.zeros((96, 128), f32),
                small[0:10, 0:128],
                jnp.concatenate([small[0:10, 128:192], jnp.zeros((10, 64), f32)], axis=1),
                jnp.zeros((12, 128), f32),
            ],
            axis=0,
        )
        put(9, jnp.where(lane < 96, plane, small.T))
        weights = jnp.concatenate([gw[0], gw[1], gw[2], gwo[...]], axis=1)
        weights = jnp.concatenate([weights[:, b * 128 : (b + 1) * 128] for b in range(6)], axis=0)
        for k in range(9):
            put(10 + k, weights[k * 128 : (k + 1) * 128])
        for k in range(19, SEND_ROWS):
            put(k, jnp.zeros((128, 128), f32))
        send_ref[...] = snd[...].astype(bf16)


def attend(x, u, east, south, diag, ids, ct, gain, nb, w3, bq, wo, bias):
    def whole(shape):
        return pl.BlockSpec(shape, lambda w: (0,) * len(shape))

    ins = [x, u, east, south, diag, ids, ct, gain, nb, w3, bq, wo]
    outs = [(432, WIDTH), (432, WIDTH), (144, WIDTH), (144, WIDTH), (128 * SEND_ROWS, 128)]
    return pl.pallas_call(
        window_kernel,
        grid=(8 // PER_STEP,),
        out_shape=[jax.ShapeDtypeStruct(o, bf16) for o in outs],
        in_specs=[whole(a.shape) for a in ins]
        + [pl.BlockSpec((PER_STEP, PAIRS, WIN_TOKENS), lambda w: (w, 0, 0))],
        out_specs=[whole(o) for o in outs],
        scratch_shapes=[
            pltpu.VMEM((2, 1152, 128), f32),
            pltpu.VMEM((2, 1152, 128), f32),
            pltpu.VMEM((2, 1152, 128), f32),
            pltpu.VMEM((WIN_TOKENS, WIDTH), f32),
            pltpu.VMEM((3, WIDTH, WIDTH), bf16),
            pltpu.VMEM((PAIRS, WIDTH), bf16),
            pltpu.VMEM((2, 8 * PAIRS, 128), f32),
            pltpu.VMEM((3, WIDTH, WIDTH), f32),
            pltpu.VMEM((WIDTH, WIDTH), f32),
            pltpu.VMEM((16, WIDTH), f32),
            pltpu.VMEM((2, 1152, 128), f32),
            pltpu.VMEM((128 * SEND_ROWS, 128), f32),
        ],
        compiler_params=pltpu.CompilerParams(
            vmem_limit_bytes=VMEM, dimension_semantics=("arbitrary",)
        ),
        cost_estimate=pl.CostEstimate(flops=4 * 10**9, bytes_accessed=8 * 10**6, transcendentals=10**6),
        name="windows",
    )(*ins, bias)


def sum_kernel(root, in_ref, out_ref):
    total = jnp.sum(in_ref[...].astype(f32).reshape(32, 4 * SEND_ROWS, 128), axis=0) * (1.0 / root)
    parts = [total[lat * SEND_ROWS : (lat + 1) * SEND_ROWS] for lat in range(4)]
    shared = (parts[0] + parts[1]) + (parts[2] + parts[3])
    tails = [
        jnp.concatenate(
            [
                parts[j][9:10, 0:90],
                parts[3][9:10, 30 * j : 30 * j + 30],
                shared[9:10, 96 + 7 * j : 103 + 7 * j],
                jnp.zeros((1, 1), f32),
            ],
            axis=1,
        )
        for j in range(3)
    ]
    rows = [p[0:9] for p in parts] + [shared[10:19]] + tails
    rows = jnp.concatenate(rows, axis=0).astype(bf16)
    for peer in range(64):
        out_ref[peer * GATHER_ROWS : (peer + 1) * GATHER_ROWS, :] = rows


def summed(received, root):
    def body(in_ref, out_ref):
        sum_kernel(root, in_ref, out_ref)

    return pl.pallas_call(
        body,
        out_shape=jax.ShapeDtypeStruct((64 * GATHER_ROWS, 128), bf16),
        in_specs=[pl.BlockSpec(memory_space=pltpu.VMEM)],
        out_specs=pl.BlockSpec(memory_space=pltpu.VMEM),
        compiler_params=pltpu.CompilerParams(vmem_limit_bytes=VMEM),
        name="sums",
    )(received)


def spread_kernel(
    scal_ref,
    own_ref,
    other_ref,
    tab_ref,
    class_ref,
    gain_ref,
    nb_ref,
    wqkv_ref,
    bqkv_ref,
    wo_ref,
    bo_ref,
    g,
    tails,
    p,
):
    core = scal_ref[32]
    half = 64 * GATHER_ROWS
    g[pl.ds(pl.multiple_of(core * half, half), half), :] = own_ref[...].astype(f32)
    g[pl.ds(pl.multiple_of((1 - core) * half, half), half), :] = other_ref[...].astype(f32)
    extra = [g[pl.ds(45 + j, 128, stride=GATHER_ROWS), :] for j in range(3)]
    for lat in range(3):
        tails[lat] = extra[lat]
    tails[3] = jnp.concatenate([e[:, 90:120] for e in extra] + [jnp.zeros((128, 38), f32)], axis=1)
    for lat in range(4):
        for w in range(8):
            kind = scal_ref[lat * 8 + w]
            for q in range(16):
                e = q * 8 + w
                src = e * GATHER_ROWS + lat * 9
                to = pl.multiple_of((q * 32 + kind) * 16, 16)
                p[pl.ds(to, 9), :] = g[src : src + 9, :]
                p[pl.ds(to + 9, 1), :] = tails[lat, e : e + 1, :]
    for m in range(144):
        k, q = m // 16, m % 16
        lu, c = m // 72, m % 72
        h, la = c // 12, c % 12
        at = (((la // 6) * 2 + lu) * 6 + la % 6) * GROUP
        tab_ref[h, :, at : at + 128] = p[pl.ds(q * 512 + k, 32, stride=16), :]
        tail = p[pl.ds(q * 512 + 9, 32, stride=16), :]
        tab_ref[h, :, at + 128 : at + GROUP] = tail[:, k * 10 : k * 10 + 10]
    weights = jnp.concatenate(
        [g[pl.ds(36 + k, 128, stride=GATHER_ROWS), :] for k in range(9)], axis=0
    )
    weights = jnp.concatenate([weights[b * 192 : (b + 1) * 192] for b in range(6)], axis=1)
    wqkv_ref[...] = weights[:, 0:576]
    wo_ref[...] = weights[:, 576:768]
    small = jnp.concatenate([e[:, 120:127] for e in extra] + [jnp.zeros((128, 107), f32)], axis=1).T
    small = jnp.concatenate([small[0:10], small[10:20]], axis=1)[:, 0:WIDTH]
    class_ref[...] = small[0:4]
    gain_ref[...] = small[4:5].reshape(WIDTH)
    nb_ref[...] = small[5:6].reshape(WIDTH)
    grad_bqkv = jnp.concatenate([small[6:7], small[7:8], small[8:9]], axis=1)
    bqkv_ref[...] = grad_bqkv.reshape(3 * WIDTH)
    bo_ref[...] = small[9:10].reshape(WIDTH)


def spread(own, other, scal):
    outs = [
        (HEADS, 32, POSITIONS),
        (CLASSES, WIDTH),
        (WIDTH,),
        (WIDTH,),
        (WIDTH, 3 * WIDTH),
        (3 * WIDTH,),
        (WIDTH, WIDTH),
        (WIDTH,),
    ]
    return pl.pallas_call(
        spread_kernel,
        out_shape=[jax.ShapeDtypeStruct(o, f32) for o in outs],
        in_specs=[
            pl.BlockSpec(memory_space=pltpu.SMEM),
            pl.BlockSpec(memory_space=pltpu.VMEM),
            pl.BlockSpec(memory_space=pltpu.VMEM),
        ],
        out_specs=[pl.BlockSpec(memory_space=pltpu.VMEM)] * len(outs),
        scratch_shapes=[
            pltpu.VMEM((128 * GATHER_ROWS, 128), f32),
            pltpu.VMEM((4, 128, 128), f32),
            pltpu.VMEM((16 * 32 * 16, 128), f32),
        ],
        compiler_params=pltpu.CompilerParams(vmem_limit_bytes=VMEM),
        name="spread",
    )(scal, own, other)


def pack_kernel(x_ref, u_ref, ids_ref, east_ref, south_ref, diag_ref, ids_out):
    lane = iota((1, WIN_TOKENS), 1)
    lat = quotient(lane, 12)
    lon = lane - 12 * lat
    ids = ids_ref[...].astype(f32)
    row = jnp.concatenate([ids[a : a + 1, :] for a in range(12)], axis=1)

    def moved_row(keep, by):
        kept = jnp.where(keep, row, 0.0)
        if by < 0:
            kept = jnp.concatenate([kept[:, -by:], jnp.zeros((1, 2 * WIDTH - WIN_TOKENS - by), f32)], axis=1)
        else:
            tail = jnp.zeros((1, 2 * WIDTH - WIN_TOKENS), f32)
            kept = jnp.concatenate([jnp.zeros((1, by), f32), kept[:, : WIN_TOKENS - by], tail], axis=1)
        return jnp.concatenate([kept, jnp.zeros((7, 2 * WIDTH), f32)], axis=0)

    def fill(out, lats, lon_at, id_rows):
        rows = []
        for a in lats:
            at = a * 96 + lon_at * 8
            rows.append(
                jnp.concatenate(
                    [x_ref[at : at + 48, :].astype(f32), u_ref[at : at + 48, :].astype(f32)], axis=1
                )
            )
        out[...] = jnp.concatenate(rows + [id_rows], axis=0).astype(bf16)

    fill(east_ref, range(3, 12), 0, moved_row((lat >= 3) & (lon < 6), -30))
    fill(south_ref, range(0, 3), 6, moved_row((lat < 3) & (lon >= 6), 102))
    fill(diag_ref, range(0, 3), 0, moved_row((lat < 3) & (lon < 6), 114))
    ids_out[...] = moved_row((lat >= 3) & (lon >= 6), -42)


def pack(x, u, ids):
    shapes = [((440, 2 * WIDTH), bf16), ((152, 2 * WIDTH), bf16), ((152, 2 * WIDTH), bf16)]
    shapes.append(((8, 2 * WIDTH), f32))
    return pl.pallas_call(
        pack_kernel,
        out_shape=[jax.ShapeDtypeStruct(*o) for o in shapes],
        in_specs=[pl.BlockSpec(memory_space=pltpu.VMEM)] * 3,
        out_specs=[pl.BlockSpec(memory_space=pltpu.VMEM)] * 4,
        compiler_params=pltpu.CompilerParams(vmem_limit_bytes=VMEM // 4),
        name="pack",
    )(x, u, ids)


def moved(array, lon_by, lat_by):
    lon, lat = lax.axis_size("lon"), lax.axis_size("lat")
    pairs = [
        (i * lat + j, ((i + lon_by) % lon) * lat + (j + lat_by) % lat)
        for i in range(lon)
        for j in range(lat)
    ]
    return lax.ppermute(array, BOTH, pairs)


def shards(
    inputs,
    upstream,
    land_ids,
    window_kinds,
    class_table,
    norm_gain,
    norm_bias,
    qkv_weight,
    qkv_bias,
    out_weight,
    bias_table,
):
    x = inputs[0].transpose(1, 2, 0, 3)
    u = upstream[0].transpose(1, 2, 0, 3)
    x = x.reshape(1152, WIDTH)
    u = u.reshape(1152, WIDTH)
    east, south, diag, own_ids = pack(x, u, land_ids)
    east = moved(east, -1, 0)
    south = moved(south, 0, -1)
    diag = moved(diag, -1, -1)

    lats = lax.axis_size("lat")
    mine_at = lax.axis_index("lat")
    kinds = jnp.zeros((lats, 8), jnp.int32)
    for by in range(lats):
        theirs = window_kinds if by == 0 else moved(window_kinds, 0, -by)
        owner = lax.rem(mine_at + by, lats)
        kinds = jnp.where((jnp.arange(lats) == owner)[:, None], theirs[None], kinds)
    kinds = kinds.reshape(32)

    last_lat = (lax.axis_index("lat") == lax.axis_size("lat") - 1).astype(jnp.int32)
    scal = jnp.concatenate([window_kinds, last_lat.reshape(1)])
    bias = expand_bias(bias_table.transpose(1, 0, 2), scal)

    bias, kinds = lax.optimization_barrier((bias, kinds))
    own, east_out, south_out, diag_out, send = attend(
        x,
        u,
        east,
        south,
        diag,
        own_ids,
        class_table,
        norm_gain.reshape(1, WIDTH),
        norm_bias.reshape(1, WIDTH),
        qkv_weight,
        qkv_bias,
        out_weight,
        bias,
    )
    east_back = moved(east_out, 1, 0).reshape(9, 6, 8, WIDTH)
    south_back = moved(south_out, 0, 1).reshape(3, 6, 8, WIDTH)
    diag_back = moved(diag_out, 1, 1).reshape(3, 6, 8, WIDTH)
    own = own.reshape(9, 6, 8, WIDTH)

    root = math.sqrt(inputs.size // WIDTH * lax.axis_size("lon") * lax.axis_size("lat"))
    received = lax.all_to_all(send.reshape(128, SEND_ROWS, 128), BOTH, 0, 0)
    grad_x = jnp.concatenate(
        [
            jnp.concatenate([diag_back, south_back], axis=1),
            jnp.concatenate([east_back, own], axis=1),
        ],
        axis=0,
    )
    received, grad_x = lax.optimization_barrier((received, grad_x))
    part = summed(received.reshape(128 * SEND_ROWS, 128), root)
    same_core = [[d for d in range(128) if d % 2 == core] for core in range(2)]
    mine = lax.all_to_all(
        part.reshape(64, GATHER_ROWS, 128), BOTH, 0, 0, axis_index_groups=same_core
    )
    other = lax.ppermute(mine, BOTH, [(d, d ^ 1) for d in range(128)])
    flat = (64 * GATHER_ROWS, 128)
    scal = jnp.concatenate([kinds, (lax.axis_index("lat") % 2).reshape(1)])
    table, grad_class, grad_gain, grad_nb, grad_wqkv, grad_bqkv, grad_wout, grad_bout = spread(
        mine.reshape(flat), other.reshape(flat), scal
    )

    return (
        grad_x.transpose(2, 0, 1, 3)[None],
        grad_class,
        grad_gain,
        grad_nb,
        grad_wqkv,
        grad_bqkv,
        grad_wout,
        grad_bout,
        table.transpose(1, 0, 2),
    )


def solution(mesh):
    placed = (
        P(None, None, "lat", "lon", None),
        P(None, None, "lat", "lon", None),
        P("lat", "lon"),
        P("lat"),
        P(),
        P(),
        P(),
        P(),
        P(),
        P(),
        P(),
    )
    return jax.shard_map(
        shards,
        mesh=mesh,
        in_specs=placed,
        out_specs=(P(None, None, "lat", "lon", None), P(), P(), P(), P(), P(), P(), P(), P()),
        check_vma=False,
    )
```

```python
import math

import jax
import jax.numpy as jnp
import numpy as np
from jax import lax
from jax.experimental import pallas as pl
from jax.experimental.pallas import tpu as pltpu
from jax.sharding import PartitionSpec as P

WIDTH = 192
HEADS = 6
HEAD_DIM = 32
CLASSES = 4
WIN_TOKENS = 144
POSITIONS = 3312
SPREAD = 23
GROUP = 138
PAIRS = 864
MASKED_SCORE = -1000000000.0
NORM_EPS = 1e-05
LOG2E = 1.4426950408889634
SCALE = HEAD_DIM ** (-0.5)
VMEM = 56 * 1024 * 1024
SEND_ROWS = 24
GATHER_ROWS = 48
BOTH = ("lon", "lat")
PER_STEP = 2

f32 = jnp.float32
bf16 = jnp.bfloat16


def dot(a, b):
    return lax.dot_general(a, b, (((1,), (0,)), ((), ())), preferred_element_type=f32)


def dot_nt(a, b):
    return lax.dot_general(a, b, (((1,), (1,)), ((), ())), preferred_element_type=f32)


def dot_tn(a, b):
    return lax.dot_general(a, b, (((0,), (0,)), ((), ())), preferred_element_type=f32)


def iota(shape, axis):
    return lax.broadcasted_iota(jnp.int32, shape, axis)


def quotient(a, b):
    return jnp.floor((a.astype(f32) + 0.5) * (1.0 / b)).astype(jnp.int32)


def bias_kernel(scal_ref, tab_ref, out_ref, sel_ref, t_ref, e_ref, stage, sems):
    for w in range(8):
        kind = scal_ref[w]
        for h in range(HEADS):
            sel_ref[h, w : w + 1, 0:POSITIONS] = tab_ref[h, pl.ds(kind, 1), :]
    last_lat = scal_ref[8]
    for lu in range(2):
        for lt in range(2):
            for a in range(6):
                g = (lt * 2 + lu) * 6 + a
                for h in range(HEADS):
                    at = h * 12 + lt * 6 + a
                    piece = sel_ref[h, :, g * GROUP : g * GROUP + 256]
                    t_ref[lu, 0, pl.ds(at, 8, stride=72), :] = piece[:, 0:128]
                    t_ref[lu, 1, pl.ds(at, 8, stride=72), :] = piece[:, 128:256]
    row = iota((576, GROUP), 0)
    lane = iota((576, GROUP), 1)
    win = quotient(row, 72)
    la = row - 12 * quotient(row, 12)
    late = (la >= 6).astype(jnp.int32)
    low_lat = ((la - 6 * late) < 3).astype(jnp.int32)
    low_key = (lane < 3 * SPREAD).astype(jnp.int32)
    cut_lat = jnp.where(win >= 4, last_lat, 0) * (low_lat ^ low_key)
    cut_lev = ((win & 3) == 3).astype(jnp.int32)
    srow = iota((GROUP, 256), 0)
    scol = iota((GROUP, 256), 1)
    col_hi = (scol >= 128).astype(jnp.int32)
    col = scol - 128 * col_hi
    a_u = quotient(col, 12)
    base = a_u * SPREAD - (col - 12 * a_u) + 11
    base = jnp.where(col < 72, base + col_hi, -1000)
    for lu in range(2):
        cut = cut_lat + cut_lev * (late if lu == 0 else 1 - late)
        t = jnp.concatenate([t_ref[lu, 0], t_ref[lu, 1]], axis=1)[:, 0:GROUP]
        t = jnp.where(cut > 0, MASKED_SCORE, t * LOG2E)
        hi = t.astype(bf16)
        rest = t - hi.astype(f32)
        mid = rest.astype(bf16)
        low = (rest - mid.astype(f32)).astype(bf16)
        for ip in range(6):
            spread = jnp.where(srow == base + 2 * ip, 1.0, 0.0).astype(bf16)
            acc = dot(hi, spread) + dot(mid, spread) + dot(low, spread)
            e_ref[lu, pl.ds(2 * ip, 576, stride=12), :] = acc[:, 0:128]
            e_ref[lu, pl.ds(2 * ip + 1, 576, stride=12), :] = acc[:, 128:256]
    copies = []
    for w in range(8):
        for lu in range(2):
            for h in range(HEADS):
                at = (w * HEADS + h) * WIN_TOKENS
                turned = e_ref[lu, at : at + WIN_TOKENS, :].T
                to = h * WIN_TOKENS + lu * 72
                stage[w, to : to + 72, :] = turned[0:72, :]
        copies.append(pltpu.make_async_copy(stage.at[w], out_ref.at[w], sems.at[w]))
        copies[-1].start()
    for copy in copies:
        copy.wait()


def expand_bias(table, scal):
    return pl.pallas_call(
        bias_kernel,
        out_shape=jax.ShapeDtypeStruct((8, PAIRS, WIN_TOKENS), f32),
        in_specs=[
            pl.BlockSpec(memory_space=pltpu.SMEM),
            pl.BlockSpec(memory_space=pltpu.VMEM),
        ],
        out_specs=pl.BlockSpec(memory_space=pl.ANY),
        scratch_shapes=[
            pltpu.VMEM((HEADS, 8, 3456), f32),
            pltpu.VMEM((2, 2, 576, 128), f32),
            pltpu.VMEM((2, 8 * PAIRS, 128), f32),
            pltpu.VMEM((8, PAIRS, WIN_TOKENS), f32),
            pltpu.SemaphoreType.DMA((8,)),
        ],
        compiler_params=pltpu.CompilerParams(vmem_limit_bytes=VMEM),
        cost_estimate=pl.CostEstimate(flops=2 * 10**9, bytes_accessed=7 * 10**6, transcendentals=0),
        name="bias",
    )(scal, table)


def window_kernel(
    scal_ref,
    x_ref,
    u_ref,
    e_ref,
    s_ref,
    d_ref,
    ids_ref,
    ct_ref,
    gain_ref,
    nb_ref,
    w_ref,
    bq_ref,
    wo_ref,
    b_ref,
    own_ref,
    eo_ref,
    so_ref,
    do_ref,
    send_ref,
    xs,
    us,
    os,
    idc,
    w3,
    mask,
    fold,
    gw,
    gwo,
    sm,
    folded,
    snd,
):
    step = pl.program_id(0)

    @pl.when(step == 0)
    def _():
        for half in range(2):
            lanes = slice(0, 128) if half == 0 else slice(128, 192)
            far = slice(192, 320) if half == 0 else slice(320, 384)
            width = 128 if half == 0 else 64
            for lat in range(12):
                at = lat * 96
                if lat < 9:
                    src = (lat + 3) * 96 + 48
                    xs[half, at : at + 48, 0:width] = x_ref[src : src + 48, lanes].astype(f32)
                    us[half, at : at + 48, 0:width] = u_ref[src : src + 48, lanes].astype(f32)
                    east, esrc = e_ref, lat * 48
                else:
                    src = (lat - 9) * 48
                    xs[half, at : at + 48, 0:width] = s_ref[src : src + 48, lanes].astype(f32)
                    us[half, at : at + 48, 0:width] = s_ref[src : src + 48, far].astype(f32)
                    east, esrc = d_ref, (lat - 9) * 48
                xs[half, at + 48 : at + 96, 0:width] = east[esrc : esrc + 48, lanes].astype(f32)
                us[half, at + 48 : at + 96, 0:width] = east[esrc : esrc + 48, far].astype(f32)
        id_row = (
            ids_ref[0:1, 0:WIN_TOKENS]
            + e_ref[432:440, 0:WIN_TOKENS].astype(f32)[0:1]
            + s_ref[144:152, 0:WIN_TOKENS].astype(f32)[0:1]
            + d_ref[144:152, 0:WIN_TOKENS].astype(f32)[0:1]
        )
        same = iota((WIN_TOKENS, WIN_TOKENS), 0) == iota((WIN_TOKENS, WIN_TOKENS), 1)
        column = jnp.sum(jnp.where(same, id_row, 0.0), axis=1, keepdims=True)
        idc[...] = jnp.broadcast_to(column, (WIN_TOKENS, WIDTH))
        head = quotient(iota((PAIRS, WIDTH), 0), WIN_TOKENS)
        mask[...] = jnp.where(head == (iota((PAIRS, WIDTH), 1) >> 5), 1.0, 0.0).astype(bf16)
        for part in range(3):
            w3[part] = w_ref[:, part * WIDTH : (part + 1) * WIDTH]
        gw[...] = jnp.zeros_like(gw)
        gwo[...] = jnp.zeros_like(gwo)
        sm[...] = jnp.zeros_like(sm)

    for sub in range(PER_STEP):
        w = step * PER_STEP + sub
        wa = w // 4
        wl = w % 4
        first = wa * 576 + 2 * wl + 1
        second = wa * 576 + lax.rem(2 * wl + 2, 8)

        def window_of(ref):
            parts = []
            for half in range(2):
                rows = jnp.concatenate(
                    [ref[half, pl.ds(first, 72, stride=8), :], ref[half, pl.ds(second, 72, stride=8), :]],
                    axis=0,
                )
                parts.append(rows)
            return jnp.concatenate(parts, axis=1)[:, 0:WIDTH]

        x = window_of(xs)
        up = window_of(us)
        up_low = up.astype(bf16)
        cell = idc[pl.ds(pl.multiple_of(wa * 72, 8), 72), :]
        cell = jnp.concatenate([cell, cell], axis=0)
        embedded = jnp.where(
            cell < 1.5,
            jnp.where(cell < 0.5, ct_ref[0:1, :], ct_ref[1:2, :]),
            jnp.where(cell < 2.5, ct_ref[2:3, :], ct_ref[3:4, :]),
        )
        hidden = x + embedded
        centred = hidden - jnp.mean(hidden, axis=1, keepdims=True)
        inv_std = lax.rsqrt(jnp.mean(centred * centred, axis=1, keepdims=True) + NORM_EPS)
        normal_hat = centred * inv_std
        normed = (normal_hat * gain_ref[...] + nb_ref[...]).astype(bf16)

        bq = bq_ref[...].reshape(1, 3 * WIDTH)
        query = (dot(normed, w3[0]) + bq[:, 0:192]).astype(bf16)
        key = dot(normed, w3[1]) + bq[:, 192:384]
        value = dot(normed, w3[2]) + bq[:, 384:576]
        key_turned, value_turned = key.T.astype(bf16), value.T.astype(bf16)
        key_heads = jnp.concatenate([key.astype(bf16)] * HEADS, axis=0) * mask[...]
        value_heads = jnp.concatenate([value.astype(bf16)] * HEADS, axis=0) * mask[...]
        grad_mixed = dot_nt(up_low, wo_ref[...]).astype(bf16)

        def heads_of(a):
            return a.reshape(HEADS, WIN_TOKENS, WIN_TOKENS)

        def by_head(turned, pairs):
            parts = [
                dot(turned[h * 32 : h * 32 + 32], pairs[h * WIN_TOKENS : (h + 1) * WIN_TOKENS])
                for h in range(HEADS)
            ]
            return jnp.concatenate(parts, axis=0)

        def own_head(wide):
            lane = iota((WIN_TOKENS, WIDTH), 1)
            picked = wide[0:WIN_TOKENS]
            for h in range(1, HEADS):
                picked = jnp.where(lane >= 32 * h, wide[h * WIN_TOKENS : (h + 1) * WIN_TOKENS], picked)
            return picked

        scores = heads_of(dot_nt(key_heads, query) * (SCALE * LOG2E) + b_ref[sub])
        powers = jnp.exp2(scores - jnp.max(scores, axis=1, keepdims=True))
        attention = powers * (1.0 / jnp.sum(powers, axis=1, keepdims=True))
        attention_low = attention.astype(bf16).reshape(PAIRS, WIN_TOKENS)
        mixed = by_head(value_turned, attention_low).astype(bf16)
        gwo[...] += dot(mixed, up_low)
        grad_attention = heads_of(dot_nt(value_heads, grad_mixed))
        grad_value = own_head(dot(attention_low, grad_mixed))
        row_sum = jnp.sum(grad_attention * attention, axis=1, keepdims=True)
        grad_scores = attention * (grad_attention - row_sum)
        grad_scores_low = grad_scores.astype(bf16).reshape(PAIRS, WIN_TOKENS)
        grad_key = own_head(dot(grad_scores_low, query)) * SCALE
        grad_query = (by_head(key_turned, grad_scores_low) * SCALE).T
        for h in range(HEADS):
            at = pl.multiple_of((w * HEADS + h) * WIN_TOKENS, WIN_TOKENS)
            for lu in range(2):
                fold[lu, pl.ds(at, WIN_TOKENS), :] = grad_scores[h, lu * 16 : lu * 16 + 128, :].T

        normed_turned = normed.T
        grad_normed = jnp.zeros((WIN_TOKENS, WIDTH), f32)
        for part, grad in enumerate((grad_query, grad_key, grad_value)):
            sm[6 + part : 7 + part, :] += jnp.sum(grad, axis=0, keepdims=True)
            grad_low = grad.astype(bf16)
            gw[part] += dot(normed_turned, grad_low)
            grad_normed = grad_normed + dot_nt(grad_low, w3[part])

        scaled = grad_normed * gain_ref[...]
        scaled_mean = jnp.mean(scaled, axis=1, keepdims=True)
        hat_mean = jnp.mean(scaled * normal_hat, axis=1, keepdims=True)
        grad_hidden = up + inv_std * (scaled - scaled_mean - normal_hat * hat_mean)
        for k in range(CLASSES):
            picked = jnp.where(cell == float(k), grad_hidden, 0.0)
            sm[k : k + 1, :] += jnp.sum(picked, axis=0, keepdims=True)
        sm[4:5, :] += jnp.sum(grad_normed * normal_hat, axis=0, keepdims=True)
        sm[5:6, :] += jnp.sum(grad_normed, axis=0, keepdims=True)
        sm[9:10, :] += jnp.sum(up, axis=0, keepdims=True)
        for half in range(2):
            if half == 0:
                part = grad_hidden[:, 0:128]
            else:
                part = jnp.concatenate([grad_hidden[:, 128:192], jnp.zeros((WIN_TOKENS, 64), f32)], axis=1)
            os[half, pl.ds(first, 72, stride=8), :] = part[0:72]
            os[half, pl.ds(second, 72, stride=8), :] = part[72:144]

    @pl.when(step == 8 // PER_STEP - 1)
    def _():
        for half in range(2):
            lanes = slice(0, 128) if half == 0 else slice(128, 192)
            width = 128 if half == 0 else 64
            for lat in range(12):
                at = lat * 96
                west, east = (own_ref, eo_ref) if lat < 9 else (so_ref, do_ref)
                to = (lat if lat < 9 else lat - 9) * 48
                west[to : to + 48, lanes] = os[half, at : at + 48, 0:width].astype(bf16)
                east[to : to + 48, lanes] = os[half, at + 48 : at + 96, 0:width].astype(bf16)
        srow = iota((256, 256), 0)
        scol = iota((256, 256), 1)
        row_hi = (srow >= 128).astype(jnp.int32)
        pos = srow - 128 * row_hi
        tail = scol - 128
        tail = tail - 10 * quotient(tail, 10) + 128
        wanted = jnp.where(scol < 128, scol, jnp.where(scol < 218, tail, -1))
        for lu in range(2):
            key_at = pos - 56 * lu
            a_u = quotient(key_at, 12)
            target = a_u * SPREAD - (key_at - 12 * a_u) + 11 + row_hi
            target = jnp.where((key_at >= 0) & (key_at < 72), target, -1000)
            acc = jnp.zeros((576, 256), f32)
            for ip in range(6):
                sums = jnp.where(target + 2 * ip == wanted, 1.0, 0.0).astype(bf16)
                both = jnp.concatenate(
                    [fold[lu, pl.ds(2 * ip + i, 576, stride=12), :] for i in range(2)], axis=1
                ).astype(bf16)
                acc = acc + dot(both, sums)
            for at in range(8):
                rows = acc[at * 72 : (at + 1) * 72]
                folded[0, pl.ds(lu * 576 + at, 72, stride=8), :] = rows[:, 0:128]
                folded[1, pl.ds(lu * 576 + at, 72, stride=8), :] = rows[:, 128:256]

        def put(k, plane):
            for core in range(2):
                rows = pl.ds(core * SEND_ROWS + k, 64, stride=2 * SEND_ROWS)
                snd[rows, :] = plane[core * 64 : (core + 1) * 64]

        for k in range(9):
            put(k, folded[0, k * 128 : (k + 1) * 128])
        lane = iota((128, 128), 1)
        slot = quotient(lane, 10)
        plane = jnp.zeros((128, 128), f32)
        for k in range(9):
            plane = jnp.where(slot == k, folded[1, k * 128 : (k + 1) * 128], plane)
        small = sm[...]
        small = jnp.concatenate(
            [
                jnp.zeros((96, 128), f32),
                small[0:10, 0:128],
                jnp.concatenate([small[0:10, 128:192], jnp.zeros((10, 64), f32)], axis=1),
                jnp.zeros((12, 128), f32),
            ],
            axis=0,
        )
        put(9, jnp.where(lane < 96, plane, small.T))
        weights = jnp.concatenate([gw[0], gw[1], gw[2], gwo[...]], axis=1)
        weights = jnp.concatenate([weights[:, b * 128 : (b + 1) * 128] for b in range(6)], axis=0)
        for k in range(9):
            put(10 + k, weights[k * 128 : (k + 1) * 128])
        kinds = jnp.zeros((128, 128), f32)
        for win in range(8):
            kinds = jnp.where(lane == win, scal_ref[win].astype(f32), kinds)
        put(19, kinds)
        for k in range(20, SEND_ROWS):
            put(k, jnp.zeros((128, 128), f32))
        send_ref[...] = snd[...].astype(bf16)


def attend(scal, x, u, east, south, diag, ids, ct, gain, nb, w3, bq, wo, bias):
    def whole(shape):
        return pl.BlockSpec(shape, lambda w: (0,) * len(shape))

    ins = [x, u, east, south, diag, ids, ct, gain, nb, w3, bq, wo]
    outs = [(432, WIDTH), (432, WIDTH), (144, WIDTH), (144, WIDTH), (128 * SEND_ROWS, 128)]
    return pl.pallas_call(
        window_kernel,
        grid=(8 // PER_STEP,),
        out_shape=[jax.ShapeDtypeStruct(o, bf16) for o in outs],
        in_specs=[pl.BlockSpec(memory_space=pltpu.SMEM)]
        + [whole(a.shape) for a in ins]
        + [pl.BlockSpec((PER_STEP, PAIRS, WIN_TOKENS), lambda w: (w, 0, 0))],
        out_specs=[whole(o) for o in outs],
        scratch_shapes=[
            pltpu.VMEM((2, 1152, 128), f32),
            pltpu.VMEM((2, 1152, 128), f32),
            pltpu.VMEM((2, 1152, 128), f32),
            pltpu.VMEM((WIN_TOKENS, WIDTH), f32),
            pltpu.VMEM((3, WIDTH, WIDTH), bf16),
            pltpu.VMEM((PAIRS, WIDTH), bf16),
            pltpu.VMEM((2, 8 * PAIRS, 128), f32),
            pltpu.VMEM((3, WIDTH, WIDTH), f32),
            pltpu.VMEM((WIDTH, WIDTH), f32),
            pltpu.VMEM((16, WIDTH), f32),
            pltpu.VMEM((2, 1152, 128), f32),
            pltpu.VMEM((128 * SEND_ROWS, 128), f32),
        ],
        compiler_params=pltpu.CompilerParams(
            vmem_limit_bytes=VMEM, dimension_semantics=("arbitrary",)
        ),
        cost_estimate=pl.CostEstimate(flops=4 * 10**9, bytes_accessed=8 * 10**6, transcendentals=10**6),
        name="windows",
    )(scal, *ins, bias)


def sum_kernel(root, core_ref, in_ref, out_ref, kinds_ref):
    first = in_ref[0 : 4 * SEND_ROWS, :].astype(f32)
    kinds = [first[lat * SEND_ROWS + 19 : lat * SEND_ROWS + 20] for lat in range(4)]
    kinds = jnp.concatenate(kinds + [jnp.zeros((4, 128), f32)], axis=0).astype(jnp.int32)
    kinds_ref[...] = jnp.where(iota((8, 128), 1) == 8, core_ref[0], kinds)
    total = jnp.sum(in_ref[...].astype(f32).reshape(32, 4 * SEND_ROWS, 128), axis=0) * (1.0 / root)
    parts = [total[lat * SEND_ROWS : (lat + 1) * SEND_ROWS] for lat in range(4)]
    shared = (parts[0] + parts[1]) + (parts[2] + parts[3])
    tails = [
        jnp.concatenate(
            [
                parts[j][9:10, 0:90],
                parts[3][9:10, 30 * j : 30 * j + 30],
                shared[9:10, 96 + 7 * j : 103 + 7 * j],
                jnp.zeros((1, 1), f32),
            ],
            axis=1,
        )
        for j in range(3)
    ]
    rows = [p[0:9] for p in parts] + [shared[10:19]] + tails
    rows = jnp.concatenate(rows, axis=0).astype(bf16)
    for peer in range(64):
        out_ref[peer * GATHER_ROWS : (peer + 1) * GATHER_ROWS, :] = rows


def summed(received, core, root):
    def body(core_ref, in_ref, out_ref, kinds_ref):
        sum_kernel(root, core_ref, in_ref, out_ref, kinds_ref)

    return pl.pallas_call(
        body,
        out_shape=[
            jax.ShapeDtypeStruct((64 * GATHER_ROWS, 128), bf16),
            jax.ShapeDtypeStruct((8, 128), jnp.int32),
        ],
        in_specs=[
            pl.BlockSpec(memory_space=pltpu.SMEM),
            pl.BlockSpec(memory_space=pltpu.VMEM),
        ],
        out_specs=[pl.BlockSpec(memory_space=pltpu.VMEM)] * 2,
        compiler_params=pltpu.CompilerParams(vmem_limit_bytes=VMEM),
        name="sums",
    )(core, received)


def spread_kernel(
    scal_ref,
    own_ref,
    other_ref,
    tab_ref,
    class_ref,
    gain_ref,
    nb_ref,
    wqkv_ref,
    bqkv_ref,
    wo_ref,
    bo_ref,
    g,
    tails,
    p,
):
    core = scal_ref[0, 8]
    half = 64 * GATHER_ROWS
    g[pl.ds(pl.multiple_of(core * half, half), half), :] = own_ref[...].astype(f32)
    g[pl.ds(pl.multiple_of((1 - core) * half, half), half), :] = other_ref[...].astype(f32)
    extra = [g[pl.ds(45 + j, 128, stride=GATHER_ROWS), :] for j in range(3)]
    for lat in range(3):
        tails[lat] = extra[lat]
    tails[3] = jnp.concatenate([e[:, 90:120] for e in extra] + [jnp.zeros((128, 38), f32)], axis=1)
    for lat in range(4):
        for w in range(8):
            kind = scal_ref[lat, w]
            for q in range(16):
                e = q * 8 + w
                src = e * GATHER_ROWS + lat * 9
                to = pl.multiple_of((q * 32 + kind) * 16, 16)
                p[pl.ds(to, 9), :] = g[src : src + 9, :]
                p[pl.ds(to + 9, 1), :] = tails[lat, e : e + 1, :]
    for m in range(144):
        k, q = m // 16, m % 16
        lu, c = m // 72, m % 72
        h, la = c // 12, c % 12
        at = (((la // 6) * 2 + lu) * 6 + la % 6) * GROUP
        tab_ref[h, :, at : at + 128] = p[pl.ds(q * 512 + k, 32, stride=16), :]
        tail = p[pl.ds(q * 512 + 9, 32, stride=16), :]
        tab_ref[h, :, at + 128 : at + GROUP] = tail[:, k * 10 : k * 10 + 10]
    weights = jnp.concatenate(
        [g[pl.ds(36 + k, 128, stride=GATHER_ROWS), :] for k in range(9)], axis=0
    )
    weights = jnp.concatenate([weights[b * 192 : (b + 1) * 192] for b in range(6)], axis=1)
    wqkv_ref[...] = weights[:, 0:576]
    wo_ref[...] = weights[:, 576:768]
    small = jnp.concatenate([e[:, 120:127] for e in extra] + [jnp.zeros((128, 107), f32)], axis=1).T
    small = jnp.concatenate([small[0:10], small[10:20]], axis=1)[:, 0:WIDTH]
    class_ref[...] = small[0:4]
    gain_ref[...] = small[4:5].reshape(WIDTH)
    nb_ref[...] = small[5:6].reshape(WIDTH)
    grad_bqkv = jnp.concatenate([small[6:7], small[7:8], small[8:9]], axis=1)
    bqkv_ref[...] = grad_bqkv.reshape(3 * WIDTH)
    bo_ref[...] = small[9:10].reshape(WIDTH)


def spread(own, other, scal):
    outs = [
        (HEADS, 32, POSITIONS),
        (CLASSES, WIDTH),
        (WIDTH,),
        (WIDTH,),
        (WIDTH, 3 * WIDTH),
        (3 * WIDTH,),
        (WIDTH, WIDTH),
        (WIDTH,),
    ]
    return pl.pallas_call(
        spread_kernel,
        out_shape=[jax.ShapeDtypeStruct(o, f32) for o in outs],
        in_specs=[
            pl.BlockSpec(memory_space=pltpu.SMEM),
            pl.BlockSpec(memory_space=pltpu.VMEM),
            pl.BlockSpec(memory_space=pltpu.VMEM),
        ],
        out_specs=[pl.BlockSpec(memory_space=pltpu.VMEM)] * len(outs),
        scratch_shapes=[
            pltpu.VMEM((128 * GATHER_ROWS, 128), f32),
            pltpu.VMEM((4, 128, 128), f32),
            pltpu.VMEM((16 * 32 * 16, 128), f32),
        ],
        compiler_params=pltpu.CompilerParams(vmem_limit_bytes=VMEM),
        name="spread",
    )(scal, own, other)


def pack_kernel(x_ref, u_ref, ids_ref, east_ref, south_ref, diag_ref, ids_out):
    lane = iota((1, WIN_TOKENS), 1)
    lat = quotient(lane, 12)
    lon = lane - 12 * lat
    ids = ids_ref[...].astype(f32)
    row = jnp.concatenate([ids[a : a + 1, :] for a in range(12)], axis=1)

    def moved_row(keep, by):
        kept = jnp.where(keep, row, 0.0)
        if by < 0:
            kept = jnp.concatenate([kept[:, -by:], jnp.zeros((1, 2 * WIDTH - WIN_TOKENS - by), f32)], axis=1)
        else:
            tail = jnp.zeros((1, 2 * WIDTH - WIN_TOKENS), f32)
            kept = jnp.concatenate([jnp.zeros((1, by), f32), kept[:, : WIN_TOKENS - by], tail], axis=1)
        return jnp.concatenate([kept, jnp.zeros((7, 2 * WIDTH), f32)], axis=0)

    def fill(out, lats, lon_at, id_rows):
        rows = []
        for a in lats:
            at = a * 96 + lon_at * 8
            rows.append(
                jnp.concatenate(
                    [x_ref[at : at + 48, :].astype(f32), u_ref[at : at + 48, :].astype(f32)], axis=1
                )
            )
        out[...] = jnp.concatenate(rows + [id_rows], axis=0).astype(bf16)

    fill(east_ref, range(3, 12), 0, moved_row((lat >= 3) & (lon < 6), -30))
    fill(south_ref, range(0, 3), 6, moved_row((lat < 3) & (lon >= 6), 102))
    fill(diag_ref, range(0, 3), 0, moved_row((lat < 3) & (lon < 6), 114))
    ids_out[...] = moved_row((lat >= 3) & (lon >= 6), -42)


def pack(x, u, ids):
    shapes = [((440, 2 * WIDTH), bf16), ((152, 2 * WIDTH), bf16), ((152, 2 * WIDTH), bf16)]
    shapes.append(((8, 2 * WIDTH), f32))
    return pl.pallas_call(
        pack_kernel,
        out_shape=[jax.ShapeDtypeStruct(*o) for o in shapes],
        in_specs=[pl.BlockSpec(memory_space=pltpu.VMEM)] * 3,
        out_specs=[pl.BlockSpec(memory_space=pltpu.VMEM)] * 4,
        compiler_params=pltpu.CompilerParams(vmem_limit_bytes=VMEM),
        name="pack",
    )(x, u, ids)


def moved(array, lon_by, lat_by):
    lon, lat = lax.axis_size("lon"), lax.axis_size("lat")
    pairs = [
        (i * lat + j, ((i + lon_by) % lon) * lat + (j + lat_by) % lat)
        for i in range(lon)
        for j in range(lat)
    ]
    return lax.ppermute(array, BOTH, pairs)


def shards(
    inputs,
    upstream,
    land_ids,
    window_kinds,
    class_table,
    norm_gain,
    norm_bias,
    qkv_weight,
    qkv_bias,
    out_weight,
    bias_table,
):
    x = inputs[0].transpose(1, 2, 0, 3)
    u = upstream[0].transpose(1, 2, 0, 3)
    x = x.reshape(1152, WIDTH)
    u = u.reshape(1152, WIDTH)
    east, south, diag, own_ids = pack(x, u, land_ids)
    east = moved(east, -1, 0)
    south = moved(south, 0, -1)
    diag = moved(diag, -1, -1)

    last_lat = (lax.axis_index("lat") == lax.axis_size("lat") - 1).astype(jnp.int32)
    scal = jnp.concatenate([window_kinds, last_lat.reshape(1)])
    bias = expand_bias(bias_table.transpose(1, 0, 2), scal)

    own, east_out, south_out, diag_out, send = attend(
        scal,
        x,
        u,
        east,
        south,
        diag,
        own_ids,
        class_table,
        norm_gain.reshape(1, WIDTH),
        norm_bias.reshape(1, WIDTH),
        qkv_weight,
        qkv_bias,
        out_weight,
        bias,
    )
    east_back = moved(east_out, 1, 0).reshape(9, 6, 8, WIDTH)
    south_back = moved(south_out, 0, 1).reshape(3, 6, 8, WIDTH)
    diag_back = moved(diag_out, 1, 1).reshape(3, 6, 8, WIDTH)
    own = own.reshape(9, 6, 8, WIDTH)

    root = math.sqrt(inputs.size // WIDTH * lax.axis_size("lon") * lax.axis_size("lat"))
    received = lax.all_to_all(send.reshape(128, SEND_ROWS, 128), BOTH, 0, 0)
    grad_x = jnp.concatenate(
        [
            jnp.concatenate([diag_back, south_back], axis=1),
            jnp.concatenate([east_back, own], axis=1),
        ],
        axis=0,
    )
    core = (lax.axis_index("lat") % 2).reshape(1)
    part, kinds = summed(received.reshape(128 * SEND_ROWS, 128), core, root)
    part, grad_x = lax.optimization_barrier((part, grad_x))
    same_core = [[d for d in range(128) if d % 2 == core] for core in range(2)]
    mine = lax.all_to_all(
        part.reshape(64, GATHER_ROWS, 128), BOTH, 0, 0, axis_index_groups=same_core
    )
    other = lax.ppermute(mine, BOTH, [(d, d ^ 1) for d in range(128)])
    flat = (64 * GATHER_ROWS, 128)
    table, grad_class, grad_gain, grad_nb, grad_wqkv, grad_bqkv, grad_wout, grad_bout = spread(
        mine.reshape(flat), other.reshape(flat), kinds
    )

    return (
        grad_x.transpose(2, 0, 1, 3)[None],
        grad_class,
        grad_gain,
        grad_nb,
        grad_wqkv,
        grad_bqkv,
        grad_wout,
        grad_bout,
        table.transpose(1, 0, 2),
    )


def solution(mesh):
    placed = (
        P(None, None, "lat", "lon", None),
        P(None, None, "lat", "lon", None),
        P("lat", "lon"),
        P("lat"),
        P(),
        P(),
        P(),
        P(),
        P(),
        P(),
        P(),
    )
    return jax.shard_map(
        shards,
        mesh=mesh,
        in_specs=placed,
        out_specs=(P(None, None, "lat", "lon", None), P(), P(), P(), P(), P(), P(), P(), P()),
        check_vma=False,
    )
```

```python
import math

import jax
import jax.numpy as jnp
import numpy as np
from jax import lax
from jax.experimental import pallas as pl
from jax.experimental.pallas import tpu as pltpu
from jax.sharding import PartitionSpec as P

WIDTH = 192
HEADS = 6
HEAD_DIM = 32
CLASSES = 4
WIN_TOKENS = 144
POSITIONS = 3312
SPREAD = 23
GROUP = 138
PAIRS = 864
MASKED_SCORE = -1000000000.0
NORM_EPS = 1e-05
LOG2E = 1.4426950408889634
SCALE = HEAD_DIM ** (-0.5)
VMEM = 56 * 1024 * 1024
SEND_ROWS = 24
GATHER_ROWS = 48
BOTH = ("lon", "lat")
PER_STEP = 2

f32 = jnp.float32
bf16 = jnp.bfloat16


def dot(a, b):
    return lax.dot_general(a, b, (((1,), (0,)), ((), ())), preferred_element_type=f32)


def dot_nt(a, b):
    return lax.dot_general(a, b, (((1,), (1,)), ((), ())), preferred_element_type=f32)


def dot_tn(a, b):
    return lax.dot_general(a, b, (((0,), (0,)), ((), ())), preferred_element_type=f32)


def iota(shape, axis):
    return lax.broadcasted_iota(jnp.int32, shape, axis)


def quotient(a, b):
    return jnp.floor((a.astype(f32) + 0.5) * (1.0 / b)).astype(jnp.int32)


def bias_kernel(scal_ref, tab_ref, out_ref, sel_ref, t_ref, e_ref, stage, sems):
    for w in range(8):
        kind = scal_ref[w]
        for h in range(HEADS):
            sel_ref[h, w : w + 1, 0:POSITIONS] = tab_ref[h, pl.ds(kind, 1), :]
    last_lat = scal_ref[8]
    for lu in range(2):
        for lt in range(2):
            for a in range(6):
                g = (lt * 2 + lu) * 6 + a
                for h in range(HEADS):
                    at = h * 12 + lt * 6 + a
                    piece = sel_ref[h, :, g * GROUP : g * GROUP + 256]
                    t_ref[lu, 0, pl.ds(at, 8, stride=72), :] = piece[:, 0:128]
                    t_ref[lu, 1, pl.ds(at, 8, stride=72), :] = piece[:, 128:256]
    row = iota((576, GROUP), 0)
    lane = iota((576, GROUP), 1)
    win = quotient(row, 72)
    la = row - 12 * quotient(row, 12)
    late = (la >= 6).astype(jnp.int32)
    low_lat = ((la - 6 * late) < 3).astype(jnp.int32)
    low_key = (lane < 3 * SPREAD).astype(jnp.int32)
    cut_lat = jnp.where(win >= 4, last_lat, 0) * (low_lat ^ low_key)
    cut_lev = ((win & 3) == 3).astype(jnp.int32)
    srow = iota((GROUP, 256), 0)
    scol = iota((GROUP, 256), 1)
    col_hi = (scol >= 128).astype(jnp.int32)
    col = scol - 128 * col_hi
    a_u = quotient(col, 12)
    base = a_u * SPREAD - (col - 12 * a_u) + 11
    base = jnp.where(col < 72, base + col_hi, -1000)
    for lu in range(2):
        cut = cut_lat + cut_lev * (late if lu == 0 else 1 - late)
        t = jnp.concatenate([t_ref[lu, 0], t_ref[lu, 1]], axis=1)[:, 0:GROUP]
        t = jnp.where(cut > 0, MASKED_SCORE, t * LOG2E)
        hi = t.astype(bf16)
        rest = t - hi.astype(f32)
        mid = rest.astype(bf16)
        low = (rest - mid.astype(f32)).astype(bf16)
        for ip in range(6):
            spread = jnp.where(srow == base + 2 * ip, 1.0, 0.0).astype(bf16)
            acc = dot(hi, spread) + dot(mid, spread) + dot(low, spread)
            e_ref[lu, pl.ds(2 * ip, 576, stride=12), :] = acc[:, 0:128]
            e_ref[lu, pl.ds(2 * ip + 1, 576, stride=12), :] = acc[:, 128:256]
    copies = []
    for w in range(8):
        for lu in range(2):
            for h in range(HEADS):
                at = (w * HEADS + h) * WIN_TOKENS
                turned = e_ref[lu, at : at + WIN_TOKENS, :].T
                to = h * WIN_TOKENS + lu * 72
                stage[w, to : to + 72, :] = turned[0:72, :]
        copies.append(pltpu.make_async_copy(stage.at[w], out_ref.at[w], sems.at[w]))
        copies[-1].start()
    for copy in copies:
        copy.wait()


def expand_bias(table, scal):
    return pl.pallas_call(
        bias_kernel,
        out_shape=jax.ShapeDtypeStruct((8, PAIRS, WIN_TOKENS), f32),
        in_specs=[
            pl.BlockSpec(memory_space=pltpu.SMEM),
            pl.BlockSpec(memory_space=pltpu.VMEM),
        ],
        out_specs=pl.BlockSpec(memory_space=pl.ANY),
        scratch_shapes=[
            pltpu.VMEM((HEADS, 8, 3456), f32),
            pltpu.VMEM((2, 2, 576, 128), f32),
            pltpu.VMEM((2, 8 * PAIRS, 128), f32),
            pltpu.VMEM((8, PAIRS, WIN_TOKENS), f32),
            pltpu.SemaphoreType.DMA((8,)),
        ],
        compiler_params=pltpu.CompilerParams(vmem_limit_bytes=VMEM),
        cost_estimate=pl.CostEstimate(flops=2 * 10**9, bytes_accessed=7 * 10**6, transcendentals=0),
        name="bias",
    )(scal, table)


def window_kernel(
    scal_ref,
    x_ref,
    u_ref,
    e_ref,
    s_ref,
    d_ref,
    ids_ref,
    ct_ref,
    gain_ref,
    nb_ref,
    w_ref,
    bq_ref,
    wo_ref,
    b_ref,
    own_ref,
    eo_ref,
    so_ref,
    do_ref,
    send_ref,
    xs,
    us,
    os,
    idc,
    w3,
    mask,
    fold,
    gw,
    gwo,
    sm,
    folded,
    snd,
):
    step = pl.program_id(0)

    @pl.when(step == 0)
    def _():
        for half in range(2):
            lanes = slice(0, 128) if half == 0 else slice(128, 192)
            far = slice(192, 320) if half == 0 else slice(320, 384)
            width = 128 if half == 0 else 64
            for lat in range(12):
                at = lat * 96
                if lat < 9:
                    src = (lat + 3) * 96 + 48
                    xs[half, at : at + 48, 0:width] = x_ref[src : src + 48, lanes].astype(f32)
                    us[half, at : at + 48, 0:width] = u_ref[src : src + 48, lanes].astype(f32)
                    east, esrc = e_ref, lat * 48
                else:
                    src = (lat - 9) * 48
                    xs[half, at : at + 48, 0:width] = s_ref[src : src + 48, lanes].astype(f32)
                    us[half, at : at + 48, 0:width] = s_ref[src : src + 48, far].astype(f32)
                    east, esrc = d_ref, (lat - 9) * 48
                xs[half, at + 48 : at + 96, 0:width] = east[esrc : esrc + 48, lanes].astype(f32)
                us[half, at + 48 : at + 96, 0:width] = east[esrc : esrc + 48, far].astype(f32)
        id_row = (
            ids_ref[0:1, 0:WIN_TOKENS]
            + e_ref[432:440, 0:WIN_TOKENS].astype(f32)[0:1]
            + s_ref[144:152, 0:WIN_TOKENS].astype(f32)[0:1]
            + d_ref[144:152, 0:WIN_TOKENS].astype(f32)[0:1]
        )
        same = iota((WIN_TOKENS, WIN_TOKENS), 0) == iota((WIN_TOKENS, WIN_TOKENS), 1)
        column = jnp.sum(jnp.where(same, id_row, 0.0), axis=1, keepdims=True)
        idc[...] = jnp.broadcast_to(column, (WIN_TOKENS, WIDTH))
        head = quotient(iota((PAIRS, WIDTH), 0), WIN_TOKENS)
        mask[...] = jnp.where(head == (iota((PAIRS, WIDTH), 1) >> 5), 1.0, 0.0).astype(bf16)
        for part in range(3):
            w3[part] = w_ref[:, part * WIDTH : (part + 1) * WIDTH]
        gw[...] = jnp.zeros_like(gw)
        gwo[...] = jnp.zeros_like(gwo)
        sm[...] = jnp.zeros_like(sm)

    for sub in range(PER_STEP):
        w = step * PER_STEP + sub
        wa = w // 4
        wl = w % 4
        first = wa * 576 + 2 * wl + 1
        second = wa * 576 + lax.rem(2 * wl + 2, 8)

        def window_of(ref):
            parts = []
            for half in range(2):
                rows = jnp.concatenate(
                    [ref[half, pl.ds(first, 72, stride=8), :], ref[half, pl.ds(second, 72, stride=8), :]],
                    axis=0,
                )
                parts.append(rows)
            return jnp.concatenate(parts, axis=1)[:, 0:WIDTH]

        x = window_of(xs)
        up = window_of(us)
        up_low = up.astype(bf16)
        cell = idc[pl.ds(pl.multiple_of(wa * 72, 8), 72), :]
        cell = jnp.concatenate([cell, cell], axis=0)
        embedded = jnp.where(
            cell < 1.5,
            jnp.where(cell < 0.5, ct_ref[0:1, :], ct_ref[1:2, :]),
            jnp.where(cell < 2.5, ct_ref[2:3, :], ct_ref[3:4, :]),
        )
        hidden = x + embedded
        centred = hidden - jnp.mean(hidden, axis=1, keepdims=True)
        inv_std = lax.rsqrt(jnp.mean(centred * centred, axis=1, keepdims=True) + NORM_EPS)
        normal_hat = centred * inv_std
        normed = (normal_hat * gain_ref[...] + nb_ref[...]).astype(bf16)

        bq = bq_ref[...].reshape(1, 3 * WIDTH)
        query = (dot(normed, w3[0]) + bq[:, 0:192]).astype(bf16)
        key = dot(normed, w3[1]) + bq[:, 192:384]
        value = dot(normed, w3[2]) + bq[:, 384:576]
        key_turned, value_turned = key.T.astype(bf16), value.T.astype(bf16)
        key_heads = jnp.concatenate([key.astype(bf16)] * HEADS, axis=0) * mask[...]
        value_heads = jnp.concatenate([value.astype(bf16)] * HEADS, axis=0) * mask[...]
        grad_mixed = dot_nt(up_low, wo_ref[...]).astype(bf16)

        def heads_of(a):
            return a.reshape(HEADS, WIN_TOKENS, WIN_TOKENS)

        def by_head(turned, pairs):
            parts = [
                dot(turned[h * 32 : h * 32 + 32], pairs[h * WIN_TOKENS : (h + 1) * WIN_TOKENS])
                for h in range(HEADS)
            ]
            return jnp.concatenate(parts, axis=0)

        def own_head(wide):
            lane = iota((WIN_TOKENS, WIDTH), 1)
            picked = wide[0:WIN_TOKENS]
            for h in range(1, HEADS):
                picked = jnp.where(lane >= 32 * h, wide[h * WIN_TOKENS : (h + 1) * WIN_TOKENS], picked)
            return picked

        scores = heads_of(dot_nt(key_heads, query) * (SCALE * LOG2E) + b_ref[sub])
        powers = jnp.exp2(scores - jnp.max(scores, axis=1, keepdims=True))
        attention = powers * (1.0 / jnp.sum(powers, axis=1, keepdims=True))
        attention_low = attention.astype(bf16).reshape(PAIRS, WIN_TOKENS)
        mixed = by_head(value_turned, attention_low).astype(bf16)
        gwo[...] += dot(mixed, up_low)
        grad_attention = heads_of(dot_nt(value_heads, grad_mixed))
        grad_value = own_head(dot(attention_low, grad_mixed))
        row_sum = jnp.sum(grad_attention * attention, axis=1, keepdims=True)
        grad_scores = attention * (grad_attention - row_sum)
        grad_scores_low = grad_scores.astype(bf16).reshape(PAIRS, WIN_TOKENS)
        grad_key = own_head(dot(grad_scores_low, query)) * SCALE
        grad_query = (by_head(key_turned, grad_scores_low) * SCALE).T
        for h in range(HEADS):
            at = pl.multiple_of((w * HEADS + h) * WIN_TOKENS, WIN_TOKENS)
            for lu in range(2):
                fold[lu, pl.ds(at, WIN_TOKENS), :] = grad_scores[h, lu * 16 : lu * 16 + 128, :].T

        normed_turned = normed.T
        grad_normed = jnp.zeros((WIN_TOKENS, WIDTH), f32)
        for part, grad in enumerate((grad_query, grad_key, grad_value)):
            sm[6 + part : 7 + part, :] += jnp.sum(grad, axis=0, keepdims=True)
            grad_low = grad.astype(bf16)
            gw[part] += dot(normed_turned, grad_low)
            grad_normed = grad_normed + dot_nt(grad_low, w3[part])

        scaled = grad_normed * gain_ref[...]
        scaled_mean = jnp.mean(scaled, axis=1, keepdims=True)
        hat_mean = jnp.mean(scaled * normal_hat, axis=1, keepdims=True)
        grad_hidden = up + inv_std * (scaled - scaled_mean - normal_hat * hat_mean)
        for k in range(CLASSES):
            picked = jnp.where(cell == float(k), grad_hidden, 0.0)
            sm[k : k + 1, :] += jnp.sum(picked, axis=0, keepdims=True)
        sm[4:5, :] += jnp.sum(grad_normed * normal_hat, axis=0, keepdims=True)
        sm[5:6, :] += jnp.sum(grad_normed, axis=0, keepdims=True)
        sm[9:10, :] += jnp.sum(up, axis=0, keepdims=True)
        for half in range(2):
            if half == 0:
                part = grad_hidden[:, 0:128]
            else:
                part = jnp.concatenate([grad_hidden[:, 128:192], jnp.zeros((WIN_TOKENS, 64), f32)], axis=1)
            os[half, pl.ds(first, 72, stride=8), :] = part[0:72]
            os[half, pl.ds(second, 72, stride=8), :] = part[72:144]

    @pl.when(step == 8 // PER_STEP - 1)
    def _():
        for half in range(2):
            lanes = slice(0, 128) if half == 0 else slice(128, 192)
            width = 128 if half == 0 else 64
            for lat in range(12):
                at = lat * 96
                west, east = (own_ref, eo_ref) if lat < 9 else (so_ref, do_ref)
                to = (lat if lat < 9 else lat - 9) * 48
                west[to : to + 48, lanes] = os[half, at : at + 48, 0:width].astype(bf16)
                east[to : to + 48, lanes] = os[half, at + 48 : at + 96, 0:width].astype(bf16)
        srow = iota((256, 256), 0)
        scol = iota((256, 256), 1)
        row_hi = (srow >= 128).astype(jnp.int32)
        pos = srow - 128 * row_hi
        tail = scol - 128
        tail = tail - 10 * quotient(tail, 10) + 128
        wanted = jnp.where(scol < 128, scol, jnp.where(scol < 218, tail, -1))
        for lu in range(2):
            key_at = pos - 56 * lu
            a_u = quotient(key_at, 12)
            target = a_u * SPREAD - (key_at - 12 * a_u) + 11 + row_hi
            target = jnp.where((key_at >= 0) & (key_at < 72), target, -1000)
            acc = jnp.zeros((576, 256), f32)
            for ip in range(6):
                sums = jnp.where(target + 2 * ip == wanted, 1.0, 0.0).astype(bf16)
                both = jnp.concatenate(
                    [fold[lu, pl.ds(2 * ip + i, 576, stride=12), :] for i in range(2)], axis=1
                ).astype(bf16)
                acc = acc + dot(both, sums)
            for at in range(8):
                rows = acc[at * 72 : (at + 1) * 72]
                folded[0, pl.ds(lu * 576 + at, 72, stride=8), :] = rows[:, 0:128]
                folded[1, pl.ds(lu * 576 + at, 72, stride=8), :] = rows[:, 128:256]

        def put(k, plane):
            for core in range(2):
                rows = pl.ds(core * SEND_ROWS + k, 64, stride=2 * SEND_ROWS)
                snd[rows, :] = plane[core * 64 : (core + 1) * 64]

        for k in range(9):
            put(k, folded[0, k * 128 : (k + 1) * 128])
        lane = iota((128, 128), 1)
        slot = quotient(lane, 10)
        plane = jnp.zeros((128, 128), f32)
        for k in range(9):
            plane = jnp.where(slot == k, folded[1, k * 128 : (k + 1) * 128], plane)
        small = sm[...]
        small = jnp.concatenate(
            [
                jnp.zeros((96, 128), f32),
                small[0:10, 0:128],
                jnp.concatenate([small[0:10, 128:192], jnp.zeros((10, 64), f32)], axis=1),
                jnp.zeros((12, 128), f32),
            ],
            axis=0,
        )
        put(9, jnp.where(lane < 96, plane, small.T))
        weights = jnp.concatenate([gw[0], gw[1], gw[2], gwo[...]], axis=1)
        weights = jnp.concatenate([weights[:, b * 128 : (b + 1) * 128] for b in range(6)], axis=0)
        for k in range(9):
            put(10 + k, weights[k * 128 : (k + 1) * 128])
        kinds = jnp.zeros((128, 128), f32)
        for win in range(8):
            kinds = jnp.where(lane == win, scal_ref[win].astype(f32), kinds)
        put(19, kinds)
        for k in range(20, SEND_ROWS):
            put(k, jnp.zeros((128, 128), f32))
        send_ref[...] = snd[...].astype(bf16)


def attend(scal, x, u, east, south, diag, ids, ct, gain, nb, w3, bq, wo, bias):
    def whole(shape):
        return pl.BlockSpec(shape, lambda w: (0,) * len(shape))

    ins = [x, u, east, south, diag, ids, ct, gain, nb, w3, bq, wo]
    outs = [(432, WIDTH), (432, WIDTH), (144, WIDTH), (144, WIDTH), (128 * SEND_ROWS, 128)]
    return pl.pallas_call(
        window_kernel,
        grid=(8 // PER_STEP,),
        out_shape=[jax.ShapeDtypeStruct(o, bf16) for o in outs],
        in_specs=[pl.BlockSpec(memory_space=pltpu.SMEM)]
        + [whole(a.shape) for a in ins]
        + [pl.BlockSpec((PER_STEP, PAIRS, WIN_TOKENS), lambda w: (w, 0, 0))],
        out_specs=[whole(o) for o in outs],
        scratch_shapes=[
            pltpu.VMEM((2, 1152, 128), f32),
            pltpu.VMEM((2, 1152, 128), f32),
            pltpu.VMEM((2, 1152, 128), f32),
            pltpu.VMEM((WIN_TOKENS, WIDTH), f32),
            pltpu.VMEM((3, WIDTH, WIDTH), bf16),
            pltpu.VMEM((PAIRS, WIDTH), bf16),
            pltpu.VMEM((2, 8 * PAIRS, 128), f32),
            pltpu.VMEM((3, WIDTH, WIDTH), f32),
            pltpu.VMEM((WIDTH, WIDTH), f32),
            pltpu.VMEM((16, WIDTH), f32),
            pltpu.VMEM((2, 1152, 128), f32),
            pltpu.VMEM((128 * SEND_ROWS, 128), f32),
        ],
        compiler_params=pltpu.CompilerParams(
            vmem_limit_bytes=VMEM, dimension_semantics=("arbitrary",)
        ),
        cost_estimate=pl.CostEstimate(flops=4 * 10**9, bytes_accessed=8 * 10**6, transcendentals=10**6),
        name="windows",
    )(scal, *ins, bias)


def sum_kernel(root, core_ref, in_ref, out_ref, kinds_ref):
    first = in_ref[0 : 4 * SEND_ROWS, :].astype(f32)
    kinds = [first[lat * SEND_ROWS + 19 : lat * SEND_ROWS + 20] for lat in range(4)]
    kinds = jnp.concatenate(kinds + [jnp.zeros((4, 128), f32)], axis=0).astype(jnp.int32)
    kinds_ref[...] = jnp.where(iota((8, 128), 1) == 8, core_ref[0], kinds)
    total = jnp.sum(in_ref[...].astype(f32).reshape(32, 4 * SEND_ROWS, 128), axis=0) * (1.0 / root)
    parts = [total[lat * SEND_ROWS : (lat + 1) * SEND_ROWS] for lat in range(4)]
    shared = (parts[0] + parts[1]) + (parts[2] + parts[3])
    tails = [
        jnp.concatenate(
            [
                parts[j][9:10, 0:90],
                parts[3][9:10, 30 * j : 30 * j + 30],
                shared[9:10, 96 + 7 * j : 103 + 7 * j],
                jnp.zeros((1, 1), f32),
            ],
            axis=1,
        )
        for j in range(3)
    ]
    rows = [p[0:9] for p in parts] + [shared[10:19]] + tails
    rows = jnp.concatenate(rows, axis=0).astype(bf16)
    for peer in range(64):
        out_ref[peer * GATHER_ROWS : (peer + 1) * GATHER_ROWS, :] = rows


def summed(received, core, root):
    def body(core_ref, in_ref, out_ref, kinds_ref):
        sum_kernel(root, core_ref, in_ref, out_ref, kinds_ref)

    return pl.pallas_call(
        body,
        out_shape=[
            jax.ShapeDtypeStruct((64 * GATHER_ROWS, 128), bf16),
            jax.ShapeDtypeStruct((8, 128), jnp.int32),
        ],
        in_specs=[
            pl.BlockSpec(memory_space=pltpu.SMEM),
            pl.BlockSpec(memory_space=pltpu.VMEM),
        ],
        out_specs=[pl.BlockSpec(memory_space=pltpu.VMEM)] * 2,
        compiler_params=pltpu.CompilerParams(vmem_limit_bytes=VMEM),
        name="sums",
    )(core, received)


def spread_kernel(
    scal_ref,
    own_ref,
    other_ref,
    tab_ref,
    class_ref,
    gain_ref,
    nb_ref,
    wqkv_ref,
    bqkv_ref,
    wo_ref,
    bo_ref,
    g,
    tails,
    p,
    stage,
    sems,
):
    core = scal_ref[0, 8]
    half = 64 * GATHER_ROWS
    g[pl.ds(pl.multiple_of(core * half, half), half), :] = own_ref[...].astype(f32)
    g[pl.ds(pl.multiple_of((1 - core) * half, half), half), :] = other_ref[...].astype(f32)
    extra = [g[pl.ds(45 + j, 128, stride=GATHER_ROWS), :] for j in range(3)]
    for lat in range(3):
        tails[lat] = extra[lat]
    tails[3] = jnp.concatenate([e[:, 90:120] for e in extra] + [jnp.zeros((128, 38), f32)], axis=1)
    for lat in range(4):
        for w in range(8):
            kind = scal_ref[lat, w]
            for q in range(16):
                e = q * 8 + w
                src = e * GATHER_ROWS + lat * 9
                to = pl.multiple_of((q * 32 + kind) * 16, 16)
                p[pl.ds(to, 9), :] = g[src : src + 9, :]
                p[pl.ds(to + 9, 1), :] = tails[lat, e : e + 1, :]
    copies = []
    for h in range(HEADS):
        for m in range(24):
            lu, la = m // 12, m % 12
            k, q = divmod(lu * 72 + h * 12 + la, 16)
            at = (((la // 6) * 2 + lu) * 6 + la % 6) * GROUP
            stage[h, :, at : at + 128] = p[pl.ds(q * 512 + k, 32, stride=16), :]
            tail = p[pl.ds(q * 512 + 9, 32, stride=16), :]
            stage[h, :, at + 128 : at + GROUP] = tail[:, k * 10 : k * 10 + 10]
        copies.append(pltpu.make_async_copy(stage.at[h], tab_ref.at[h], sems.at[h]))
        copies[-1].start()
    weights = jnp.concatenate(
        [g[pl.ds(36 + k, 128, stride=GATHER_ROWS), :] for k in range(9)], axis=0
    )
    weights = jnp.concatenate([weights[b * 192 : (b + 1) * 192] for b in range(6)], axis=1)
    wqkv_ref[...] = weights[:, 0:576]
    wo_ref[...] = weights[:, 576:768]
    small = jnp.concatenate([e[:, 120:127] for e in extra] + [jnp.zeros((128, 107), f32)], axis=1).T
    small = jnp.concatenate([small[0:10], small[10:20]], axis=1)[:, 0:WIDTH]
    class_ref[...] = small[0:4]
    gain_ref[...] = small[4:5].reshape(WIDTH)
    nb_ref[...] = small[5:6].reshape(WIDTH)
    grad_bqkv = jnp.concatenate([small[6:7], small[7:8], small[8:9]], axis=1)
    bqkv_ref[...] = grad_bqkv.reshape(3 * WIDTH)
    bo_ref[...] = small[9:10].reshape(WIDTH)
    for copy in copies:
        copy.wait()


def spread(own, other, scal):
    outs = [
        (HEADS, 32, POSITIONS),
        (CLASSES, WIDTH),
        (WIDTH,),
        (WIDTH,),
        (WIDTH, 3 * WIDTH),
        (3 * WIDTH,),
        (WIDTH, WIDTH),
        (WIDTH,),
    ]
    return pl.pallas_call(
        spread_kernel,
        out_shape=[jax.ShapeDtypeStruct(o, f32) for o in outs],
        in_specs=[
            pl.BlockSpec(memory_space=pltpu.SMEM),
            pl.BlockSpec(memory_space=pltpu.VMEM),
            pl.BlockSpec(memory_space=pltpu.VMEM),
        ],
        out_specs=[pl.BlockSpec(memory_space=pl.ANY)]
        + [pl.BlockSpec(memory_space=pltpu.VMEM)] * (len(outs) - 1),
        scratch_shapes=[
            pltpu.VMEM((128 * GATHER_ROWS, 128), f32),
            pltpu.VMEM((4, 128, 128), f32),
            pltpu.VMEM((16 * 32 * 16, 128), f32),
            pltpu.VMEM((HEADS, 32, POSITIONS), f32),
            pltpu.SemaphoreType.DMA((HEADS,)),
        ],
        compiler_params=pltpu.CompilerParams(vmem_limit_bytes=VMEM),
        cost_estimate=pl.CostEstimate(flops=10**10, bytes_accessed=10**7, transcendentals=0),
        name="spread",
    )(scal, own, other)


def pack_kernel(x_ref, u_ref, ids_ref, east_ref, south_ref, diag_ref, ids_out):
    lane = iota((1, WIN_TOKENS), 1)
    lat = quotient(lane, 12)
    lon = lane - 12 * lat
    ids = ids_ref[...].astype(f32)
    row = jnp.concatenate([ids[a : a + 1, :] for a in range(12)], axis=1)

    def moved_row(keep, by):
        kept = jnp.where(keep, row, 0.0)
        if by < 0:
            kept = jnp.concatenate([kept[:, -by:], jnp.zeros((1, 2 * WIDTH - WIN_TOKENS - by), f32)], axis=1)
        else:
            tail = jnp.zeros((1, 2 * WIDTH - WIN_TOKENS), f32)
            kept = jnp.concatenate([jnp.zeros((1, by), f32), kept[:, : WIN_TOKENS - by], tail], axis=1)
        return jnp.concatenate([kept, jnp.zeros((7, 2 * WIDTH), f32)], axis=0)

    def fill(out, lats, lon_at, id_rows):
        rows = []
        for a in lats:
            at = a * 96 + lon_at * 8
            rows.append(
                jnp.concatenate(
                    [x_ref[at : at + 48, :].astype(f32), u_ref[at : at + 48, :].astype(f32)], axis=1
                )
            )
        out[...] = jnp.concatenate(rows + [id_rows], axis=0).astype(bf16)

    fill(east_ref, range(3, 12), 0, moved_row((lat >= 3) & (lon < 6), -30))
    fill(south_ref, range(0, 3), 6, moved_row((lat < 3) & (lon >= 6), 102))
    fill(diag_ref, range(0, 3), 0, moved_row((lat < 3) & (lon < 6), 114))
    ids_out[...] = moved_row((lat >= 3) & (lon >= 6), -42)


def pack(x, u, ids):
    shapes = [((440, 2 * WIDTH), bf16), ((152, 2 * WIDTH), bf16), ((152, 2 * WIDTH), bf16)]
    shapes.append(((8, 2 * WIDTH), f32))
    return pl.pallas_call(
        pack_kernel,
        out_shape=[jax.ShapeDtypeStruct(*o) for o in shapes],
        in_specs=[pl.BlockSpec(memory_space=pltpu.VMEM)] * 3,
        out_specs=[pl.BlockSpec(memory_space=pltpu.VMEM)] * 4,
        compiler_params=pltpu.CompilerParams(vmem_limit_bytes=VMEM),
        name="pack",
    )(x, u, ids)


def moved(array, lon_by, lat_by):
    lon, lat = lax.axis_size("lon"), lax.axis_size("lat")
    pairs = [
        (i * lat + j, ((i + lon_by) % lon) * lat + (j + lat_by) % lat)
        for i in range(lon)
        for j in range(lat)
    ]
    return lax.ppermute(array, BOTH, pairs)


def shards(
    inputs,
    upstream,
    land_ids,
    window_kinds,
    class_table,
    norm_gain,
    norm_bias,
    qkv_weight,
    qkv_bias,
    out_weight,
    bias_table,
):
    x = inputs[0].transpose(1, 2, 0, 3)
    u = upstream[0].transpose(1, 2, 0, 3)
    x = x.reshape(1152, WIDTH)
    u = u.reshape(1152, WIDTH)
    east, south, diag, own_ids = pack(x, u, land_ids)
    east = moved(east, -1, 0)
    south = moved(south, 0, -1)
    diag = moved(diag, -1, -1)

    last_lat = (lax.axis_index("lat") == lax.axis_size("lat") - 1).astype(jnp.int32)
    scal = jnp.concatenate([window_kinds, last_lat.reshape(1)])
    bias = expand_bias(bias_table.transpose(1, 0, 2), scal)

    own, east_out, south_out, diag_out, send = attend(
        scal,
        x,
        u,
        east,
        south,
        diag,
        own_ids,
        class_table,
        norm_gain.reshape(1, WIDTH),
        norm_bias.reshape(1, WIDTH),
        qkv_weight,
        qkv_bias,
        out_weight,
        bias,
    )
    east_back = moved(east_out, 1, 0).reshape(9, 6, 8, WIDTH)
    south_back = moved(south_out, 0, 1).reshape(3, 6, 8, WIDTH)
    diag_back = moved(diag_out, 1, 1).reshape(3, 6, 8, WIDTH)
    own = own.reshape(9, 6, 8, WIDTH)

    root = math.sqrt(inputs.size // WIDTH * lax.axis_size("lon") * lax.axis_size("lat"))
    received = lax.all_to_all(send.reshape(128, SEND_ROWS, 128), BOTH, 0, 0)
    core = (lax.axis_index("lat") % 2).reshape(1)
    part, kinds = summed(received.reshape(128 * SEND_ROWS, 128), core, root)
    same_core = [[d for d in range(128) if d % 2 == core] for core in range(2)]
    mine = lax.all_to_all(
        part.reshape(64, GATHER_ROWS, 128), BOTH, 0, 0, axis_index_groups=same_core
    )
    other = lax.ppermute(mine, BOTH, [(d, d ^ 1) for d in range(128)])
    flat = (64 * GATHER_ROWS, 128)
    table, grad_class, grad_gain, grad_nb, grad_wqkv, grad_bqkv, grad_wout, grad_bout = spread(
        mine.reshape(flat), other.reshape(flat), kinds
    )
    table, east_back, south_back, diag_back = lax.optimization_barrier(
        (table, east_back, south_back, diag_back)
    )
    grad_x = jnp.concatenate(
        [
            jnp.concatenate([diag_back, south_back], axis=1),
            jnp.concatenate([east_back, own], axis=1),
        ],
        axis=0,
    )

    return (
        grad_x.transpose(2, 0, 1, 3)[None],
        grad_class,
        grad_gain,
        grad_nb,
        grad_wqkv,
        grad_bqkv,
        grad_wout,
        grad_bout,
        table.transpose(1, 0, 2),
    )


def solution(mesh):
    placed = (
        P(None, None, "lat", "lon", None),
        P(None, None, "lat", "lon", None),
        P("lat", "lon"),
        P("lat"),
        P(),
        P(),
        P(),
        P(),
        P(),
        P(),
        P(),
    )
    return jax.shard_map(
        shards,
        mesh=mesh,
        in_specs=placed,
        out_specs=(P(None, None, "lat", "lon", None), P(), P(), P(), P(), P(), P(), P(), P()),
        check_vma=False,
    )
```

```python
import math

import jax
import jax.numpy as jnp
import numpy as np
from jax import lax
from jax.experimental import pallas as pl
from jax.experimental.pallas import tpu as pltpu
from jax.sharding import PartitionSpec as P

WIDTH = 192
HEADS = 6
HEAD_DIM = 32
CLASSES = 4
WIN_TOKENS = 144
POSITIONS = 3312
SPREAD = 23
GROUP = 138
PAIRS = 864
MASKED_SCORE = -1000000000.0
NORM_EPS = 1e-05
LOG2E = 1.4426950408889634
SCALE = HEAD_DIM ** (-0.5)
MIB = 1024 * 1024
SEND_ROWS = 24
GATHER_ROWS = 48
BOTH = ("lon", "lat")
PER_STEP = 2

f32 = jnp.float32
bf16 = jnp.bfloat16


def dot(a, b):
    return lax.dot_general(a, b, (((1,), (0,)), ((), ())), preferred_element_type=f32)


def dot_nt(a, b):
    return lax.dot_general(a, b, (((1,), (1,)), ((), ())), preferred_element_type=f32)


def dot_tn(a, b):
    return lax.dot_general(a, b, (((0,), (0,)), ((), ())), preferred_element_type=f32)


def iota(shape, axis):
    return lax.broadcasted_iota(jnp.int32, shape, axis)


def quotient(a, b):
    return jnp.floor((a.astype(f32) + 0.5) * (1.0 / b)).astype(jnp.int32)


def bias_kernel(scal_ref, tab_ref, out_ref, sel_ref, t_ref, e_ref, stage, sems):
    for w in range(8):
        kind = scal_ref[w]
        for h in range(HEADS):
            sel_ref[h, w : w + 1, 0:POSITIONS] = tab_ref[h, pl.ds(kind, 1), :]
    last_lat = scal_ref[8]
    for lu in range(2):
        for lt in range(2):
            for a in range(6):
                g = (lt * 2 + lu) * 6 + a
                for h in range(HEADS):
                    at = h * 12 + lt * 6 + a
                    piece = sel_ref[h, :, g * GROUP : g * GROUP + 256]
                    t_ref[lu, 0, pl.ds(at, 8, stride=72), :] = piece[:, 0:128]
                    t_ref[lu, 1, pl.ds(at, 8, stride=72), :] = piece[:, 128:256]
    row = iota((576, GROUP), 0)
    lane = iota((576, GROUP), 1)
    win = quotient(row, 72)
    la = row - 12 * quotient(row, 12)
    late = (la >= 6).astype(jnp.int32)
    low_lat = ((la - 6 * late) < 3).astype(jnp.int32)
    low_key = (lane < 3 * SPREAD).astype(jnp.int32)
    cut_lat = jnp.where(win >= 4, last_lat, 0) * (low_lat ^ low_key)
    cut_lev = ((win & 3) == 3).astype(jnp.int32)
    srow = iota((GROUP, 256), 0)
    scol = iota((GROUP, 256), 1)
    col_hi = (scol >= 128).astype(jnp.int32)
    col = scol - 128 * col_hi
    a_u = quotient(col, 12)
    base = a_u * SPREAD - (col - 12 * a_u) + 11
    base = jnp.where(col < 72, base + col_hi, -1000)
    for lu in range(2):
        cut = cut_lat + cut_lev * (late if lu == 0 else 1 - late)
        t = jnp.concatenate([t_ref[lu, 0], t_ref[lu, 1]], axis=1)[:, 0:GROUP]
        t = jnp.where(cut > 0, MASKED_SCORE, t * LOG2E)
        hi = t.astype(bf16)
        rest = t - hi.astype(f32)
        mid = rest.astype(bf16)
        low = (rest - mid.astype(f32)).astype(bf16)
        for ip in range(6):
            spread = jnp.where(srow == base + 2 * ip, 1.0, 0.0).astype(bf16)
            acc = dot(hi, spread) + dot(mid, spread) + dot(low, spread)
            e_ref[lu, pl.ds(2 * ip, 576, stride=12), :] = acc[:, 0:128]
            e_ref[lu, pl.ds(2 * ip + 1, 576, stride=12), :] = acc[:, 128:256]
    copies = []
    for w in range(8):
        for lu in range(2):
            for h in range(HEADS):
                at = (w * HEADS + h) * WIN_TOKENS
                turned = e_ref[lu, at : at + WIN_TOKENS, :].T
                to = h * WIN_TOKENS + lu * 72
                stage[w, to : to + 72, :] = turned[0:72, :]
        copies.append(pltpu.make_async_copy(stage.at[w], out_ref.at[w], sems.at[w]))
        copies[-1].start()
    for copy in copies:
        copy.wait()


def expand_bias(table, scal):
    return pl.pallas_call(
        bias_kernel,
        out_shape=jax.ShapeDtypeStruct((8, PAIRS, WIN_TOKENS), f32),
        in_specs=[
            pl.BlockSpec(memory_space=pltpu.SMEM),
            pl.BlockSpec(memory_space=pltpu.VMEM),
        ],
        out_specs=pl.BlockSpec(memory_space=pl.ANY),
        scratch_shapes=[
            pltpu.VMEM((HEADS, 8, 3456), f32),
            pltpu.VMEM((2, 2, 576, 128), f32),
            pltpu.VMEM((2, 8 * PAIRS, 128), f32),
            pltpu.VMEM((8, PAIRS, WIN_TOKENS), f32),
            pltpu.SemaphoreType.DMA((8,)),
        ],
        compiler_params=pltpu.CompilerParams(vmem_limit_bytes=28 * MIB),
        cost_estimate=pl.CostEstimate(flops=2 * 10**9, bytes_accessed=7 * 10**6, transcendentals=0),
        name="bias",
    )(scal, table)


def window_kernel(
    scal_ref,
    x_ref,
    u_ref,
    e_ref,
    s_ref,
    d_ref,
    ids_ref,
    ct_ref,
    gain_ref,
    nb_ref,
    w_ref,
    bq_ref,
    wo_ref,
    b_ref,
    own_ref,
    eo_ref,
    so_ref,
    do_ref,
    send_ref,
    xs,
    us,
    os,
    idc,
    w3,
    mask,
    fold,
    gw,
    gwo,
    sm,
    folded,
    snd,
):
    step = pl.program_id(0)

    @pl.when(step == 0)
    def _():
        for half in range(2):
            lanes = slice(0, 128) if half == 0 else slice(128, 192)
            far = slice(192, 320) if half == 0 else slice(320, 384)
            width = 128 if half == 0 else 64
            for lat in range(12):
                at = lat * 96
                if lat < 9:
                    src = (lat + 3) * 96 + 48
                    xs[half, at : at + 48, 0:width] = x_ref[src : src + 48, lanes].astype(f32)
                    us[half, at : at + 48, 0:width] = u_ref[src : src + 48, lanes].astype(f32)
                    east, esrc = e_ref, lat * 48
                else:
                    src = (lat - 9) * 48
                    xs[half, at : at + 48, 0:width] = s_ref[src : src + 48, lanes].astype(f32)
                    us[half, at : at + 48, 0:width] = s_ref[src : src + 48, far].astype(f32)
                    east, esrc = d_ref, (lat - 9) * 48
                xs[half, at + 48 : at + 96, 0:width] = east[esrc : esrc + 48, lanes].astype(f32)
                us[half, at + 48 : at + 96, 0:width] = east[esrc : esrc + 48, far].astype(f32)
        id_row = (
            ids_ref[0:1, 0:WIN_TOKENS]
            + e_ref[432:440, 0:WIN_TOKENS].astype(f32)[0:1]
            + s_ref[144:152, 0:WIN_TOKENS].astype(f32)[0:1]
            + d_ref[144:152, 0:WIN_TOKENS].astype(f32)[0:1]
        )
        same = iota((WIN_TOKENS, WIN_TOKENS), 0) == iota((WIN_TOKENS, WIN_TOKENS), 1)
        column = jnp.sum(jnp.where(same, id_row, 0.0), axis=1, keepdims=True)
        idc[...] = jnp.broadcast_to(column, (WIN_TOKENS, WIDTH))
        head = quotient(iota((PAIRS, WIDTH), 0), WIN_TOKENS)
        mask[...] = jnp.where(head == (iota((PAIRS, WIDTH), 1) >> 5), 1.0, 0.0).astype(bf16)
        for part in range(3):
            w3[part] = w_ref[:, part * WIDTH : (part + 1) * WIDTH]
        gw[...] = jnp.zeros_like(gw)
        gwo[...] = jnp.zeros_like(gwo)
        sm[...] = jnp.zeros_like(sm)

    for sub in range(PER_STEP):
        w = step * PER_STEP + sub
        wa = w // 4
        wl = w % 4
        first = wa * 576 + 2 * wl + 1
        second = wa * 576 + lax.rem(2 * wl + 2, 8)

        def window_of(ref):
            parts = []
            for half in range(2):
                rows = jnp.concatenate(
                    [ref[half, pl.ds(first, 72, stride=8), :], ref[half, pl.ds(second, 72, stride=8), :]],
                    axis=0,
                )
                parts.append(rows)
            return jnp.concatenate(parts, axis=1)[:, 0:WIDTH]

        x = window_of(xs)
        up = window_of(us)
        up_low = up.astype(bf16)
        cell = idc[pl.ds(pl.multiple_of(wa * 72, 8), 72), :]
        cell = jnp.concatenate([cell, cell], axis=0)
        embedded = jnp.where(
            cell < 1.5,
            jnp.where(cell < 0.5, ct_ref[0:1, :], ct_ref[1:2, :]),
            jnp.where(cell < 2.5, ct_ref[2:3, :], ct_ref[3:4, :]),
        )
        hidden = x + embedded
        centred = hidden - jnp.mean(hidden, axis=1, keepdims=True)
        inv_std = lax.rsqrt(jnp.mean(centred * centred, axis=1, keepdims=True) + NORM_EPS)
        normal_hat = centred * inv_std
        normed = (normal_hat * gain_ref[...] + nb_ref[...]).astype(bf16)

        bq = bq_ref[...].reshape(1, 3 * WIDTH)
        query = (dot(normed, w3[0]) + bq[:, 0:192]).astype(bf16)
        key = dot(normed, w3[1]) + bq[:, 192:384]
        value = dot(normed, w3[2]) + bq[:, 384:576]
        key_turned, value_turned = key.T.astype(bf16), value.T.astype(bf16)
        key_heads = jnp.concatenate([key.astype(bf16)] * HEADS, axis=0) * mask[...]
        value_heads = jnp.concatenate([value.astype(bf16)] * HEADS, axis=0) * mask[...]
        grad_mixed = dot_nt(up_low, wo_ref[...]).astype(bf16)

        def heads_of(a):
            return a.reshape(HEADS, WIN_TOKENS, WIN_TOKENS)

        def by_head(turned, pairs):
            parts = [
                dot(turned[h * 32 : h * 32 + 32], pairs[h * WIN_TOKENS : (h + 1) * WIN_TOKENS])
                for h in range(HEADS)
            ]
            return jnp.concatenate(parts, axis=0)

        def own_head(wide):
            lane = iota((WIN_TOKENS, WIDTH), 1)
            picked = wide[0:WIN_TOKENS]
            for h in range(1, HEADS):
                picked = jnp.where(lane >= 32 * h, wide[h * WIN_TOKENS : (h + 1) * WIN_TOKENS], picked)
            return picked

        scores = heads_of(dot_nt(key_heads, query) * (SCALE * LOG2E) + b_ref[sub])
        powers = jnp.exp2(scores - jnp.max(scores, axis=1, keepdims=True))
        attention = powers * (1.0 / jnp.sum(powers, axis=1, keepdims=True))
        attention_low = attention.astype(bf16).reshape(PAIRS, WIN_TOKENS)
        mixed = by_head(value_turned, attention_low).astype(bf16)
        gwo[...] += dot(mixed, up_low)
        grad_attention = heads_of(dot_nt(value_heads, grad_mixed))
        grad_value = own_head(dot(attention_low, grad_mixed))
        row_sum = jnp.sum(grad_attention * attention, axis=1, keepdims=True)
        grad_scores = attention * (grad_attention - row_sum)
        grad_scores_low = grad_scores.astype(bf16).reshape(PAIRS, WIN_TOKENS)
        grad_key = own_head(dot(grad_scores_low, query)) * SCALE
        grad_query = (by_head(key_turned, grad_scores_low) * SCALE).T
        for h in range(HEADS):
            at = pl.multiple_of((w * HEADS + h) * WIN_TOKENS, WIN_TOKENS)
            for lu in range(2):
                fold[lu, pl.ds(at, WIN_TOKENS), :] = grad_scores[h, lu * 16 : lu * 16 + 128, :].T

        normed_turned = normed.T
        grad_normed = jnp.zeros((WIN_TOKENS, WIDTH), f32)
        for part, grad in enumerate((grad_query, grad_key, grad_value)):
            sm[6 + part : 7 + part, :] += jnp.sum(grad, axis=0, keepdims=True)
            grad_low = grad.astype(bf16)
            gw[part] += dot(normed_turned, grad_low)
            grad_normed = grad_normed + dot_nt(grad_low, w3[part])

        scaled = grad_normed * gain_ref[...]
        scaled_mean = jnp.mean(scaled, axis=1, keepdims=True)
        hat_mean = jnp.mean(scaled * normal_hat, axis=1, keepdims=True)
        grad_hidden = up + inv_std * (scaled - scaled_mean - normal_hat * hat_mean)
        for k in range(CLASSES):
            picked = jnp.where(cell == float(k), grad_hidden, 0.0)
            sm[k : k + 1, :] += jnp.sum(picked, axis=0, keepdims=True)
        sm[4:5, :] += jnp.sum(grad_normed * normal_hat, axis=0, keepdims=True)
        sm[5:6, :] += jnp.sum(grad_normed, axis=0, keepdims=True)
        sm[9:10, :] += jnp.sum(up, axis=0, keepdims=True)
        for half in range(2):
            if half == 0:
                part = grad_hidden[:, 0:128]
            else:
                part = jnp.concatenate([grad_hidden[:, 128:192], jnp.zeros((WIN_TOKENS, 64), f32)], axis=1)
            os[half, pl.ds(first, 72, stride=8), :] = part[0:72]
            os[half, pl.ds(second, 72, stride=8), :] = part[72:144]

    @pl.when(step == 8 // PER_STEP - 1)
    def _():
        for half in range(2):
            lanes = slice(0, 128) if half == 0 else slice(128, 192)
            width = 128 if half == 0 else 64
            for lat in range(12):
                at = lat * 96
                west, east = (own_ref, eo_ref) if lat < 9 else (so_ref, do_ref)
                to = (lat if lat < 9 else lat - 9) * 48
                west[to : to + 48, lanes] = os[half, at : at + 48, 0:width].astype(bf16)
                east[to : to + 48, lanes] = os[half, at + 48 : at + 96, 0:width].astype(bf16)
        srow = iota((256, 256), 0)
        scol = iota((256, 256), 1)
        row_hi = (srow >= 128).astype(jnp.int32)
        pos = srow - 128 * row_hi
        tail = scol - 128
        tail = tail - 10 * quotient(tail, 10) + 128
        wanted = jnp.where(scol < 128, scol, jnp.where(scol < 218, tail, -1))
        for lu in range(2):
            key_at = pos - 56 * lu
            a_u = quotient(key_at, 12)
            target = a_u * SPREAD - (key_at - 12 * a_u) + 11 + row_hi
            target = jnp.where((key_at >= 0) & (key_at < 72), target, -1000)
            acc = jnp.zeros((576, 256), f32)
            for ip in range(6):
                sums = jnp.where(target + 2 * ip == wanted, 1.0, 0.0).astype(bf16)
                both = jnp.concatenate(
                    [fold[lu, pl.ds(2 * ip + i, 576, stride=12), :] for i in range(2)], axis=1
                ).astype(bf16)
                acc = acc + dot(both, sums)
            for at in range(8):
                rows = acc[at * 72 : (at + 1) * 72]
                folded[0, pl.ds(lu * 576 + at, 72, stride=8), :] = rows[:, 0:128]
                folded[1, pl.ds(lu * 576 + at, 72, stride=8), :] = rows[:, 128:256]

        def put(k, plane):
            for core in range(2):
                rows = pl.ds(core * SEND_ROWS + k, 64, stride=2 * SEND_ROWS)
                snd[rows, :] = plane[core * 64 : (core + 1) * 64]

        for k in range(9):
            put(k, folded[0, k * 128 : (k + 1) * 128])
        lane = iota((128, 128), 1)
        slot = quotient(lane, 10)
        plane = jnp.zeros((128, 128), f32)
        for k in range(9):
            plane = jnp.where(slot == k, folded[1, k * 128 : (k + 1) * 128], plane)
        small = sm[...]
        small = jnp.concatenate(
            [
                jnp.zeros((96, 128), f32),
                small[0:10, 0:128],
                jnp.concatenate([small[0:10, 128:192], jnp.zeros((10, 64), f32)], axis=1),
                jnp.zeros((12, 128), f32),
            ],
            axis=0,
        )
        put(9, jnp.where(lane < 96, plane, small.T))
        weights = jnp.concatenate([gw[0], gw[1], gw[2], gwo[...]], axis=1)
        weights = jnp.concatenate([weights[:, b * 128 : (b + 1) * 128] for b in range(6)], axis=0)
        for k in range(9):
            put(10 + k, weights[k * 128 : (k + 1) * 128])
        kinds = jnp.zeros((128, 128), f32)
        for win in range(8):
            kinds = jnp.where(lane == win, scal_ref[win].astype(f32), kinds)
        put(19, kinds)
        for k in range(20, SEND_ROWS):
            put(k, jnp.zeros((128, 128), f32))
        send_ref[...] = snd[...].astype(bf16)


def attend(scal, x, u, east, south, diag, ids, ct, gain, nb, w3, bq, wo, bias):
    def whole(shape):
        return pl.BlockSpec(shape, lambda w: (0,) * len(shape))

    ins = [x, u, east, south, diag, ids, ct, gain, nb, w3, bq, wo]
    outs = [(432, WIDTH), (432, WIDTH), (144, WIDTH), (144, WIDTH), (128 * SEND_ROWS, 128)]
    return pl.pallas_call(
        window_kernel,
        grid=(8 // PER_STEP,),
        out_shape=[jax.ShapeDtypeStruct(o, bf16) for o in outs],
        in_specs=[pl.BlockSpec(memory_space=pltpu.SMEM)]
        + [whole(a.shape) for a in ins]
        + [pl.BlockSpec((PER_STEP, PAIRS, WIN_TOKENS), lambda w: (w, 0, 0))],
        out_specs=[whole(o) for o in outs],
        scratch_shapes=[
            pltpu.VMEM((2, 1152, 128), f32),
            pltpu.VMEM((2, 1152, 128), f32),
            pltpu.VMEM((2, 1152, 128), f32),
            pltpu.VMEM((WIN_TOKENS, WIDTH), f32),
            pltpu.VMEM((3, WIDTH, WIDTH), bf16),
            pltpu.VMEM((PAIRS, WIDTH), bf16),
            pltpu.VMEM((2, 8 * PAIRS, 128), f32),
            pltpu.VMEM((3, WIDTH, WIDTH), f32),
            pltpu.VMEM((WIDTH, WIDTH), f32),
            pltpu.VMEM((16, WIDTH), f32),
            pltpu.VMEM((2, 1152, 128), f32),
            pltpu.VMEM((128 * SEND_ROWS, 128), f32),
        ],
        compiler_params=pltpu.CompilerParams(
            vmem_limit_bytes=34 * MIB, dimension_semantics=("arbitrary",)
        ),
        cost_estimate=pl.CostEstimate(flops=4 * 10**9, bytes_accessed=8 * 10**6, transcendentals=10**6),
        name="windows",
    )(scal, *ins, bias)


def sum_kernel(root, core_ref, in_ref, out_ref, kinds_ref):
    first = in_ref[0 : 4 * SEND_ROWS, :].astype(f32)
    kinds = [first[lat * SEND_ROWS + 19 : lat * SEND_ROWS + 20] for lat in range(4)]
    kinds = jnp.concatenate(kinds + [jnp.zeros((4, 128), f32)], axis=0).astype(jnp.int32)
    kinds_ref[...] = jnp.where(iota((8, 128), 1) == 8, core_ref[0], kinds)
    total = jnp.sum(in_ref[...].astype(f32).reshape(32, 4 * SEND_ROWS, 128), axis=0) * (1.0 / root)
    parts = [total[lat * SEND_ROWS : (lat + 1) * SEND_ROWS] for lat in range(4)]
    shared = (parts[0] + parts[1]) + (parts[2] + parts[3])
    tails = [
        jnp.concatenate(
            [
                parts[j][9:10, 0:90],
                parts[3][9:10, 30 * j : 30 * j + 30],
                shared[9:10, 96 + 7 * j : 103 + 7 * j],
                jnp.zeros((1, 1), f32),
            ],
            axis=1,
        )
        for j in range(3)
    ]
    rows = [p[0:9] for p in parts] + [shared[10:19]] + tails
    rows = jnp.concatenate(rows, axis=0).astype(bf16)
    for peer in range(64):
        out_ref[peer * GATHER_ROWS : (peer + 1) * GATHER_ROWS, :] = rows


def summed(received, core, root):
    def body(core_ref, in_ref, out_ref, kinds_ref):
        sum_kernel(root, core_ref, in_ref, out_ref, kinds_ref)

    return pl.pallas_call(
        body,
        out_shape=[
            jax.ShapeDtypeStruct((64 * GATHER_ROWS, 128), bf16),
            jax.ShapeDtypeStruct((8, 128), jnp.int32),
        ],
        in_specs=[
            pl.BlockSpec(memory_space=pltpu.SMEM),
            pl.BlockSpec(memory_space=pltpu.VMEM),
        ],
        out_specs=[pl.BlockSpec(memory_space=pltpu.VMEM)] * 2,
        compiler_params=pltpu.CompilerParams(vmem_limit_bytes=10 * MIB),
        name="sums",
    )(core, received)


def spread_kernel(
    scal_ref,
    own_ref,
    other_ref,
    tab_ref,
    class_ref,
    gain_ref,
    nb_ref,
    wqkv_ref,
    bqkv_ref,
    wo_ref,
    bo_ref,
    g,
    tails,
    p,
    stage,
    sems,
):
    core = scal_ref[0, 8]
    half = 64 * GATHER_ROWS
    g[pl.ds(pl.multiple_of(core * half, half), half), :] = own_ref[...].astype(f32)
    g[pl.ds(pl.multiple_of((1 - core) * half, half), half), :] = other_ref[...].astype(f32)
    extra = [g[pl.ds(45 + j, 128, stride=GATHER_ROWS), :] for j in range(3)]
    for lat in range(3):
        tails[lat] = extra[lat]
    tails[3] = jnp.concatenate([e[:, 90:120] for e in extra] + [jnp.zeros((128, 38), f32)], axis=1)
    for lat in range(4):
        for w in range(8):
            kind = scal_ref[lat, w]
            for q in range(16):
                e = q * 8 + w
                src = e * GATHER_ROWS + lat * 9
                to = pl.multiple_of((q * 32 + kind) * 16, 16)
                p[pl.ds(to, 9), :] = g[src : src + 9, :]
                p[pl.ds(to + 9, 1), :] = tails[lat, e : e + 1, :]
    copies = []
    for h in range(HEADS):
        for m in range(24):
            lu, la = m // 12, m % 12
            k, q = divmod(lu * 72 + h * 12 + la, 16)
            at = (((la // 6) * 2 + lu) * 6 + la % 6) * GROUP
            stage[h, :, at : at + 128] = p[pl.ds(q * 512 + k, 32, stride=16), :]
            tail = p[pl.ds(q * 512 + 9, 32, stride=16), :]
            stage[h, :, at + 128 : at + GROUP] = tail[:, k * 10 : k * 10 + 10]
        copies.append(pltpu.make_async_copy(stage.at[h], tab_ref.at[h], sems.at[h]))
        copies[-1].start()
    weights = jnp.concatenate(
        [g[pl.ds(36 + k, 128, stride=GATHER_ROWS), :] for k in range(9)], axis=0
    )
    weights = jnp.concatenate([weights[b * 192 : (b + 1) * 192] for b in range(6)], axis=1)
    wqkv_ref[...] = weights[:, 0:576]
    wo_ref[...] = weights[:, 576:768]
    small = jnp.concatenate([e[:, 120:127] for e in extra] + [jnp.zeros((128, 107), f32)], axis=1).T
    small = jnp.concatenate([small[0:10], small[10:20]], axis=1)[:, 0:WIDTH]
    class_ref[...] = small[0:4]
    gain_ref[...] = small[4:5].reshape(WIDTH)
    nb_ref[...] = small[5:6].reshape(WIDTH)
    grad_bqkv = jnp.concatenate([small[6:7], small[7:8], small[8:9]], axis=1)
    bqkv_ref[...] = grad_bqkv.reshape(3 * WIDTH)
    bo_ref[...] = small[9:10].reshape(WIDTH)
    for copy in copies:
        copy.wait()


def spread(own, other, scal):
    outs = [
        (HEADS, 32, POSITIONS),
        (CLASSES, WIDTH),
        (WIDTH,),
        (WIDTH,),
        (WIDTH, 3 * WIDTH),
        (3 * WIDTH,),
        (WIDTH, WIDTH),
        (WIDTH,),
    ]
    return pl.pallas_call(
        spread_kernel,
        out_shape=[jax.ShapeDtypeStruct(o, f32) for o in outs],
        in_specs=[
            pl.BlockSpec(memory_space=pltpu.SMEM),
            pl.BlockSpec(memory_space=pltpu.VMEM),
            pl.BlockSpec(memory_space=pltpu.VMEM),
        ],
        out_specs=[pl.BlockSpec(memory_space=pl.ANY)]
        + [pl.BlockSpec(memory_space=pltpu.VMEM)] * (len(outs) - 1),
        scratch_shapes=[
            pltpu.VMEM((128 * GATHER_ROWS, 128), f32),
            pltpu.VMEM((4, 128, 128), f32),
            pltpu.VMEM((16 * 32 * 16, 128), f32),
            pltpu.VMEM((HEADS, 32, POSITIONS), f32),
            pltpu.SemaphoreType.DMA((HEADS,)),
        ],
        compiler_params=pltpu.CompilerParams(vmem_limit_bytes=24 * MIB),
        cost_estimate=pl.CostEstimate(flops=10**9, bytes_accessed=10**7, transcendentals=0),
        name="spread",
    )(scal, own, other)


def pack_kernel(x_ref, u_ref, ids_ref, east_ref, south_ref, diag_ref, ids_out):
    lane = iota((1, WIN_TOKENS), 1)
    lat = quotient(lane, 12)
    lon = lane - 12 * lat
    ids = ids_ref[...].astype(f32)
    row = jnp.concatenate([ids[a : a + 1, :] for a in range(12)], axis=1)

    def moved_row(keep, by):
        kept = jnp.where(keep, row, 0.0)
        if by < 0:
            kept = jnp.concatenate([kept[:, -by:], jnp.zeros((1, 2 * WIDTH - WIN_TOKENS - by), f32)], axis=1)
        else:
            tail = jnp.zeros((1, 2 * WIDTH - WIN_TOKENS), f32)
            kept = jnp.concatenate([jnp.zeros((1, by), f32), kept[:, : WIN_TOKENS - by], tail], axis=1)
        return jnp.concatenate([kept, jnp.zeros((7, 2 * WIDTH), f32)], axis=0)

    def fill(out, lats, lon_at, id_rows):
        rows = []
        for a in lats:
            at = a * 96 + lon_at * 8
            rows.append(
                jnp.concatenate(
                    [x_ref[at : at + 48, :].astype(f32), u_ref[at : at + 48, :].astype(f32)], axis=1
                )
            )
        out[...] = jnp.concatenate(rows + [id_rows], axis=0).astype(bf16)

    fill(east_ref, range(3, 12), 0, moved_row((lat >= 3) & (lon < 6), -30))
    fill(south_ref, range(0, 3), 6, moved_row((lat < 3) & (lon >= 6), 102))
    fill(diag_ref, range(0, 3), 0, moved_row((lat < 3) & (lon < 6), 114))
    ids_out[...] = moved_row((lat >= 3) & (lon >= 6), -42)


def pack(x, u, ids):
    shapes = [((440, 2 * WIDTH), bf16), ((152, 2 * WIDTH), bf16), ((152, 2 * WIDTH), bf16)]
    shapes.append(((8, 2 * WIDTH), f32))
    return pl.pallas_call(
        pack_kernel,
        out_shape=[jax.ShapeDtypeStruct(*o) for o in shapes],
        in_specs=[pl.BlockSpec(memory_space=pltpu.VMEM)] * 3,
        out_specs=[pl.BlockSpec(memory_space=pltpu.VMEM)] * 4,
        compiler_params=pltpu.CompilerParams(vmem_limit_bytes=56 * MIB),
        name="pack",
    )(x, u, ids)


def moved(array, lon_by, lat_by):
    lon, lat = lax.axis_size("lon"), lax.axis_size("lat")
    pairs = [
        (i * lat + j, ((i + lon_by) % lon) * lat + (j + lat_by) % lat)
        for i in range(lon)
        for j in range(lat)
    ]
    return lax.ppermute(array, BOTH, pairs)


def shards(
    inputs,
    upstream,
    land_ids,
    window_kinds,
    class_table,
    norm_gain,
    norm_bias,
    qkv_weight,
    qkv_bias,
    out_weight,
    bias_table,
):
    x = inputs[0].transpose(1, 2, 0, 3)
    u = upstream[0].transpose(1, 2, 0, 3)
    x = x.reshape(1152, WIDTH)
    u = u.reshape(1152, WIDTH)
    east, south, diag, own_ids = pack(x, u, land_ids)
    east = moved(east, -1, 0)
    south = moved(south, 0, -1)
    diag = moved(diag, -1, -1)

    last_lat = (lax.axis_index("lat") == lax.axis_size("lat") - 1).astype(jnp.int32)
    scal = jnp.concatenate([window_kinds, last_lat.reshape(1)])
    bias = expand_bias(bias_table.transpose(1, 0, 2), scal)

    own, east_out, south_out, diag_out, send = attend(
        scal,
        x,
        u,
        east,
        south,
        diag,
        own_ids,
        class_table,
        norm_gain.reshape(1, WIDTH),
        norm_bias.reshape(1, WIDTH),
        qkv_weight,
        qkv_bias,
        out_weight,
        bias,
    )
    east_back = moved(east_out, 1, 0).reshape(9, 6, 8, WIDTH)
    south_back = moved(south_out, 0, 1).reshape(3, 6, 8, WIDTH)
    diag_back = moved(diag_out, 1, 1).reshape(3, 6, 8, WIDTH)
    own = own.reshape(9, 6, 8, WIDTH)

    root = math.sqrt(inputs.size // WIDTH * lax.axis_size("lon") * lax.axis_size("lat"))
    received = lax.all_to_all(send.reshape(128, SEND_ROWS, 128), BOTH, 0, 0)
    core = (lax.axis_index("lat") % 2).reshape(1)
    part, kinds = summed(received.reshape(128 * SEND_ROWS, 128), core, root)
    same_core = [[d for d in range(128) if d % 2 == core] for core in range(2)]
    mine = lax.all_to_all(
        part.reshape(64, GATHER_ROWS, 128), BOTH, 0, 0, axis_index_groups=same_core
    )
    mine, east_back, south_back, diag_back = lax.optimization_barrier(
        (mine, east_back, south_back, diag_back)
    )
    other = lax.ppermute(mine, BOTH, [(d, d ^ 1) for d in range(128)])
    flat = (64 * GATHER_ROWS, 128)
    table, grad_class, grad_gain, grad_nb, grad_wqkv, grad_bqkv, grad_wout, grad_bout = spread(
        mine.reshape(flat), other.reshape(flat), kinds
    )
    grad_x = jnp.concatenate(
        [
            jnp.concatenate([diag_back, south_back], axis=1),
            jnp.concatenate([east_back, own], axis=1),
        ],
        axis=0,
    )

    return (
        grad_x.transpose(2, 0, 1, 3)[None],
        grad_class,
        grad_gain,
        grad_nb,
        grad_wqkv,
        grad_bqkv,
        grad_wout,
        grad_bout,
        table.transpose(1, 0, 2),
    )


def solution(mesh):
    placed = (
        P(None, None, "lat", "lon", None),
        P(None, None, "lat", "lon", None),
        P("lat", "lon"),
        P("lat"),
        P(),
        P(),
        P(),
        P(),
        P(),
        P(),
        P(),
    )
    return jax.shard_map(
        shards,
        mesh=mesh,
        in_specs=placed,
        out_specs=(P(None, None, "lat", "lon", None), P(), P(), P(), P(), P(), P(), P(), P()),
        check_vma=False,
    )
```

```python
import math

import jax
import jax.numpy as jnp
import numpy as np
from jax import lax
from jax.experimental import pallas as pl
from jax.experimental.pallas import tpu as pltpu
from jax.sharding import PartitionSpec as P

WIDTH = 192
HEADS = 6
HEAD_DIM = 32
CLASSES = 4
WIN_TOKENS = 144
POSITIONS = 3312
SPREAD = 23
GROUP = 138
PAIRS = 864
MASKED_SCORE = -1000000000.0
NORM_EPS = 1e-05
LOG2E = 1.4426950408889634
SCALE = HEAD_DIM ** (-0.5)
MIB = 1024 * 1024
SEND_ROWS = 24
GATHER_ROWS = 48
BOTH = ("lon", "lat")
PER_STEP = 2

f32 = jnp.float32
bf16 = jnp.bfloat16


def dot(a, b):
    return lax.dot_general(a, b, (((1,), (0,)), ((), ())), preferred_element_type=f32)


def dot_nt(a, b):
    return lax.dot_general(a, b, (((1,), (1,)), ((), ())), preferred_element_type=f32)


def dot_tn(a, b):
    return lax.dot_general(a, b, (((0,), (0,)), ((), ())), preferred_element_type=f32)


def iota(shape, axis):
    return lax.broadcasted_iota(jnp.int32, shape, axis)


def quotient(a, b):
    return jnp.floor((a.astype(f32) + 0.5) * (1.0 / b)).astype(jnp.int32)


def bias_kernel(scal_ref, tab_ref, out_ref, sel_ref, t_ref, e_ref, stage, sems):
    for w in range(8):
        kind = scal_ref[w]
        for h in range(HEADS):
            sel_ref[h, w : w + 1, 0:POSITIONS] = tab_ref[h, pl.ds(kind, 1), :]
    last_lat = scal_ref[8]
    for lu in range(2):
        for lt in range(2):
            for a in range(6):
                g = (lt * 2 + lu) * 6 + a
                for h in range(HEADS):
                    at = h * 12 + lt * 6 + a
                    piece = sel_ref[h, :, g * GROUP : g * GROUP + 256]
                    t_ref[lu, 0, pl.ds(at, 8, stride=72), :] = piece[:, 0:128]
                    t_ref[lu, 1, pl.ds(at, 8, stride=72), :] = piece[:, 128:256]
    row = iota((576, GROUP), 0)
    lane = iota((576, GROUP), 1)
    win = quotient(row, 72)
    la = row - 12 * quotient(row, 12)
    late = (la >= 6).astype(jnp.int32)
    low_lat = ((la - 6 * late) < 3).astype(jnp.int32)
    low_key = (lane < 3 * SPREAD).astype(jnp.int32)
    cut_lat = jnp.where(win >= 4, last_lat, 0) * (low_lat ^ low_key)
    cut_lev = ((win & 3) == 3).astype(jnp.int32)
    srow = iota((GROUP, 256), 0)
    scol = iota((GROUP, 256), 1)
    col_hi = (scol >= 128).astype(jnp.int32)
    col = scol - 128 * col_hi
    a_u = quotient(col, 12)
    base = a_u * SPREAD - (col - 12 * a_u) + 11
    base = jnp.where(col < 72, base + col_hi, -1000)
    for lu in range(2):
        cut = cut_lat + cut_lev * (late if lu == 0 else 1 - late)
        t = jnp.concatenate([t_ref[lu, 0], t_ref[lu, 1]], axis=1)[:, 0:GROUP]
        t = jnp.where(cut > 0, MASKED_SCORE, t * LOG2E)
        hi = t.astype(bf16)
        rest = t - hi.astype(f32)
        mid = rest.astype(bf16)
        low = (rest - mid.astype(f32)).astype(bf16)
        for ip in range(6):
            spread = jnp.where(srow == base + 2 * ip, 1.0, 0.0).astype(bf16)
            acc = dot(hi, spread) + dot(mid, spread) + dot(low, spread)
            e_ref[lu, pl.ds(2 * ip, 576, stride=12), :] = acc[:, 0:128]
            e_ref[lu, pl.ds(2 * ip + 1, 576, stride=12), :] = acc[:, 128:256]
    copies = []
    for w in range(8):
        for lu in range(2):
            for h in range(HEADS):
                at = (w * HEADS + h) * WIN_TOKENS
                turned = e_ref[lu, at : at + WIN_TOKENS, :].T
                to = h * WIN_TOKENS + lu * 72
                stage[w, to : to + 72, :] = turned[0:72, :]
        copies.append(pltpu.make_async_copy(stage.at[w], out_ref.at[w], sems.at[w]))
        copies[-1].start()
    for copy in copies:
        copy.wait()


def expand_bias(table, scal):
    return pl.pallas_call(
        bias_kernel,
        out_shape=jax.ShapeDtypeStruct((8, PAIRS, WIN_TOKENS), f32),
        in_specs=[
            pl.BlockSpec(memory_space=pltpu.SMEM),
            pl.BlockSpec(memory_space=pltpu.VMEM),
        ],
        out_specs=pl.BlockSpec(memory_space=pl.ANY),
        scratch_shapes=[
            pltpu.VMEM((HEADS, 8, 3456), f32),
            pltpu.VMEM((2, 2, 576, 128), f32),
            pltpu.VMEM((2, 8 * PAIRS, 128), f32),
            pltpu.VMEM((8, PAIRS, WIN_TOKENS), f32),
            pltpu.SemaphoreType.DMA((8,)),
        ],
        compiler_params=pltpu.CompilerParams(vmem_limit_bytes=28 * MIB),
        cost_estimate=pl.CostEstimate(flops=2 * 10**9, bytes_accessed=7 * 10**6, transcendentals=0),
        name="bias",
    )(scal, table)


def window_kernel(
    scal_ref,
    x_ref,
    u_ref,
    e_ref,
    s_ref,
    d_ref,
    ids_ref,
    ct_ref,
    gain_ref,
    nb_ref,
    w_ref,
    bq_ref,
    wo_ref,
    b_ref,
    own_ref,
    eo_ref,
    so_ref,
    do_ref,
    send_ref,
    xs,
    us,
    os,
    idc,
    w3,
    mask,
    fold,
    gw,
    gwo,
    sm,
    folded,
    snd,
):
    step = pl.program_id(0)

    @pl.when(step == 0)
    def _():
        for half in range(2):
            lanes = slice(0, 128) if half == 0 else slice(128, 192)
            far = slice(192, 320) if half == 0 else slice(320, 384)
            width = 128 if half == 0 else 64
            for lat in range(12):
                at = lat * 96
                if lat < 9:
                    src = (lat + 3) * 96 + 48
                    xs[half, at : at + 48, 0:width] = x_ref[src : src + 48, lanes].astype(f32)
                    us[half, at : at + 48, 0:width] = u_ref[src : src + 48, lanes].astype(f32)
                    east, esrc = e_ref, lat * 48
                else:
                    src = (lat - 9) * 48
                    xs[half, at : at + 48, 0:width] = s_ref[src : src + 48, lanes].astype(f32)
                    us[half, at : at + 48, 0:width] = s_ref[src : src + 48, far].astype(f32)
                    east, esrc = d_ref, (lat - 9) * 48
                xs[half, at + 48 : at + 96, 0:width] = east[esrc : esrc + 48, lanes].astype(f32)
                us[half, at + 48 : at + 96, 0:width] = east[esrc : esrc + 48, far].astype(f32)
        id_row = (
            ids_ref[0:1, 0:WIN_TOKENS]
            + e_ref[432:440, 0:WIN_TOKENS].astype(f32)[0:1]
            + s_ref[144:152, 0:WIN_TOKENS].astype(f32)[0:1]
            + d_ref[144:152, 0:WIN_TOKENS].astype(f32)[0:1]
        )
        same = iota((WIN_TOKENS, WIN_TOKENS), 0) == iota((WIN_TOKENS, WIN_TOKENS), 1)
        column = jnp.sum(jnp.where(same, id_row, 0.0), axis=1, keepdims=True)
        idc[...] = jnp.broadcast_to(column, (WIN_TOKENS, WIDTH))
        head = quotient(iota((PAIRS, WIDTH), 0), WIN_TOKENS)
        mask[...] = jnp.where(head == (iota((PAIRS, WIDTH), 1) >> 5), 1.0, 0.0).astype(bf16)
        for part in range(3):
            w3[part] = w_ref[:, part * WIDTH : (part + 1) * WIDTH]
        gw[...] = jnp.zeros_like(gw)
        gwo[...] = jnp.zeros_like(gwo)
        sm[...] = jnp.zeros_like(sm)

    for sub in range(PER_STEP):
        w = step * PER_STEP + sub
        wa = w // 4
        wl = w % 4
        first = wa * 576 + 2 * wl + 1
        second = wa * 576 + lax.rem(2 * wl + 2, 8)

        def window_of(ref):
            parts = []
            for half in range(2):
                rows = jnp.concatenate(
                    [ref[half, pl.ds(first, 72, stride=8), :], ref[half, pl.ds(second, 72, stride=8), :]],
                    axis=0,
                )
                parts.append(rows)
            return jnp.concatenate(parts, axis=1)[:, 0:WIDTH]

        x = window_of(xs)
        up = window_of(us)
        up_low = up.astype(bf16)
        cell = idc[pl.ds(pl.multiple_of(wa * 72, 8), 72), :]
        cell = jnp.concatenate([cell, cell], axis=0)
        embedded = jnp.where(
            cell < 1.5,
            jnp.where(cell < 0.5, ct_ref[0:1, :], ct_ref[1:2, :]),
            jnp.where(cell < 2.5, ct_ref[2:3, :], ct_ref[3:4, :]),
        )
        hidden = x + embedded
        centred = hidden - jnp.mean(hidden, axis=1, keepdims=True)
        inv_std = lax.rsqrt(jnp.mean(centred * centred, axis=1, keepdims=True) + NORM_EPS)
        normal_hat = centred * inv_std
        normed = (normal_hat * gain_ref[...] + nb_ref[...]).astype(bf16)

        bq = bq_ref[...].reshape(1, 3 * WIDTH)
        query = (dot(normed, w3[0]) + bq[:, 0:192]).astype(bf16)
        key = dot(normed, w3[1]) + bq[:, 192:384]
        value = dot(normed, w3[2]) + bq[:, 384:576]
        key_turned, value_turned = key.T.astype(bf16), value.T.astype(bf16)
        key_heads = jnp.concatenate([key.astype(bf16)] * HEADS, axis=0) * mask[...]
        value_heads = jnp.concatenate([value.astype(bf16)] * HEADS, axis=0) * mask[...]
        grad_mixed = dot_nt(up_low, wo_ref[...]).astype(bf16)

        def heads_of(a):
            return a.reshape(HEADS, WIN_TOKENS, WIN_TOKENS)

        def by_head(turned, pairs):
            parts = [
                dot(turned[h * 32 : h * 32 + 32], pairs[h * WIN_TOKENS : (h + 1) * WIN_TOKENS])
                for h in range(HEADS)
            ]
            return jnp.concatenate(parts, axis=0)

        def own_head(wide):
            lane = iota((WIN_TOKENS, WIDTH), 1)
            picked = wide[0:WIN_TOKENS]
            for h in range(1, HEADS):
                picked = jnp.where(lane >= 32 * h, wide[h * WIN_TOKENS : (h + 1) * WIN_TOKENS], picked)
            return picked

        scores = heads_of(dot_nt(key_heads, query) * (SCALE * LOG2E) + b_ref[sub])
        powers = jnp.exp2(scores - jnp.max(scores, axis=1, keepdims=True))
        attention = powers * (1.0 / jnp.sum(powers, axis=1, keepdims=True))
        attention_low = attention.astype(bf16).reshape(PAIRS, WIN_TOKENS)
        mixed = by_head(value_turned, attention_low).astype(bf16)
        gwo[...] += dot(mixed, up_low)
        grad_attention = heads_of(dot_nt(value_heads, grad_mixed))
        grad_value = own_head(dot(attention_low, grad_mixed))
        row_sum = jnp.sum(grad_attention * attention, axis=1, keepdims=True)
        grad_scores = attention * (grad_attention - row_sum)
        grad_scores_low = grad_scores.astype(bf16).reshape(PAIRS, WIN_TOKENS)
        grad_key = own_head(dot(grad_scores_low, query)) * SCALE
        grad_query = (by_head(key_turned, grad_scores_low) * SCALE).T
        for h in range(HEADS):
            at = pl.multiple_of((w * HEADS + h) * WIN_TOKENS, WIN_TOKENS)
            for lu in range(2):
                fold[lu, pl.ds(at, WIN_TOKENS), :] = grad_scores[h, lu * 16 : lu * 16 + 128, :].T

        normed_turned = normed.T
        grad_normed = jnp.zeros((WIN_TOKENS, WIDTH), f32)
        for part, grad in enumerate((grad_query, grad_key, grad_value)):
            sm[6 + part : 7 + part, :] += jnp.sum(grad, axis=0, keepdims=True)
            grad_low = grad.astype(bf16)
            gw[part] += dot(normed_turned, grad_low)
            grad_normed = grad_normed + dot_nt(grad_low, w3[part])

        scaled = grad_normed * gain_ref[...]
        scaled_mean = jnp.mean(scaled, axis=1, keepdims=True)
        hat_mean = jnp.mean(scaled * normal_hat, axis=1, keepdims=True)
        grad_hidden = up + inv_std * (scaled - scaled_mean - normal_hat * hat_mean)
        for k in range(CLASSES):
            picked = jnp.where(cell == float(k), grad_hidden, 0.0)
            sm[k : k + 1, :] += jnp.sum(picked, axis=0, keepdims=True)
        sm[4:5, :] += jnp.sum(grad_normed * normal_hat, axis=0, keepdims=True)
        sm[5:6, :] += jnp.sum(grad_normed, axis=0, keepdims=True)
        sm[9:10, :] += jnp.sum(up, axis=0, keepdims=True)
        for half in range(2):
            if half == 0:
                part = grad_hidden[:, 0:128]
            else:
                part = jnp.concatenate([grad_hidden[:, 128:192], jnp.zeros((WIN_TOKENS, 64), f32)], axis=1)
            os[half, pl.ds(first, 72, stride=8), :] = part[0:72]
            os[half, pl.ds(second, 72, stride=8), :] = part[72:144]

    @pl.when(step == 8 // PER_STEP - 1)
    def _():
        for half in range(2):
            lanes = slice(0, 128) if half == 0 else slice(128, 192)
            width = 128 if half == 0 else 64
            for lat in range(12):
                at = lat * 96
                west, east = (own_ref, eo_ref) if lat < 9 else (so_ref, do_ref)
                to = (lat if lat < 9 else lat - 9) * 48
                west[to : to + 48, lanes] = os[half, at : at + 48, 0:width].astype(bf16)
                east[to : to + 48, lanes] = os[half, at + 48 : at + 96, 0:width].astype(bf16)
        srow = iota((256, 256), 0)
        scol = iota((256, 256), 1)
        row_hi = (srow >= 128).astype(jnp.int32)
        pos = srow - 128 * row_hi
        tail = scol - 128
        tail = tail - 10 * quotient(tail, 10) + 128
        wanted = jnp.where(scol < 128, scol, jnp.where(scol < 218, tail, -1))
        for lu in range(2):
            key_at = pos - 56 * lu
            a_u = quotient(key_at, 12)
            target = a_u * SPREAD - (key_at - 12 * a_u) + 11 + row_hi
            target = jnp.where((key_at >= 0) & (key_at < 72), target, -1000)
            acc = jnp.zeros((576, 256), f32)
            for ip in range(6):
                sums = jnp.where(target + 2 * ip == wanted, 1.0, 0.0).astype(bf16)
                both = jnp.concatenate(
                    [fold[lu, pl.ds(2 * ip + i, 576, stride=12), :] for i in range(2)], axis=1
                ).astype(bf16)
                acc = acc + dot(both, sums)
            for at in range(8):
                rows = acc[at * 72 : (at + 1) * 72]
                folded[0, pl.ds(lu * 576 + at, 72, stride=8), :] = rows[:, 0:128]
                folded[1, pl.ds(lu * 576 + at, 72, stride=8), :] = rows[:, 128:256]

        def put(k, plane):
            for core in range(2):
                rows = pl.ds(core * SEND_ROWS + k, 64, stride=2 * SEND_ROWS)
                snd[rows, :] = plane[core * 64 : (core + 1) * 64]

        for k in range(9):
            put(k, folded[0, k * 128 : (k + 1) * 128])
        lane = iota((128, 128), 1)
        slot = quotient(lane, 10)
        plane = jnp.zeros((128, 128), f32)
        for k in range(9):
            plane = jnp.where(slot == k, folded[1, k * 128 : (k + 1) * 128], plane)
        small = sm[...]
        small = jnp.concatenate(
            [
                jnp.zeros((96, 128), f32),
                small[0:10, 0:128],
                jnp.concatenate([small[0:10, 128:192], jnp.zeros((10, 64), f32)], axis=1),
                jnp.zeros((12, 128), f32),
            ],
            axis=0,
        )
        put(9, jnp.where(lane < 96, plane, small.T))
        weights = jnp.concatenate([gw[0], gw[1], gw[2], gwo[...]], axis=1)
        weights = jnp.concatenate([weights[:, b * 128 : (b + 1) * 128] for b in range(6)], axis=0)
        for k in range(9):
            put(10 + k, weights[k * 128 : (k + 1) * 128])
        kinds = jnp.zeros((128, 128), f32)
        for win in range(8):
            kinds = jnp.where(lane == win, scal_ref[win].astype(f32), kinds)
        put(19, kinds)
        for k in range(20, SEND_ROWS):
            put(k, jnp.zeros((128, 128), f32))
        send_ref[...] = snd[...].astype(bf16)


def attend(scal, x, u, east, south, diag, ids, ct, gain, nb, w3, bq, wo, bias):
    def whole(shape):
        return pl.BlockSpec(shape, lambda w: (0,) * len(shape))

    ins = [x, u, east, south, diag, ids, ct, gain, nb, w3, bq, wo]
    outs = [(432, WIDTH), (432, WIDTH), (144, WIDTH), (144, WIDTH), (128 * SEND_ROWS, 128)]
    return pl.pallas_call(
        window_kernel,
        grid=(8 // PER_STEP,),
        out_shape=[jax.ShapeDtypeStruct(o, bf16) for o in outs],
        in_specs=[pl.BlockSpec(memory_space=pltpu.SMEM)]
        + [whole(a.shape) for a in ins]
        + [pl.BlockSpec((PER_STEP, PAIRS, WIN_TOKENS), lambda w: (w, 0, 0))],
        out_specs=[whole(o) for o in outs],
        scratch_shapes=[
            pltpu.VMEM((2, 1152, 128), f32),
            pltpu.VMEM((2, 1152, 128), f32),
            pltpu.VMEM((2, 1152, 128), f32),
            pltpu.VMEM((WIN_TOKENS, WIDTH), f32),
            pltpu.VMEM((3, WIDTH, WIDTH), bf16),
            pltpu.VMEM((PAIRS, WIDTH), bf16),
            pltpu.VMEM((2, 8 * PAIRS, 128), f32),
            pltpu.VMEM((3, WIDTH, WIDTH), f32),
            pltpu.VMEM((WIDTH, WIDTH), f32),
            pltpu.VMEM((16, WIDTH), f32),
            pltpu.VMEM((2, 1152, 128), f32),
            pltpu.VMEM((128 * SEND_ROWS, 128), f32),
        ],
        compiler_params=pltpu.CompilerParams(
            vmem_limit_bytes=34 * MIB, dimension_semantics=("arbitrary",)
        ),
        cost_estimate=pl.CostEstimate(flops=4 * 10**9, bytes_accessed=8 * 10**6, transcendentals=10**6),
        name="windows",
    )(scal, *ins, bias)


def sum_kernel(root, core_ref, in_ref, out_ref, kinds_ref):
    first = in_ref[0 : 4 * SEND_ROWS, :].astype(f32)
    kinds = [first[lat * SEND_ROWS + 19 : lat * SEND_ROWS + 20] for lat in range(4)]
    kinds = jnp.concatenate(kinds + [jnp.zeros((4, 128), f32)], axis=0).astype(jnp.int32)
    kinds_ref[...] = jnp.where(iota((8, 128), 1) == 8, core_ref[0], kinds)
    total = jnp.sum(in_ref[...].astype(f32).reshape(32, 4 * SEND_ROWS, 128), axis=0) * (1.0 / root)
    parts = [total[lat * SEND_ROWS : (lat + 1) * SEND_ROWS] for lat in range(4)]
    shared = (parts[0] + parts[1]) + (parts[2] + parts[3])
    tails = [
        jnp.concatenate(
            [
                parts[j][9:10, 0:90],
                parts[3][9:10, 30 * j : 30 * j + 30],
                shared[9:10, 96 + 7 * j : 103 + 7 * j],
                jnp.zeros((1, 1), f32),
            ],
            axis=1,
        )
        for j in range(3)
    ]
    rows = [p[0:9] for p in parts] + [shared[10:19]] + tails
    rows = jnp.concatenate(rows, axis=0).astype(bf16)
    for peer in range(64):
        out_ref[peer * GATHER_ROWS : (peer + 1) * GATHER_ROWS, :] = rows


def summed(received, core, root):
    def body(core_ref, in_ref, out_ref, kinds_ref):
        sum_kernel(root, core_ref, in_ref, out_ref, kinds_ref)

    return pl.pallas_call(
        body,
        out_shape=[
            jax.ShapeDtypeStruct((64 * GATHER_ROWS, 128), bf16),
            jax.ShapeDtypeStruct((8, 128), jnp.int32),
        ],
        in_specs=[
            pl.BlockSpec(memory_space=pltpu.SMEM),
            pl.BlockSpec(memory_space=pltpu.VMEM),
        ],
        out_specs=[pl.BlockSpec(memory_space=pltpu.VMEM)] * 2,
        compiler_params=pltpu.CompilerParams(vmem_limit_bytes=10 * MIB),
        name="sums",
    )(core, received)


def spread_kernel(
    scal_ref,
    own_ref,
    other_ref,
    tab_ref,
    class_ref,
    gain_ref,
    nb_ref,
    wqkv_ref,
    bqkv_ref,
    wo_ref,
    bo_ref,
    g,
    tails,
    p,
    stage,
    sems,
):
    core = scal_ref[0, 8]
    half = 64 * GATHER_ROWS
    g[pl.ds(pl.multiple_of(core * half, half), half), :] = own_ref[...].astype(f32)
    g[pl.ds(pl.multiple_of((1 - core) * half, half), half), :] = other_ref[...].astype(f32)
    extra = [g[pl.ds(45 + j, 128, stride=GATHER_ROWS), :] for j in range(3)]
    for lat in range(3):
        tails[lat] = extra[lat]
    tails[3] = jnp.concatenate([e[:, 90:120] for e in extra] + [jnp.zeros((128, 38), f32)], axis=1)
    for lat in range(4):
        for w in range(8):
            kind = scal_ref[lat, w]
            for q in range(16):
                e = q * 8 + w
                src = e * GATHER_ROWS + lat * 9
                to = pl.multiple_of((q * 32 + kind) * 16, 16)
                p[pl.ds(to, 9), :] = g[src : src + 9, :]
                p[pl.ds(to + 9, 1), :] = tails[lat, e : e + 1, :]
    copies = []
    for h in range(HEADS):
        for m in range(24):
            lu, la = m // 12, m % 12
            k, q = divmod(lu * 72 + h * 12 + la, 16)
            at = (((la // 6) * 2 + lu) * 6 + la % 6) * GROUP
            stage[h, :, at : at + 128] = p[pl.ds(q * 512 + k, 32, stride=16), :]
            tail = p[pl.ds(q * 512 + 9, 32, stride=16), :]
            stage[h, :, at + 128 : at + GROUP] = tail[:, k * 10 : k * 10 + 10]
        copies.append(pltpu.make_async_copy(stage.at[h], tab_ref.at[h], sems.at[h]))
        copies[-1].start()
    weights = jnp.concatenate(
        [g[pl.ds(36 + k, 128, stride=GATHER_ROWS), :] for k in range(9)], axis=0
    )
    weights = jnp.concatenate([weights[b * 192 : (b + 1) * 192] for b in range(6)], axis=1)
    wqkv_ref[...] = weights[:, 0:576]
    wo_ref[...] = weights[:, 576:768]
    small = jnp.concatenate([e[:, 120:127] for e in extra] + [jnp.zeros((128, 107), f32)], axis=1).T
    small = jnp.concatenate([small[0:10], small[10:20]], axis=1)[:, 0:WIDTH]
    class_ref[...] = small[0:4]
    gain_ref[...] = small[4:5].reshape(WIDTH)
    nb_ref[...] = small[5:6].reshape(WIDTH)
    grad_bqkv = jnp.concatenate([small[6:7], small[7:8], small[8:9]], axis=1)
    bqkv_ref[...] = grad_bqkv.reshape(3 * WIDTH)
    bo_ref[...] = small[9:10].reshape(WIDTH)
    for copy in copies:
        copy.wait()


def spread(own, other, scal):
    outs = [
        (HEADS, 32, POSITIONS),
        (CLASSES, WIDTH),
        (WIDTH,),
        (WIDTH,),
        (WIDTH, 3 * WIDTH),
        (3 * WIDTH,),
        (WIDTH, WIDTH),
        (WIDTH,),
    ]
    return pl.pallas_call(
        spread_kernel,
        out_shape=[jax.ShapeDtypeStruct(o, f32) for o in outs],
        in_specs=[
            pl.BlockSpec(memory_space=pltpu.SMEM),
            pl.BlockSpec(memory_space=pltpu.VMEM),
            pl.BlockSpec(memory_space=pltpu.VMEM),
        ],
        out_specs=[pl.BlockSpec(memory_space=pl.ANY)]
        + [pl.BlockSpec(memory_space=pltpu.VMEM)] * (len(outs) - 1),
        scratch_shapes=[
            pltpu.VMEM((128 * GATHER_ROWS, 128), f32),
            pltpu.VMEM((4, 128, 128), f32),
            pltpu.VMEM((16 * 32 * 16, 128), f32),
            pltpu.VMEM((HEADS, 32, POSITIONS), f32),
            pltpu.SemaphoreType.DMA((HEADS,)),
        ],
        compiler_params=pltpu.CompilerParams(vmem_limit_bytes=24 * MIB),
        cost_estimate=pl.CostEstimate(flops=10**10, bytes_accessed=10**7, transcendentals=0),
        name="spread",
    )(scal, own, other)


def pack_kernel(x_ref, u_ref, ids_ref, east_ref, south_ref, diag_ref, ids_out):
    lane = iota((1, WIN_TOKENS), 1)
    lat = quotient(lane, 12)
    lon = lane - 12 * lat
    ids = ids_ref[...].astype(f32)
    row = jnp.concatenate([ids[a : a + 1, :] for a in range(12)], axis=1)

    def moved_row(keep, by):
        kept = jnp.where(keep, row, 0.0)
        if by < 0:
            kept = jnp.concatenate([kept[:, -by:], jnp.zeros((1, 2 * WIDTH - WIN_TOKENS - by), f32)], axis=1)
        else:
            tail = jnp.zeros((1, 2 * WIDTH - WIN_TOKENS), f32)
            kept = jnp.concatenate([jnp.zeros((1, by), f32), kept[:, : WIN_TOKENS - by], tail], axis=1)
        return jnp.concatenate([kept, jnp.zeros((7, 2 * WIDTH), f32)], axis=0)

    def fill(out, lats, lon_at, id_rows):
        rows = []
        for a in lats:
            at = a * 96 + lon_at * 8
            rows.append(
                jnp.concatenate(
                    [x_ref[at : at + 48, :].astype(f32), u_ref[at : at + 48, :].astype(f32)], axis=1
                )
            )
        out[...] = jnp.concatenate(rows + [id_rows], axis=0).astype(bf16)

    fill(east_ref, range(3, 12), 0, moved_row((lat >= 3) & (lon < 6), -30))
    fill(south_ref, range(0, 3), 6, moved_row((lat < 3) & (lon >= 6), 102))
    fill(diag_ref, range(0, 3), 0, moved_row((lat < 3) & (lon < 6), 114))
    ids_out[...] = moved_row((lat >= 3) & (lon >= 6), -42)


def pack(x, u, ids):
    shapes = [((440, 2 * WIDTH), bf16), ((152, 2 * WIDTH), bf16), ((152, 2 * WIDTH), bf16)]
    shapes.append(((8, 2 * WIDTH), f32))
    return pl.pallas_call(
        pack_kernel,
        out_shape=[jax.ShapeDtypeStruct(*o) for o in shapes],
        in_specs=[pl.BlockSpec(memory_space=pltpu.VMEM)] * 3,
        out_specs=[pl.BlockSpec(memory_space=pltpu.VMEM)] * 4,
        compiler_params=pltpu.CompilerParams(vmem_limit_bytes=56 * MIB),
        name="pack",
    )(x, u, ids)


def moved(array, lon_by, lat_by):
    lon, lat = lax.axis_size("lon"), lax.axis_size("lat")
    pairs = [
        (i * lat + j, ((i + lon_by) % lon) * lat + (j + lat_by) % lat)
        for i in range(lon)
        for j in range(lat)
    ]
    return lax.ppermute(array, BOTH, pairs)


def shards(
    inputs,
    upstream,
    land_ids,
    window_kinds,
    class_table,
    norm_gain,
    norm_bias,
    qkv_weight,
    qkv_bias,
    out_weight,
    bias_table,
):
    x = inputs[0].transpose(1, 2, 0, 3)
    u = upstream[0].transpose(1, 2, 0, 3)
    x = x.reshape(1152, WIDTH)
    u = u.reshape(1152, WIDTH)
    east, south, diag, own_ids = pack(x, u, land_ids)
    east = moved(east, -1, 0)
    south = moved(south, 0, -1)
    diag = moved(diag, -1, -1)

    last_lat = (lax.axis_index("lat") == lax.axis_size("lat") - 1).astype(jnp.int32)
    scal = jnp.concatenate([window_kinds, last_lat.reshape(1)])
    bias = expand_bias(bias_table.transpose(1, 0, 2), scal)

    own, east_out, south_out, diag_out, send = attend(
        scal,
        x,
        u,
        east,
        south,
        diag,
        own_ids,
        class_table,
        norm_gain.reshape(1, WIDTH),
        norm_bias.reshape(1, WIDTH),
        qkv_weight,
        qkv_bias,
        out_weight,
        bias,
    )
    root = math.sqrt(inputs.size // WIDTH * lax.axis_size("lon") * lax.axis_size("lat"))
    received = lax.all_to_all(send.reshape(128, SEND_ROWS, 128), BOTH, 0, 0)
    core = (lax.axis_index("lat") % 2).reshape(1)
    part, kinds = summed(received.reshape(128 * SEND_ROWS, 128), core, root)
    same_core = [[d for d in range(128) if d % 2 == core] for core in range(2)]
    mine = lax.all_to_all(
        part.reshape(64, GATHER_ROWS, 128), BOTH, 0, 0, axis_index_groups=same_core
    )
    other = lax.ppermute(mine, BOTH, [(d, d ^ 1) for d in range(128)])
    other, east_out, south_out, diag_out = lax.optimization_barrier(
        (other, east_out, south_out, diag_out)
    )
    east_back = moved(east_out, 1, 0).reshape(9, 6, 8, WIDTH)
    south_back = moved(south_out, 0, 1).reshape(3, 6, 8, WIDTH)
    diag_back = moved(diag_out, 1, 1).reshape(3, 6, 8, WIDTH)
    own = own.reshape(9, 6, 8, WIDTH)
    flat = (64 * GATHER_ROWS, 128)
    table, grad_class, grad_gain, grad_nb, grad_wqkv, grad_bqkv, grad_wout, grad_bout = spread(
        mine.reshape(flat), other.reshape(flat), kinds
    )
    table, east_back, south_back, diag_back = lax.optimization_barrier(
        (table, east_back, south_back, diag_back)
    )
    grad_x = jnp.concatenate(
        [
            jnp.concatenate([diag_back, south_back], axis=1),
            jnp.concatenate([east_back, own], axis=1),
        ],
        axis=0,
    )

    return (
        grad_x.transpose(2, 0, 1, 3)[None],
        grad_class,
        grad_gain,
        grad_nb,
        grad_wqkv,
        grad_bqkv,
        grad_wout,
        grad_bout,
        table.transpose(1, 0, 2),
    )


def solution(mesh):
    placed = (
        P(None, None, "lat", "lon", None),
        P(None, None, "lat", "lon", None),
        P("lat", "lon"),
        P("lat"),
        P(),
        P(),
        P(),
        P(),
        P(),
        P(),
        P(),
    )
    return jax.shard_map(
        shards,
        mesh=mesh,
        in_specs=placed,
        out_specs=(P(None, None, "lat", "lon", None), P(), P(), P(), P(), P(), P(), P(), P()),
        check_vma=False,
    )
```
